32 devices in a mesh: dp: 8 (over z, y), seq: 4 (over x, core).
Axes of the slice: x: 2, y: 2, z: 4, core: 2. Of those that a mesh axis runs over, the one named last changes fastest.
Arguments:
- image_counts: int32 [8], P('dp'), may hold values from 1 to 12, as said below
- patches: bfloat16 [196, 96, 768], P(None, 'dp', 'seq'), may hold values from -6 to 6
- ln1_gain: float32 [768], P('seq'), may hold values from 0.1 to 1.9
- ln1_bias: float32 [768], P('seq'), may hold values from -1.5 to 1.5
- tok_in_weight: bfloat16 [384, 196], replicated, may hold values from -0.4375 to 0.4375
- tok_in_bias: float32 [384], replicated, may hold values from -2.5 to 2.5
- tok_out_weight: bfloat16 [196, 384], replicated, may hold values from -0.3125 to 0.3125
- tok_out_bias: float32 [196], replicated, may hold values from -2.5 to 2.5
- ln2_gain: float32 [768], P('seq'), may hold values from 0.1 to 1.9
- ln2_bias: float32 [768], P('seq'), may hold values from -1.5 to 1.5
- chan_in_weight: bfloat16 [768, 3072], P(None, 'seq'), may hold values from -0.21875 to 0.21875
- chan_in_bias: float32 [3072], P('seq'), may hold values from -2.5 to 2.5
- chan_out_weight: bfloat16 [3072, 768], P('seq'), may hold values from -0.109375 to 0.109375
- chan_out_bias: float32 [768], P('seq'), may hold values from -1.5 to 1.5
- cotangent: bfloat16 [196, 96, 768], P(None, 'dp', 'seq'), may hold values from -6 to 6
Outputs:
- mixed: bfloat16 [196, 96, 768], P(None, 'dp', 'seq')
- input_grad: bfloat16 [196, 96, 768], P(None, 'dp', 'seq')
- grad_ln1_gain: float32 [768], P('seq')
- grad_ln1_bias: float32 [768], P('seq')
- grad_tok_in: float32 [384, 196], replicated
- grad_tok_in_bias: float32 [384], replicated
- grad_tok_out: float32 [196, 384], replicated
- grad_tok_out_bias: float32 [196], replicated
- grad_ln2_gain: float32 [768], P('seq')
- grad_ln2_bias: float32 [768], P('seq')
- grad_chan_in: float32 [768, 3072], P(None, 'seq')
- grad_chan_in_bias: float32 [3072], P('seq')
- grad_chan_out: float32 [3072, 768], P('seq')
- grad_chan_out_bias: float32 [768], P('seq')
The draws below stay inside these ranges and needn't reach their ends.
Inputs may be any that keep to these rules, and one draw needn't show every extreme that they name: `image_counts`: each entry is at least 1 and at most 12; some index of dp has all 12 slots in use.
All inputs are finite; a program needn't handle non-finite values.
Results may differ from the reference program's by a relative error of at most 0.012.
Values may be sent and summed in bfloat16 or wider, within the bound.
A program may use at most 192 MiB of HBM per device.

```python
import jax
import jax.numpy as jnp
from jax import lax

D = 768
DS = 384
DC = 3072
S = 196
IMG_DEV = 12
IMAGES = 96
N_DP = 8


def draw_image_counts(key, part):
    key = jax.random.fold_in(key, 7)
    first, second = jax.random.split(key)
    counts = jax.random.randint(first, (N_DP,), 1, IMG_DEV + 1)
    filled = jax.random.randint(second, (), 0, N_DP)
    return jnp.where(jnp.arange(N_DP, dtype=jnp.int32) == filled, IMG_DEV, counts).astype(jnp.int32)


def block_levels(key, shape, pieces, low, top_value):
    level = 1.0
    for axis_at, blocks in pieces:
        heights = jax.random.uniform(jax.random.fold_in(jax.random.fold_in(key, 6), axis_at), (blocks,), jnp.float32, low / len(pieces), top_value / len(pieces))
        level = level * jnp.repeat(jnp.exp(heights), shape[axis_at] // blocks).reshape((-1,) + (1,) * (len(shape) - 1 - axis_at))
    return level


def gaussian(stream_key, shape, width, bound, cuts=(), kind=jnp.bfloat16):
    level = block_levels(stream_key, shape, cuts, -0.22, 0.18) if cuts else 1.0
    drawn = jax.random.normal(stream_key, shape, jnp.float32) * width * level
    return jnp.minimum(jnp.maximum(drawn, -bound), bound).astype(kind)


def setup_inputs(seed: int = 0) -> dict:
    streams_of = jax.random.split(jax.random.key(seed), 16)
    return {
        "image_counts": draw_image_counts(jax.random.fold_in(streams_of[15], 71), 0),
        "patches": gaussian(streams_of[1], (S, IMAGES, D), 1.0, 6.0, ((1, 8), (2, 4))),
        "ln1_gain": jnp.clip(1.0 + 0.18 * jax.random.normal(streams_of[2], (D,), jnp.float32), 0.1, 1.9),
        "ln1_bias": gaussian(streams_of[3], (D,), 0.3, 1.5, ((0, 4),), jnp.float32),
        "tok_in_weight": gaussian(streams_of[4], (DS, S), S ** -0.5, 0.4375),
        "tok_in_bias": gaussian(streams_of[5], (DS,), 0.5, 2.5, (), jnp.float32),
        "tok_out_weight": gaussian(streams_of[6], (S, DS), DS ** -0.5, 0.3125),
        "tok_out_bias": gaussian(streams_of[7], (S,), 0.5, 2.5, (), jnp.float32),
        "ln2_gain": jnp.clip(1.0 + 0.18 * jax.random.normal(streams_of[8], (D,), jnp.float32), 0.1, 1.9),
        "ln2_bias": gaussian(streams_of[9], (D,), 0.3, 1.5, ((0, 4),), jnp.float32),
        "chan_in_weight": gaussian(streams_of[10], (D, DC), D ** -0.5, 0.21875, ((1, 4),)),
        "chan_in_bias": gaussian(streams_of[11], (DC,), 0.5, 2.5, ((0, 4),), jnp.float32),
        "chan_out_weight": gaussian(streams_of[12], (DC, D), DC ** -0.5, 0.109375, ((0, 4),)),
        "chan_out_bias": gaussian(streams_of[13], (D,), 0.3, 1.5, ((0, 4),), jnp.float32),
        "cotangent": gaussian(streams_of[14], (S, IMAGES, D), 1.0, 6.0, ((1, 8), (2, 4))),
    }


@jax.custom_vjp
def low(v):
    return lax.optimization_barrier(v.astype(jnp.bfloat16)).astype(jnp.float32)

@jax.custom_vjp
def low_back(v):
    return v

def low_keep(v):
    return (low(v), None)

def low_pass(kept, grad):
    return (grad,)

def back_keep(v):
    return (v, None)

def back_low(kept, grad):
    return (low(grad),)
low.defvjp(low_keep, low_pass)
low_back.defvjp(back_keep, back_low)

def layer_norm(values, gain, shift):
    mean = lax.optimization_barrier(jnp.mean(values, axis=-1, keepdims=True))
    centred = values - mean
    spread = lax.optimization_barrier(jnp.mean(centred * centred, axis=-1, keepdims=True))
    return centred * lax.rsqrt(spread + 1e-06) * gain + shift

def mixer(params, block, valid):
    gain_one, bias_one, w_tin, b_tin, w_tout, b_tout, gain_two, bias_two, w_cin, b_cin, w_cout, b_cout = params
    highest = lax.Precision.HIGHEST
    normed_one = low(layer_norm(block, gain_one, bias_one))
    token_pre = low_back(jnp.einsum('jp,pbc->jbc', w_tin, normed_one, precision=highest) + b_tin[:, None, None])
    token_act = low(jax.nn.gelu(token_pre))
    token_out = low_back(jnp.einsum('pj,jbc->pbc', w_tout, token_act, precision=highest) + b_tout[:, None, None])
    middle = block + token_out
    normed_two = low(layer_norm(middle, gain_two, bias_two))
    hidden_pre = low_back(jnp.einsum('pbc,ch->pbh', normed_two, w_cin, precision=highest) + b_cin)
    hidden_act = low(jax.nn.gelu(hidden_pre))
    chan_out = jnp.einsum('pbh,hc->pbc', hidden_act, w_cout, precision=highest) + b_cout
    return valid[None, :, None] * (middle + chan_out)

def reference(image_counts, patches, ln1_gain, ln1_bias, tok_in_weight, tok_in_bias, tok_out_weight, tok_out_bias, ln2_gain, ln2_bias, chan_in_weight, chan_in_bias, chan_out_weight, chan_out_bias, cotangent):
    params = (ln1_gain, ln1_bias, tok_in_weight.astype(jnp.float32), tok_in_bias, tok_out_weight.astype(jnp.float32), tok_out_bias, ln2_gain, ln2_bias, chan_in_weight.astype(jnp.float32), chan_in_bias, chan_out_weight.astype(jnp.float32), chan_out_bias)
    blocks = jnp.moveaxis(patches.reshape(S, N_DP, IMG_DEV, D), 1, 0)
    grads_in = jnp.moveaxis(cotangent.reshape(S, N_DP, IMG_DEV, D), 1, 0)

    def step(total, item):
        count, block, grad_block = item
        valid = (jnp.arange(IMG_DEV, dtype=jnp.int32) < count).astype(jnp.float32)
        result, back = jax.vjp(lambda p, v: mixer(p, v, valid), params, block.astype(jnp.float32))
        grad_params, grad_block_in = back(grad_block.astype(jnp.float32))
        total = jax.tree.map(lambda a, b: a + b, total, grad_params)
        return (total, (result.astype(jnp.bfloat16), grad_block_in.astype(jnp.bfloat16)))
    zeros = jax.tree.map(jnp.zeros_like, params)
    total, (results, grads) = lax.scan(step, zeros, (image_counts, blocks, grads_in))
    mixed = jnp.moveaxis(results, 0, 1).reshape(S, N_DP * IMG_DEV, D)
    input_grad = jnp.moveaxis(grads, 0, 1).reshape(S, N_DP * IMG_DEV, D)
    return (mixed, input_grad, total[0], total[1], total[2], total[3], total[4], total[5], total[6], total[7], total[8], total[9], total[10], total[11])
```

```python
import functools

import jax
import jax.numpy as jnp
from jax import lax
from jax.experimental import pallas as pl
from jax.experimental.pallas import tpu as pltpu
from jax.sharding import PartitionSpec as P

MESH = pl.DeviceIdType.MESH
BF = jnp.bfloat16
F32 = jnp.float32
EPS = 1e-06
GELU_A = 0.7978845608028654
GELU_B = GELU_A * 0.044715
LANE = 128


def gelu_parts(x):
    square = x * x
    tanh = jnp.tanh(x * (GELU_A + GELU_B * square))
    half = 0.5 + 0.5 * tanh
    slope = half + (0.5 * x) * (1.0 - tanh * tanh) * (GELU_A + (3.0 * GELU_B) * square)
    return x * half, slope


def dot(a, b):
    return lax.dot_general(a, b, (((1,), (0,)), ((), ())), preferred_element_type=F32)


def dot_nt(a, b):
    return lax.dot_general(a, b, (((1,), (1,)), ((), ())), preferred_element_type=F32)


def dot_tn(a, b):
    return lax.dot_general(a, b, (((0,), (0,)), ((), ())), preferred_element_type=F32)


def column(values, at):
    lanes = lax.broadcasted_iota(jnp.int32, values.shape, 1)
    return jnp.sum(jnp.where(lanes == at, values, 0.0), axis=-1, keepdims=True)


def put_columns(ref, first, second, at):
    lanes = lax.broadcasted_iota(jnp.int32, ref.shape, 1)
    ref[...] = jnp.where(lanes == at, first, jnp.where(lanes == at + 1, second, ref[...]))


def layer_kernel(
    cfg,
    patches_hbm,
    cot_hbm,
    vec_in,
    hidden_bias,
    tok_in,
    tok_in_t,
    tok_out,
    tok_out_t,
    tok_in_bias,
    tok_out_bias,
    win_hbm,
    wout_hbm,
    mixed_out,
    gin_out,
    gci_out,
    gco_out,
    tok_final,
    vec_final,
    win,
    wout,
    pwin,
    cwin,
    vwin,
    vown,
    vother,
    raw,
    ntb,
    gb,
    acts,
    ghs,
    gci,
    gco,
    cib,
    outp,
    outr,
    backp,
    backr,
    outx,
    backx,
    s2own,
    s2x,
    s1own,
    s1x,
    n1s,
    tas,
    tsl,
    mids,
    sc1s,
    sc2s,
    inv1s,
    inv2s,
    gms,
    w1s,
    gis,
    mos,
    gbuf,
    fbuf,
    rbuf,
    tg,
    tb,
    tcore,
    tcur,
    txr,
    tdp,
    trd,
    vg,
    vcore,
    vsend,
    vrd,
    sem_win_l,
    sem_p_l,
    sem_c_l,
    sem_p_w,
    sem_c_w,
    sem_v,
    sem_xp,
    sem_xc,
    sem_nt,
    sem_g,
    sem_op,
    sem_bp,
    sem_ox,
    sem_bx,
    sem_s,
    sem_mo,
    sem_gi,
    sem_mo_l,
    sem_gi_l,
    sem_rs,
    sem_ag,
    sem_out,
    sem_t,
    sem_tdp,
    sem_vdp,
):
    n_dp, bits, own, rows, half, full, hidden, toks, chunks, chunk = cfg
    d = lax.axis_index("dp")
    s = lax.axis_index("seq")
    c = s % 2
    x = s // 2
    core = (d, s + 1 - 2 * c)
    across = (d, s + 2 - 4 * x)

    def dp_bit(t):
        return (d // (1 << t)) % 2

    def dp_peer(t):
        m = 1 << t
        return (d + m - 2 * m * dp_bit(t), s)

    def remote(src, dst, sems, at, target):
        return pltpu.make_async_remote_copy(
            src_ref=src,
            dst_ref=dst,
            send_sem=sems.at[(0,) + at],
            recv_sem=sems.at[(1,) + at],
            device_id=target,
            device_id_type=MESH,
        )

    mine = pl.multiple_of(x * half, LANE)
    theirs = pl.multiple_of((1 - x) * half, LANE)
    weight_copies = [
        pltpu.make_async_copy(win_hbm.at[pl.ds(mine, half)], win.at[pl.ds(0, half)], sem_win_l.at[0]),
        pltpu.make_async_copy(win_hbm.at[pl.ds(theirs, half)], win.at[pl.ds(half, half)], sem_win_l.at[1]),
        pltpu.make_async_copy(wout_hbm.at[:, pl.ds(mine, half)], wout.at[:, pl.ds(0, half)], sem_win_l.at[2]),
        pltpu.make_async_copy(wout_hbm.at[:, pl.ds(theirs, half)], wout.at[:, pl.ds(half, half)], sem_win_l.at[3]),
    ]

    def p_local(j):
        return pltpu.make_async_copy(patches_hbm.at[c * own + j], pwin.at[c, j], sem_p_l.at[j])

    def c_local(j):
        return pltpu.make_async_copy(cot_hbm.at[c * own + j], cwin.at[c, j], sem_c_l.at[j])

    def p_swap(j):
        return remote(patches_hbm.at[(1 - c) * own + j], pwin.at[c, j], sem_p_w, (j,), core)

    def c_swap(j):
        return remote(cot_hbm.at[(1 - c) * own + j], cwin.at[c, j], sem_c_w, (j,), core)

    v_swap = remote(vec_in, vwin, sem_v, (0,), core)
    v_across = remote(vown, vother, sem_v, (1,), across)

    def p_across(j):
        return remote(raw.at[j, :, pl.ds(0, half)], raw.at[j, :, pl.ds(half, half)], sem_xp, (j,), across)

    def c_across(j):
        return remote(
            gb.at[j, pl.ds(0, rows), pl.ds(0, half)],
            gb.at[j, pl.ds(0, rows), pl.ds(half, half)],
            sem_xc,
            (j,),
            across,
        )

    def nt_share(j):
        return remote(ntb.at[j, pl.ds(0, rows)], ntb.at[j, pl.ds(rows, rows)], sem_nt, (j,), core)

    def g_share(j):
        return remote(gb.at[j, pl.ds(0, rows)], gb.at[j, pl.ds(rows, rows)], sem_g, (j,), core)

    def out_pair(j):
        return remote(outp.at[j, pl.ds(rows, rows)], outr.at[j], sem_op, (j,), core)

    def back_pair(j):
        return remote(backp.at[j, pl.ds(rows, rows)], backr.at[j], sem_bp, (j,), core)

    def out_across(j):
        return remote(outp.at[j, pl.ds(0, rows), pl.ds(half, half)], outx.at[j], sem_ox, (j,), across)

    def back_across(j):
        return remote(backp.at[j, pl.ds(0, rows), pl.ds(half, half)], backx.at[j], sem_bx, (j,), across)

    s2_across = remote(s2own, s2x, sem_s, (0,), across)
    s1_across = remote(s1own, s1x, sem_s, (1,), across)

    give = pl.multiple_of((1 - c) * LANE, LANE)
    keep = pl.multiple_of(c * LANE, LANE)

    def mixed_give(j):
        return remote(mos.at[j, :, pl.ds(give, 2 * LANE)], mixed_out.at[c * own + j], sem_mo, (j,), core)

    def gin_give(j):
        return remote(gis.at[j, :, pl.ds(give, 2 * LANE)], gin_out.at[c * own + j], sem_gi, (j,), core)

    def mixed_keep(j):
        return pltpu.make_async_copy(mos.at[j, :, pl.ds(keep, 2 * LANE)], mixed_out.at[c * own + j], sem_mo_l.at[j])

    def gin_keep(j):
        return pltpu.make_async_copy(gis.at[j, :, pl.ds(keep, 2 * LANE)], gin_out.at[c * own + j], sem_gi_l.at[j])

    def segment(k, t):
        start = k * chunk
        for u in range(t):
            start = start + dp_bit(u) * (chunk >> (u + 1))
        return start

    rb_base = []
    base = 0
    for t in range(bits):
        rb_base.append(base)
        base += chunks * (chunk >> (t + 1))

    def rs_at(k, t):
        size = chunk >> (t + 1)
        return pl.ds(pl.multiple_of(rb_base[t] + k * size, 16), size)

    def rs_send(k, t):
        size = chunk >> (t + 1)
        start = segment(k, t) + (1 - dp_bit(t)) * size
        return remote(
            gbuf.at[pl.ds(pl.multiple_of(start, 16), size)], rbuf.at[rs_at(k, t)], sem_rs, (t, k), dp_peer(t)
        )

    def rs_add(k, t, target):
        size = chunk >> (t + 1)
        at = pl.ds(pl.multiple_of(segment(k, t + 1), 16), size)
        total = gbuf[at].astype(F32) + rbuf[rs_at(k, t)].astype(F32)
        target[at] = total.astype(BF)

    def ag_send(k, t):
        size = chunk >> (t + 1)
        at = pl.ds(pl.multiple_of(segment(k, t + 1), 16), size)
        return remote(fbuf.at[at], fbuf.at[at], sem_ag, (t, k), dp_peer(t))

    t_half = tb.shape[0] // 2
    t_quarter = t_half // 2
    tc_keep = pl.multiple_of(c * t_half, 16)
    tc_give = pl.multiple_of((1 - c) * t_half, 16)
    tx_keep = pl.multiple_of(x * t_quarter, 16)
    tx_give = pl.multiple_of((1 - x) * t_quarter, 16)
    t_mine = pl.multiple_of(c * t_half + x * t_quarter, 16)
    t_core = remote(tb.at[pl.ds(tc_give, t_half)], tcore, sem_t, (0,), core)
    t_across = remote(tcur.at[pl.ds(tx_give, t_quarter)], txr, sem_t, (1,), across)
    t_back_x = remote(tok_final.at[pl.ds(t_mine, t_quarter)], tok_final.at[pl.ds(t_mine, t_quarter)], sem_t, (2,), across)
    t_back_c = remote(tok_final.at[pl.ds(tc_keep, t_half)], tok_final.at[pl.ds(tc_keep, t_half)], sem_t, (3,), core)
    v_core = remote(vg.at[pl.ds(0, 8)], vcore, sem_t, (4,), core)

    def t_dp(t):
        return remote(tdp.at[t], trd.at[t], sem_tdp, (t,), dp_peer(t))

    def v_dp(t):
        return remote(vsend.at[t], vrd.at[t], sem_vdp, (t,), dp_peer(t))

    barrier = pltpu.get_barrier_semaphore()
    peers = [core, across] + [dp_peer(t) for t in range(bits)]
    for peer in peers:
        pl.semaphore_signal(barrier, inc=1, device_id=peer, device_id_type=MESH)
    pl.semaphore_wait(barrier, len(peers))

    def start_windows(j, carry):
        p_swap(j).start()
        p_local(j).start()
        c_swap(j).start()
        c_local(j).start()
        return carry

    v_swap.start()
    lax.fori_loop(0, own, start_windows, 0)
    for copy in weight_copies:
        copy.start()

    gci[...] = jnp.zeros_like(gci)
    gco[...] = jnp.zeros_like(gco)
    cib[...] = jnp.zeros_like(cib)
    tg[...] = jnp.zeros_like(tg)
    vg[...] = jnp.zeros_like(vg)
    s2own[...] = jnp.zeros_like(s2own)
    s1own[...] = jnp.zeros_like(s1own)

    def merge(first, second):
        middle = first[:, LANE:].astype(F32) + second[:, :LANE].astype(F32)
        return first[:, :LANE], middle.astype(first.dtype), second[:, LANE:]

    def merge_send(j):
        p_swap(j).wait_recv()
        p_local(j).wait()
        for at, part in enumerate(merge(pwin[0, j], pwin[1, j])):
            raw[j, :, pl.ds(at * LANE, LANE)] = part
        p_across(j).start()
        c_swap(j).wait_recv()
        c_local(j).wait()
        for at, part in enumerate(merge(cwin[0, j], cwin[1, j])):
            gb[j, pl.ds(0, rows), pl.ds(at * LANE, LANE)] = part
        c_across(j).start()

    merge_send(0)
    v_swap.wait_recv()
    vmine = vec_in[...]
    vpart = vwin[...]
    v0 = jnp.where(c == 0, vmine, vpart)
    v1 = jnp.where(c == 0, vpart, vmine)
    vown[:, pl.ds(0, LANE)] = v0[:, :LANE]
    vown[:, pl.ds(LANE, LANE)] = v0[:, LANE:] + v1[:, :LANE]
    vown[:, pl.ds(2 * LANE, LANE)] = v1[:, LANE:]
    v_across.start()
    merge_send(1)
    v_across.wait_recv()

    def vector(row):
        return jnp.concatenate([vown[pl.ds(row, 1), :], vother[pl.ds(row, 1), :]], axis=1)

    def token_forward(j):
        values = raw[j].astype(F32)
        mean = jnp.sum(values, axis=-1, keepdims=True) * (1.0 / full)
        centred = values - mean
        inverse = lax.rsqrt(jnp.sum(centred * centred, axis=-1, keepdims=True) * (1.0 / full) + EPS)
        scaled = centred * inverse
        normed = (scaled * vector(0) + vector(1)).astype(BF)
        sc1s[j] = scaled[:, :half].astype(BF)
        inv1s[j] = inverse
        n1s[j] = normed[:, :half]
        act, slope = gelu_parts(dot(tok_in[...], normed) + tok_in_bias[...])
        act = act.astype(BF)
        tas[j] = act[:, :half]
        tsl[j] = slope[:, :half].astype(BF)
        middle = values + (dot(tok_out[...], act) + tok_out_bias[...])
        mids[j] = middle[:, :half]
        mean = jnp.sum(middle, axis=-1, keepdims=True) * (1.0 / full)
        centred = middle - mean
        inverse = lax.rsqrt(jnp.sum(centred * centred, axis=-1, keepdims=True) * (1.0 / full) + EPS)
        scaled = centred * inverse
        sc2s[j] = scaled[:, :half].astype(BF)
        inv2s[j] = inverse
        ntb[j, pl.ds(0, rows)] = (scaled * vector(2) + vector(3)).astype(BF)

    def channel(j):
        nt = ntb[j]
        g = gb[j]
        width = 256
        for at in range(hidden // width):
            cols = pl.ds(at * width, width)
            pre = dot(nt, win[:, cols]) + hidden_bias[:, cols]
            back = dot_nt(g, wout[cols, :])
            act, slope = gelu_parts(pre)
            acts[:, cols] = act.astype(BF)
            grad = (slope * back).astype(BF)
            ghs[:, cols] = grad
            cib[:, cols] += jnp.sum(grad.astype(F32), axis=0, keepdims=True)
        backp[j] = dot_nt(ghs[...], win[...]).astype(BF)
        back_pair(j).start()
        outp[j] = dot(acts[...], wout[...]).astype(BF)
        out_pair(j).start()
        gco[...] += dot_tn(acts[...], g)
        gci[...] += dot_tn(nt, ghs[...])

    def phase_a(j, carry):
        @pl.when(j + 2 < own)
        def _():
            merge_send(j + 2)

        @pl.when(j < own)
        def _():
            p_across(j).wait_recv()
            token_forward(j)
            nt_share(j).start()
            c_across(j).wait_recv()
            g_share(j).start()

        @pl.when(j == 0)
        def _():
            for copy in weight_copies:
                copy.wait()

        @pl.when(j > 0)
        def _():
            nt_share(j - 1).wait_recv()
            g_share(j - 1).wait_recv()
            channel(j - 1)

        return carry

    lax.fori_loop(0, own + 1, phase_a, 0)

    tiles = hidden // LANE
    for at in range(tiles):
        gbuf[pl.ds(at * full, full)] = gci[:, pl.ds(at * LANE, LANE)].astype(BF)
    for at in range(full // LANE):
        gbuf[pl.ds(tiles * full + at * hidden, hidden)] = gco[:, pl.ds(at * LANE, LANE)].astype(BF)

    def start_rs(k, carry):
        rs_send(k, 0).start()
        return carry

    lax.fori_loop(0, chunks, start_rs, 0)

    def pair_sums(j, carry):
        back_pair(j).wait_recv()
        total = backp[j, pl.ds(0, rows)].astype(F32) + backr[j].astype(F32)
        first = jnp.sum(total * vector(2), axis=-1, keepdims=True)
        second = jnp.sum(total * (ntb[j, pl.ds(0, rows)].astype(F32) - vector(3)), axis=-1, keepdims=True)
        put_columns(s2own, first, second, 2 * j)
        backp[j, pl.ds(0, rows)] = total.astype(BF)
        back_across(j).start()
        return carry

    lax.fori_loop(0, own, pair_sums, 0)
    s2_across.start()

    def pair_outs(j, carry):
        out_pair(j).wait_recv()
        total = outp[j, pl.ds(0, rows)].astype(F32) + outr[j].astype(F32)
        outp[j, pl.ds(0, rows)] = total.astype(BF)
        out_across(j).start()
        return carry

    lax.fori_loop(0, own, pair_outs, 0)
    s2_across.wait_recv()
    s2x[...] = (s2own[...] + s2x[...]) * (1.0 / full)

    def token_backward(j):
        back_across(j).wait_recv()
        grad_normed = backp[j, pl.ds(0, rows), pl.ds(0, half)].astype(F32) + backx[j].astype(F32)
        scaled = sc2s[j].astype(F32)
        grad_out = gb[j, pl.ds(0, rows), pl.ds(0, half)].astype(F32)
        sums = s2x[...]
        weighted = grad_normed * vown[pl.ds(2, 1), :]
        grad_mid = grad_out + inv2s[j] * (weighted - column(sums, 2 * j) - scaled * column(sums, 2 * j + 1))
        gms[j] = grad_mid
        vg[pl.ds(2, 1), :] += jnp.sum(grad_normed * scaled, axis=0, keepdims=True)
        vg[pl.ds(3, 1), :] += jnp.sum(grad_normed, axis=0, keepdims=True)
        vg[pl.ds(4, 1), :] += jnp.sum(grad_out, axis=0, keepdims=True)
        low = grad_mid.astype(BF)
        tg[pl.ds(0, rows), pl.ds(rows + 1, 1)] += jnp.sum(low.astype(F32), axis=-1, keepdims=True)
        tg[pl.ds(toks, toks), pl.ds(0, rows)] += dot_nt(tas[j], low)
        grad_pre = (tsl[j].astype(F32) * dot(tok_out_t[...], low)).astype(BF)
        tg[pl.ds(0, toks), pl.ds(rows, 1)] += jnp.sum(grad_pre.astype(F32), axis=-1, keepdims=True)
        tg[pl.ds(0, toks), pl.ds(0, rows)] += dot_nt(grad_pre, n1s[j])
        grad_one = dot(tok_in_t[...], grad_pre)
        scaled = sc1s[j].astype(F32)
        vg[pl.ds(0, 1), :] += jnp.sum(grad_one * scaled, axis=0, keepdims=True)
        vg[pl.ds(1, 1), :] += jnp.sum(grad_one, axis=0, keepdims=True)
        weighted = grad_one * vown[pl.ds(0, 1), :]
        w1s[j] = weighted
        put_columns(
            s1own,
            jnp.sum(weighted, axis=-1, keepdims=True),
            jnp.sum(weighted * scaled, axis=-1, keepdims=True),
            2 * j,
        )

    def input_grads(j, carry):
        sums = (s1own[...] + s1x[...]) * (1.0 / full)
        scaled = sc1s[j].astype(F32)
        grad = gms[j] + inv1s[j] * (w1s[j] - column(sums, 2 * j) - scaled * column(sums, 2 * j + 1))
        gis[j] = grad.astype(BF)
        gin_give(j).start()
        gin_keep(j).start()
        return carry

    def mixed_parts(j):
        out_across(j).wait_recv()
        total = outp[j, pl.ds(0, rows), pl.ds(0, half)].astype(F32) + outx[j].astype(F32)
        mos[j] = (mids[j] + (total + vown[pl.ds(4, 1), :])).astype(BF)
        mixed_give(j).start()
        mixed_keep(j).start()

    def gradient_step(i):
        for e in reversed(range(2 * bits)):
            k = i - e

            @pl.when((k >= 0) & (k < chunks))
            def _(e=e, k=k):
                if e < bits:
                    rs_send(k, e).wait_recv()
                    if e + 1 < bits:
                        rs_add(k, e, gbuf)
                        rs_send(k, e + 1).start()
                    else:
                        rs_add(k, e, fbuf)
                        ag_send(k, e).start()
                else:
                    t = 2 * bits - 1 - e
                    ag_send(k, t).wait_recv()
                    if t > 0:
                        ag_send(k, t - 1).start()

    def token_step(e):
        if e == 0:
            tb[...] = tg[...].astype(BF)
            for at in range(hidden // half):
                vg[pl.ds(8 + at, 1), :] = cib[:, pl.ds(at * half, half)]
            t_core.start()
            v_core.start()
            s1_across.start()
        elif e == 1:
            t_core.wait_recv()
            v_core.wait_recv()
            tcur[...] = (tb[pl.ds(tc_keep, t_half)].astype(F32) + tcore[...].astype(F32)).astype(BF)
            t_across.start()
            vsend[0, pl.ds(0, 8)] = vg[pl.ds(0, 8)] + vcore[...]
            vsend[0, pl.ds(8, 8)] = vg[pl.ds(8, 8)]
            v_dp(0).start()
            s1_across.wait_recv()
            lax.fori_loop(0, own, input_grads, 0)
        elif e == 2:
            t_across.wait_recv()
            tdp[0] = (tcur[pl.ds(tx_keep, t_quarter)].astype(F32) + txr[...].astype(F32)).astype(BF)
            t_dp(0).start()
        elif e < 3 + bits:
            t = e - 3
            t_dp(t).wait_recv()
            v_dp(t).wait_recv()
            total = (tdp[t].astype(F32) + trd[t].astype(F32)).astype(BF)
            vec = vsend[t] + vrd[t]
            if t + 1 < bits:
                tdp[t + 1] = total
                vsend[t + 1] = vec
                t_dp(t + 1).start()
                v_dp(t + 1).start()
            else:
                tok_final[pl.ds(t_mine, t_quarter)] = total
                vec_final[...] = vec
                t_back_x.start()
        elif e == 3 + bits:
            t_back_x.wait_recv()
            t_back_c.start()
        else:
            t_back_c.wait_recv()

    token_first = own
    token_steps = 5 + bits
    last = max(chunks + 2 * bits - 1, token_first + token_steps)

    def phase_b(i, carry):
        gradient_step(i)

        @pl.when(i < own)
        def _():
            token_backward(i)

        for e in range(token_steps):

            @pl.when(i == token_first + e)
            def _(e=e):
                token_step(e)

        @pl.when((i >= own) & (i < 2 * own))
        def _():
            mixed_parts(i - own)

        return carry

    lax.fori_loop(0, max(last, 2 * own), phase_b, 0)

    def out_copies():
        copies = []
        for at in range(tiles):
            lanes = pl.ds(at * LANE, LANE)
            for part, to in enumerate((mine, theirs)):
                copies.append(
                    pltpu.make_async_copy(
                        fbuf.at[pl.ds(at * full + part * half, half)],
                        gci_out.at[pl.ds(to, half), lanes],
                        sem_out.at[len(copies)],
                    )
                )
        for at in range(full // LANE):
            to = mine if at < half // LANE else theirs
            lanes = pl.ds(pl.multiple_of(to + (at % (half // LANE)) * LANE, LANE), LANE)
            copies.append(
                pltpu.make_async_copy(
                    fbuf.at[pl.ds(tiles * full + at * hidden, hidden)],
                    gco_out.at[:, lanes],
                    sem_out.at[len(copies)],
                )
            )
        return copies

    outs = out_copies()
    for copy in outs:
        copy.start()

    def drain(j, carry):
        for make in (
            p_swap, c_swap, p_across, c_across, nt_share, g_share, out_pair, back_pair, out_across, back_across
        ):
            make(j).wait_send()
        mixed_give(j).wait()
        gin_give(j).wait()
        mixed_keep(j).wait()
        gin_keep(j).wait()
        return carry

    lax.fori_loop(0, own, drain, 0)

    def drain_sums(k, carry):
        for t in range(bits):
            rs_send(k, t).wait_send()
            ag_send(k, t).wait_send()
        return carry

    lax.fori_loop(0, chunks, drain_sums, 0)
    for copy in [v_swap, v_across, s2_across, s1_across, t_core, t_across, t_back_x, t_back_c, v_core]:
        copy.wait_send()
    for t in range(bits):
        t_dp(t).wait_send()
        v_dp(t).wait_send()
    for copy in outs:
        copy.wait()


def run_layer(n_dp, patches, cot, vec, hidden_bias, tok_in, tok_out, tok_in_bias, tok_out_bias, win, wout):
    batch, rows, _ = patches.shape
    own = batch // 2
    full, hidden = win.shape
    half = full // 2
    toks = tok_in.shape[0]
    bits = n_dp.bit_length() - 1
    grad_rows = 2 * full * hidden // LANE
    chunks = next(k for k in (6, 9, 3, 1) if grad_rows % (k * n_dp * 16) == 0)
    chunk = grad_rows // chunks
    cfg = (n_dp, bits, own, rows, half, full, hidden, toks, chunks, chunk)
    vmem = pltpu.VMEM
    dma = pltpu.SemaphoreType.DMA
    rs_rows = sum(chunks * (chunk >> (t + 1)) for t in range(bits))
    scratch = [
        vmem((full, hidden), BF),
        vmem((hidden, full), BF),
        vmem((2, own, rows, 2 * LANE), BF),
        vmem((2, own, rows, 2 * LANE), BF),
        vmem((8, 2 * LANE), F32),
        vmem((8, half), F32),
        vmem((8, half), F32),
        vmem((own, rows, full), BF),
        vmem((own, 2 * rows, full), BF),
        vmem((own, 2 * rows, full), BF),
        vmem((2 * rows, hidden), BF),
        vmem((2 * rows, hidden), BF),
        vmem((full, hidden), F32),
        vmem((hidden, full), F32),
        vmem((1, hidden), F32),
        vmem((own, 2 * rows, full), BF),
        vmem((own, rows, full), BF),
        vmem((own, 2 * rows, full), BF),
        vmem((own, rows, full), BF),
        vmem((own, rows, half), BF),
        vmem((own, rows, half), BF),
        vmem((rows, LANE), F32),
        vmem((rows, LANE), F32),
        vmem((rows, LANE), F32),
        vmem((rows, LANE), F32),
        vmem((own, rows, half), BF),
        vmem((own, toks, half), BF),
        vmem((own, toks, half), BF),
        vmem((own, rows, half), F32),
        vmem((own, rows, half), BF),
        vmem((own, rows, half), BF),
        vmem((own, rows, 1), F32),
        vmem((own, rows, 1), F32),
        vmem((own, rows, half), F32),
        vmem((own, rows, half), F32),
        vmem((own, rows, half), BF),
        vmem((own, rows, half), BF),
        vmem((grad_rows, LANE), BF),
        vmem((grad_rows, LANE), BF),
        vmem((rs_rows, LANE), BF),
        vmem((2 * toks, 2 * LANE), F32),
        vmem((2 * toks, 2 * LANE), BF),
        vmem((toks, 2 * LANE), BF),
        vmem((toks, 2 * LANE), BF),
        vmem((toks // 2, 2 * LANE), BF),
        vmem((bits, toks // 2, 2 * LANE), BF),
        vmem((bits, toks // 2, 2 * LANE), BF),
        vmem((16, half), F32),
        vmem((8, half), F32),
        vmem((bits, 16, half), F32),
        vmem((bits, 16, half), F32),
        dma((4,)),
        dma((own,)),
        dma((own,)),
        dma((2, own)),
        dma((2, own)),
        dma((2, 2)),
        dma((2, own)),
        dma((2, own)),
        dma((2, own)),
        dma((2, own)),
        dma((2, own)),
        dma((2, own)),
        dma((2, own)),
        dma((2, own)),
        dma((2, 2)),
        dma((2, own)),
        dma((2, own)),
        dma((own,)),
        dma((own,)),
        dma((2, bits, chunks)),
        dma((2, bits, chunks)),
        dma((2 * (hidden // LANE) + full // LANE,)),
        dma((2, 5)),
        dma((2, bits)),
        dma((2, bits)),
    ]
    hbm = pl.BlockSpec(memory_space=pl.ANY)
    inside = pl.BlockSpec(memory_space=pltpu.VMEM)
    return pl.pallas_call(
        functools.partial(layer_kernel, cfg),
        out_shape=(
            jax.ShapeDtypeStruct((batch, rows, 2 * LANE), BF),
            jax.ShapeDtypeStruct((batch, rows, 2 * LANE), BF),
            jax.ShapeDtypeStruct((full, hidden), BF),
            jax.ShapeDtypeStruct((hidden, full), BF),
            jax.ShapeDtypeStruct((2 * toks, 2 * LANE), BF),
            jax.ShapeDtypeStruct((16, half), F32),
        ),
        in_specs=[hbm, hbm] + [inside] * 8 + [hbm, hbm],
        out_specs=(hbm, hbm, hbm, hbm, inside, inside),
        scratch_shapes=scratch,
        compiler_params=pltpu.CompilerParams(
            collective_id=0, has_side_effects=True, vmem_limit_bytes=63 * 2**20
        ),
        name="mixer_layer",
    )(
        patches, cot, vec, hidden_bias, tok_in, tok_in.T, tok_out, tok_out.T, tok_in_bias, tok_out_bias, win, wout
    )


def per_device(
    n_dp,
    image_counts,
    patches,
    ln1_gain,
    ln1_bias,
    tok_in_weight,
    tok_in_bias,
    tok_out_weight,
    tok_out_bias,
    ln2_gain,
    ln2_bias,
    chan_in_weight,
    chan_in_bias,
    chan_out_weight,
    chan_out_bias,
    cotangent,
):
    count, batch, width = patches.shape
    rows = -(-count // 16) * 16
    c = lax.axis_index("seq") % 2
    spare = 2 * LANE - width
    valid = jnp.arange(batch, dtype=jnp.int32) < image_counts[0]

    def window(values):
        low = [(0, 0)] * (values.ndim - 1)
        return jnp.where(c == 0, jnp.pad(values, low + [(0, spare)]), jnp.pad(values, low + [(spare, 0)]))

    def images(values):
        moved = jnp.transpose(values, (1, 0, 2))
        return window(jnp.pad(moved, ((0, 0), (0, rows - count), (0, 0))))

    masked = jnp.where(valid[None, :, None], cotangent, jnp.zeros((), BF))
    vec = window(
        jnp.concatenate(
            [
                jnp.stack([ln1_gain, ln1_bias, ln2_gain, ln2_bias, chan_out_bias]),
                jnp.zeros((3, width), F32),
            ]
        )
    )
    pad = rows - count
    mixed, gin, gci, gco, tok, vecs = run_layer(
        n_dp,
        images(patches),
        images(masked),
        vec,
        chan_in_bias[None, :],
        jnp.pad(tok_in_weight, ((0, 0), (0, pad))),
        jnp.pad(tok_out_weight, ((0, pad), (0, 0))),
        tok_in_bias[:, None],
        jnp.pad(tok_out_bias, (0, pad))[:, None],
        chan_in_weight,
        chan_out_weight,
    )

    def rows_of(values):
        return jnp.transpose(
            lax.dynamic_slice_in_dim(values[:, :count], c * spare, width, axis=2), (1, 0, 2)
        )

    toks = tok_in_weight.shape[0]
    mine = lax.dynamic_slice_in_dim(vecs[:5], c * width, width, axis=1)
    result = jnp.where(valid[None, :, None], rows_of(mixed), jnp.zeros((), BF))
    tok = tok.astype(F32)
    return (
        result,
        rows_of(gin),
        mine[0],
        mine[1],
        tok[:toks, :count],
        tok[:toks, rows],
        tok[toks:, :count].T,
        tok[:count, rows + 1],
        mine[2],
        mine[3],
        gci.astype(F32),
        vecs[8:10].reshape(-1),
        gco.astype(F32),
        mine[4],
    )


def solution(mesh):
    in_specs = (
        P("dp"),
        P(None, "dp", "seq"),
        P("seq"),
        P("seq"),
        P(),
        P(),
        P(),
        P(),
        P("seq"),
        P("seq"),
        P(None, "seq"),
        P("seq"),
        P("seq", None),
        P("seq"),
        P(None, "dp", "seq"),
    )
    out_specs = (
        P(None, "dp", "seq"),
        P(None, "dp", "seq"),
        P("seq"),
        P("seq"),
        P(),
        P(),
        P(),
        P(),
        P("seq"),
        P("seq"),
        P(None, "seq"),
        P("seq"),
        P("seq", None),
        P("seq"),
    )
    return jax.shard_map(
        functools.partial(per_device, mesh.shape["dp"]),
        mesh=mesh,
        in_specs=in_specs,
        out_specs=out_specs,
        check_vma=False,
    )
```

```python
import functools

import jax
import jax.numpy as jnp
from jax import lax
from jax.experimental import pallas as pl
from jax.experimental.pallas import tpu as pltpu
from jax.sharding import PartitionSpec as P

MESH = pl.DeviceIdType.MESH
BF = jnp.bfloat16
F32 = jnp.float32
EPS = 1e-06
GELU_A = 0.7978845608028654
GELU_B = GELU_A * 0.044715
LANE = 128


def gelu_parts(x):
    square = x * x
    tanh = jnp.tanh(x * (GELU_A + GELU_B * square))
    half = 0.5 + 0.5 * tanh
    slope = half + (0.5 * x) * (1.0 - tanh * tanh) * (GELU_A + (3.0 * GELU_B) * square)
    return x * half, slope


def dot(a, b):
    return lax.dot_general(a, b, (((1,), (0,)), ((), ())), preferred_element_type=F32)


def dot_nt(a, b):
    return lax.dot_general(a, b, (((1,), (1,)), ((), ())), preferred_element_type=F32)


def dot_tn(a, b):
    return lax.dot_general(a, b, (((0,), (0,)), ((), ())), preferred_element_type=F32)


def diagonal(rows, columns):
    return lax.broadcasted_iota(jnp.int32, (rows, columns), 0) == lax.broadcasted_iota(
        jnp.int32, (rows, columns), 1
    )


def to_row(values, columns):
    return jnp.sum(jnp.where(diagonal(values.shape[0], columns), values, 0.0), axis=0, keepdims=True)


def to_column(values, rows):
    return jnp.sum(jnp.where(diagonal(rows, values.shape[1]), values, 0.0), axis=1, keepdims=True)


def row_sum(values):
    return jnp.sum(values, axis=-1, keepdims=True)


def layer_kernel(cfg, names, *refs):
    n_dp, own, count, rows, half, full, hidden, toks, chunks, chunk = cfg
    r = dict(zip(names, refs))
    width = half // 2
    d = lax.axis_index("dp")
    s = lax.axis_index("seq")
    c = s % 2
    x = s // 2
    core = (d, s + 1 - 2 * c)
    across = (d, s + 2 - 4 * x)
    folded = n_dp == 8
    bits = n_dp.bit_length() - 1

    def dp_bit(t):
        return (d // (1 << t)) % 2

    def dp_peer(t):
        m = 1 << t
        return (d + m - 2 * m * dp_bit(t), s)

    a = d // 2
    b = d % 2
    end = a % 3 == 0
    middle = a % 3 != 0
    m = a // 2
    side = dp_peer(0)
    fold = dp_peer(1)
    mirror = ((n_dp // 2 - 1 - a) * 2 + b, s)
    sum_peers = [side, fold, mirror] if folded else [dp_peer(t) for t in range(bits)]

    def remote(src, dst, sems, at, target):
        return pltpu.make_async_remote_copy(
            src_ref=src,
            dst_ref=dst,
            send_sem=r[sems].at[(0,) + at],
            recv_sem=r[sems].at[(1,) + at],
            device_id=target,
            device_id_type=MESH,
        )

    def local(src, dst, sems, at):
        return pltpu.make_async_copy(src, dst, r[sems].at[at])

    win, wout, pin, cin, raw = r["win"], r["wout"], r["pin"], r["cin"], r["raw"]
    ntb, gb, outp, outr, backp, backr = r["ntb"], r["gb"], r["outp"], r["outr"], r["backp"], r["backr"]
    outx, backx, s2o, s2x, s1o, s1x = r["outx"], r["backx"], r["s2o"], r["s2x"], r["s1o"], r["s1x"]
    vown, vother, tg, vg, vec_out = r["vown"], r["vother"], r["tg"], r["vg"], r["vec_out"]
    gbuf, fbuf, mos, gis = r["gbuf"], r["fbuf"], r["mos"], r["gis"]

    mine = pl.multiple_of(x * half, LANE)
    theirs = pl.multiple_of((1 - x) * half, LANE)
    weight_copies = [
        local(r["win_hbm"].at[pl.ds(mine, half)], win.at[pl.ds(0, half)], "sem_w", 0),
        local(r["win_hbm"].at[pl.ds(theirs, half)], win.at[pl.ds(half, half)], "sem_w", 1),
        local(r["wout_hbm"].at[:, pl.ds(mine, half)], wout.at[:, pl.ds(0, half)], "sem_w", 2),
        local(r["wout_hbm"].at[:, pl.ds(theirs, half)], wout.at[:, pl.ds(half, half)], "sem_w", 3),
    ]

    place = pl.ds(pl.multiple_of(c * width, 16), width)

    def p_local(j):
        return local(r["patches"].at[c * own + j], pin.at[j, place], "sem_pl", j)

    def c_local(j):
        return local(r["cot"].at[c * own + j], cin.at[j, place], "sem_cl", j)

    def p_swap(j):
        return remote(r["patches"].at[(1 - c) * own + j], pin.at[j, place], "sem_ps", (j,), core)

    def c_swap(j):
        return remote(r["cot"].at[(1 - c) * own + j], cin.at[j, place], "sem_cs", (j,), core)

    v_swap = remote(r["vmine"], r["vpart"], "sem_v", (0,), core)
    v_across = remote(vown, vother, "sem_v", (1,), across)

    first = pl.ds(0, rows)
    second = pl.ds(rows, rows)
    near = pl.ds(0, half)
    far = pl.ds(half, half)

    def p_across(j):
        return remote(raw.at[j, :, near], raw.at[j, :, far], "sem_px", (j,), across)

    def c_across(j):
        return remote(gb.at[j, first, near], gb.at[j, first, far], "sem_cx", (j,), across)

    def nt_share(j):
        return remote(ntb.at[j, first], ntb.at[j, second], "sem_nt", (j,), core)

    def g_share(j):
        return remote(gb.at[j, first], gb.at[j, second], "sem_g", (j,), core)

    def out_pair(j):
        return remote(outp.at[j, second], outr.at[j], "sem_op", (j,), core)

    def back_pair(j):
        return remote(backp.at[j, second], backr.at[j], "sem_bp", (j,), core)

    def out_across(j):
        return remote(outp.at[j, first, far], outx.at[j], "sem_ox", (j,), across)

    def back_across(j):
        return remote(backp.at[j, first, far], backx.at[j], "sem_bx", (j,), across)

    def s2_across(j):
        return remote(s2o.at[j], s2x.at[j], "sem_s2", (j,), across)

    def s1_across(j):
        return remote(s1o.at[j], s1x.at[j], "sem_s1", (j,), across)

    other = pl.ds(pl.multiple_of((1 - c) * width, 16), width)

    def mixed_give(j):
        return remote(mos.at[j, other], r["mixed"].at[c * own + j], "sem_mg", (j,), core)

    def gin_give(j):
        return remote(gis.at[j, other], r["gin"].at[c * own + j], "sem_gg", (j,), core)

    def mixed_keep(j):
        return local(mos.at[j, place], r["mixed"].at[c * own + j], "sem_mk", j)

    def gin_keep(j):
        return local(gis.at[j, place], r["gin"].at[c * own + j], "sem_gk", j)

    def span(start, size):
        return pl.ds(pl.multiple_of(start, 16), size)

    def add_into(target, at, source, source_at):
        target[at] = (gbuf[at].astype(F32) + r[source][source_at].astype(F32)).astype(BF)


    if folded:
        pairs = chunks // 2
        two, four = chunk // 2, chunk // 4

        def even(k):
            return 2 * k * chunk

        def e_side(k):
            return remote(
                gbuf.at[span(even(k) + (1 - b) * two, two)], r["e0"].at[span(k * two, two)], "sem_e0", (k,), side
            )

        def e_half(k):
            return span(even(k) + b * two, two)

        def e_fold(k):
            return remote(gbuf.at[e_half(k)], r["e1"].at[span(k * two, two)], "sem_e1", (k,), fold)

        def e_mirror(k):
            return remote(
                gbuf.at[span(even(k) + b * two + (1 - m) * four, four)],
                r["e2"].at[span(k * four, four)],
                "sem_e2",
                (k,),
                mirror,
            )

        def e_quarter(k):
            return span(even(k) + b * two + m * four, four)

        def e_mirror_back(k):
            return remote(fbuf.at[e_quarter(k)], fbuf.at[e_quarter(k)], "sem_e3", (k,), mirror)

        def e_fold_back(k):
            return remote(fbuf.at[e_half(k)], fbuf.at[e_half(k)], "sem_e4", (k,), fold)

        def e_side_back(k):
            return remote(fbuf.at[e_half(k)], fbuf.at[e_half(k)], "sem_e5", (k,), side)

        def odd(k):
            return (2 * k + 1) * chunk

        def o_fold(k):
            return remote(gbuf.at[span(odd(k), chunk)], r["o0"].at[span(k * chunk, chunk)], "sem_o0", (k,), fold)

        def o_mirror(k):
            return remote(
                gbuf.at[span(odd(k) + (1 - m) * two, two)], r["o1"].at[span(k * two, two)], "sem_o1", (k,), mirror
            )

        def o_half(k):
            return span(odd(k) + m * two, two)

        def o_rest(k):
            return span(odd(k) + (1 - m) * two, two)

        def o_side(k):
            return remote(
                gbuf.at[span(odd(k) + m * two + (1 - b) * four, four)],
                r["o2"].at[span(k * four, four)],
                "sem_o2",
                (k,),
                side,
            )

        def o_quarter(k):
            return span(odd(k) + m * two + b * four, four)

        def o_side_back(k):
            return remote(fbuf.at[o_quarter(k)], fbuf.at[o_quarter(k)], "sem_o3", (k,), side)

        def o_mirror_back(k):
            return remote(fbuf.at[o_half(k)], fbuf.at[o_half(k)], "sem_o4", (k,), mirror)

        def o_fold_back(k):
            return remote(fbuf.at[o_half(k)], fbuf.at[o_half(k)], "sem_o5", (k,), fold)

        def o_fold_rest(k):
            return remote(fbuf.at[o_rest(k)], fbuf.at[o_rest(k)], "sem_o6", (k,), fold)

        def e_step(e, k):
            if e == 0:
                e_side(k).wait_recv()
                add_into(gbuf, e_half(k), "e0", span(k * two, two))

                @pl.when(end)
                def _():
                    e_fold(k).start()

            elif e == 1:

                @pl.when(middle)
                def _():
                    e_fold(k).wait_recv()
                    add_into(gbuf, e_half(k), "e1", span(k * two, two))
                    e_mirror(k).start()

            elif e == 2:

                @pl.when(middle)
                def _():
                    e_mirror(k).wait_recv()
                    add_into(fbuf, e_quarter(k), "e2", span(k * four, four))
                    e_mirror_back(k).start()

            elif e == 3:

                @pl.when(middle)
                def _():
                    e_mirror_back(k).wait_recv()
                    e_fold_back(k).start()
                    e_side_back(k).start()

            else:

                @pl.when(end)
                def _():
                    e_fold_back(k).wait_recv()
                    e_side_back(k).start()

        def o_step(e, k):
            @pl.when(middle)
            def _():
                if e == 0:
                    o_fold(k).wait_recv()
                    add_into(gbuf, span(odd(k), chunk), "o0", span(k * chunk, chunk))
                    o_mirror(k).start()
                elif e == 1:
                    o_mirror(k).wait_recv()
                    add_into(gbuf, o_half(k), "o1", span(k * two, two))
                    o_side(k).start()
                elif e == 2:
                    o_side(k).wait_recv()
                    add_into(fbuf, o_quarter(k), "o2", span(k * four, four))
                    o_side_back(k).start()
                elif e == 3:
                    o_side_back(k).wait_recv()
                    o_mirror_back(k).start()
                    o_fold_back(k).start()
                else:
                    o_mirror_back(k).wait_recv()
                    o_fold_rest(k).start()

        stages = 5
        ahead = 3

        def o_first(k):
            @pl.when(end)
            def _():
                o_fold(k).start()

        def gradient_first():
            def start(k, carry):
                e_side(k).start()
                return carry

            lax.fori_loop(0, pairs, start, 0)
            for k in range(ahead):
                o_first(k)

        def gradient_step(i):
            @pl.when(i + ahead < pairs)
            def _():
                o_first(i + ahead)

            for e in reversed(range(stages)):
                k = i - e

                @pl.when((k >= 0) & (k < pairs))
                def _(e=e, k=k):
                    e_step(e, k)
                    o_step(e, k)

        def gradient_last(k):
            e_side_back(k).wait_recv()
            e_side(k).wait_send()
            e_side_back(k).wait_send()

            @pl.when(end)
            def _():
                o_fold_back(k).wait_recv()
                o_fold_rest(k).wait_recv()
                e_fold(k).wait_send()
                o_fold(k).wait_send()

            @pl.when(middle)
            def _():
                for make in (e_mirror, e_mirror_back, e_fold_back, o_mirror, o_side, o_side_back):
                    make(k).wait_send()
                for make in (o_mirror_back, o_fold_back, o_fold_rest):
                    make(k).wait_send()

        gradient_ticks = pairs + stages - 1
        gradient_items = pairs
    else:
        def segment(k, t):
            start = k * chunk
            for u in range(t):
                start = start + dp_bit(u) * (chunk >> (u + 1))
            return start

        bases = [chunks * (chunk - (chunk >> t)) for t in range(bits)]

        def rs_at(k, t):
            size = chunk >> (t + 1)
            return span(bases[t] + k * size, size)

        def rs_send(k, t):
            size = chunk >> (t + 1)
            return remote(
                gbuf.at[span(segment(k, t) + (1 - dp_bit(t)) * size, size)],
                r["rbuf"].at[rs_at(k, t)],
                "sem_rs",
                (t, k),
                dp_peer(t),
            )

        def ag_send(k, t):
            at = span(segment(k, t + 1), chunk >> (t + 1))
            return remote(fbuf.at[at], fbuf.at[at], "sem_ag", (t, k), dp_peer(t))

        def gradient_first():
            def start(k, carry):
                rs_send(k, 0).start()
                return carry

            lax.fori_loop(0, chunks, start, 0)

        def gradient_step(i):
            for e in reversed(range(2 * bits - 1)):
                k = i - e

                @pl.when((k >= 0) & (k < chunks))
                def _(e=e, k=k):
                    if e < bits:
                        rs_send(k, e).wait_recv()
                        at = span(segment(k, e + 1), chunk >> (e + 1))
                        add_into(gbuf if e + 1 < bits else fbuf, at, "rbuf", rs_at(k, e))
                        if e + 1 < bits:
                            rs_send(k, e + 1).start()
                        else:
                            ag_send(k, e).start()
                    else:
                        t = 2 * bits - 1 - e
                        ag_send(k, t).wait_recv()
                        ag_send(k, t - 1).start()

        def gradient_last(k):
            ag_send(k, 0).wait_recv()
            for t in range(bits):
                rs_send(k, t).wait_send()
                ag_send(k, t).wait_send()

        gradient_ticks = chunks + 2 * bits - 2
        gradient_items = chunks

    t_half = tg.shape[0] // 2
    t_quarter = t_half // 2
    tc_keep = span(c * t_half, t_half)
    tc_give = span((1 - c) * t_half, t_half)
    tx_keep = span(x * t_quarter, t_quarter)
    tx_give = span((1 - x) * t_quarter, t_quarter)
    t_mine = span(c * t_half + x * t_quarter, t_quarter)
    tb, tcore, tcur, txr, tdp, trd, tall = (r[n] for n in ("tb", "tcore", "tcur", "txr", "tdp", "trd", "tall"))
    vcore, vsend, vrd = r["vcore"], r["vsend"], r["vrd"]
    t_core = remote(tb.at[tc_give], tcore, "sem_t", (0,), core)
    t_across = remote(tcur.at[tx_give], txr, "sem_t", (1,), across)
    t_back_x = remote(tall.at[t_mine], tall.at[t_mine], "sem_t", (2,), across)
    t_back_c = remote(tall.at[tc_keep], tall.at[tc_keep], "sem_t", (3,), core)
    v_core = remote(vg.at[pl.ds(0, 8)], vcore, "sem_t", (4,), core)

    def t_dp(t):
        return remote(tdp.at[t], trd.at[t], "sem_td", (t,), sum_peers[t])

    def v_dp(t):
        return remote(vsend.at[t], vrd.at[t], "sem_vd", (t,), sum_peers[t])

    barrier = pltpu.get_barrier_semaphore()
    peers = [core, across] + sum_peers
    for peer in peers:
        pl.semaphore_signal(barrier, inc=1, device_id=peer, device_id_type=MESH)

    small_names = ("ln1_gain", "ln1_bias", "ln2_gain", "ln2_bias", "chan_out_bias")
    small_names += ("hidden_bias", "tok_in_bias", "tok_out_bias", "tok_in_raw", "tok_out_raw")
    small_copies = [local(r[n], r["in_" + n], "sem_small", at) for at, n in enumerate(small_names)]
    for copy in small_copies:
        copy.start()

    def start_local(j, carry):
        p_local(j).start()
        c_local(j).start()
        return carry

    lax.fori_loop(0, own, start_local, 0)
    for copy in weight_copies:
        copy.start()

    eye, wide = r["eye"], r["wide"]
    eye[...] = jnp.where(diagonal(rows, count), 1.0, 0.0).astype(BF)
    wide[...] = jnp.where(diagonal(half, half), 1.0, 0.0).astype(BF)
    gci, gco, cib = r["gci"], r["gco"], r["cib"]
    gci[...] = jnp.zeros_like(gci)
    gco[...] = jnp.zeros_like(gco)
    cib[...] = jnp.zeros_like(cib)
    tg[...] = jnp.zeros_like(tg)
    vg[...] = jnp.zeros_like(vg)
    s2o[...] = jnp.zeros_like(s2o)
    s1o[...] = jnp.zeros_like(s1o)
    for copy in small_copies:
        copy.wait()
    vpad = r["vpad"]
    vpad[...] = jnp.zeros_like(vpad)
    for at, name in enumerate(small_names[:5]):
        vpad[pl.ds(at, 1), pl.ds(0, width)] = r["in_" + name][...]
    vectors = vpad[...]
    r["vmine"][...] = jnp.where(c == 0, vectors, pltpu.roll(vectors, width, 1))
    hidden_bias = r["hidden_row"]
    for at in range(hidden // LANE):
        hidden_bias[:, pl.ds(at * LANE, LANE)] = r["in_hidden_bias"][pl.ds(at, 1), :]
    for at in range(toks // LANE):
        r["tok_row"][:, pl.ds(at * LANE, LANE)] = r["in_tok_in_bias"][pl.ds(at, 1), :]
    r["tib"][...] = to_column(r["tok_row"][...], toks)
    r["tob"][...] = to_column(r["in_tok_out_bias"][...], rows)
    tok_in_t, tok_in, tok_out, tok_out_t = r["tok_in_t"], r["tok_in"], r["tok_out"], r["tok_out_t"]
    tok_in_t[...] = dot(eye[...], r["in_tok_in_raw"][...]).astype(BF)
    tok_in[...] = dot_nt(wide[...], tok_in_t[...]).astype(BF)
    tok_out[...] = dot(eye[...], r["in_tok_out_raw"][...]).astype(BF)
    tok_out_t[...] = dot_nt(wide[...], tok_out[...]).astype(BF)

    pl.semaphore_wait(barrier, len(peers))

    def start_images(j, carry):
        p_swap(j).start()
        c_swap(j).start()
        return carry

    v_swap.start()
    lax.fori_loop(0, own, start_images, 0)

    def turn_in(ref, j):
        return dot_nt(eye[...], ref[j])

    def turn_out(values):
        return dot_nt(wide[...], values)[:, :count].astype(BF)

    def merge_send(j):
        p_swap(j).wait_recv()
        p_local(j).wait()
        raw[j, :, near] = turn_in(pin, j).astype(BF)
        p_across(j).start()
        c_swap(j).wait_recv()
        c_local(j).wait()
        valid = jnp.where(c * own + j < r["counts"][0], 1.0, 0.0)
        gb[j, first, near] = (turn_in(cin, j) * valid).astype(BF)
        c_across(j).start()

    merge_send(0)
    v_swap.wait_recv()
    vown[...] = r["vmine"][...] + r["vpart"][...]
    v_across.start()
    merge_send(1)
    merge_send(2)

    v_across.wait_recv()

    def vector(row):
        return jnp.concatenate([vown[pl.ds(row, 1), :], vother[pl.ds(row, 1), :]], axis=1)

    def normalise(values):
        centred = values - row_sum(values) * (1.0 / full)
        inverse = lax.rsqrt(row_sum(centred * centred) * (1.0 / full) + EPS)
        return centred * inverse, inverse

    def token_forward(j):
        values = raw[j].astype(F32)
        scaled, inverse = normalise(values)
        normed = (scaled * vector(0) + vector(1)).astype(BF)
        r["sc1"][j] = scaled[:, :half].astype(BF)
        r["inv1"][j] = inverse
        r["n1"][j] = normed[:, :half]
        act, slope = gelu_parts(dot(tok_in[...], normed) + r["tib"][...])
        act = act.astype(BF)
        r["ta"][j] = act[:, :half]
        r["tsl"][j] = slope[:, :half].astype(BF)
        mid = values + (dot(tok_out[...], act) + r["tob"][...])
        r["mid"][j] = mid[:, :half]
        scaled, inverse = normalise(mid)
        r["sc2"][j] = scaled[:, :half].astype(BF)
        r["inv2"][j] = inverse
        ntb[j, first] = (scaled * vector(2) + vector(3)).astype(BF)

    acts, ghs = r["acts"], r["ghs"]

    def channel(j):
        nt = ntb[j]
        g = gb[j]
        step = 256
        for at in range(hidden // step):
            cols = pl.ds(at * step, step)
            pre = dot(nt, win[:, cols]) + hidden_bias[:, cols]
            back = dot_nt(g, wout[cols, :])
            act, slope = gelu_parts(pre)
            acts[:, cols] = act.astype(BF)
            grad = (slope * back).astype(BF)
            ghs[:, cols] = grad
            cib[:, cols] += jnp.sum(grad.astype(F32), axis=0, keepdims=True)
        backp[j] = dot_nt(ghs[...], win[...]).astype(BF)
        back_pair(j).start()
        outp[j] = dot(acts[...], wout[...]).astype(BF)
        out_pair(j).start()
        gco[...] += dot_tn(acts[...], g)
        gci[...] += dot_tn(nt, ghs[...])

    def pair_sums(j):
        back_pair(j).wait_recv()
        total = backp[j, first].astype(F32) + backr[j].astype(F32)
        s2o[j, pl.ds(0, 1)] = to_row(row_sum(total * vector(2)), rows)
        s2o[j, pl.ds(1, 1)] = to_row(row_sum(total * (ntb[j, first].astype(F32) - vector(3))), rows)
        backp[j, first] = total.astype(BF)
        s2_across(j).start()
        back_across(j).start()

    def gather_phase(j, carry):
        @pl.when(j + 3 < own)
        def _():
            merge_send(j + 3)

        @pl.when(j < own)
        def _():
            p_across(j).wait_recv()
            token_forward(j)
            nt_share(j).start()
            c_across(j).wait_recv()
            g_share(j).start()

        @pl.when(j == 0)
        def _():
            for copy in weight_copies:
                copy.wait()

        @pl.when(j > 0)
        def _():
            nt_share(j - 1).wait_recv()
            g_share(j - 1).wait_recv()
            channel(j - 1)

        @pl.when(j > 1)
        def _():
            pair_sums(j - 2)

        return carry

    lax.fori_loop(0, own + 1, gather_phase, 0)

    tiles = hidden // LANE
    for at in range(tiles):
        gbuf[pl.ds(at * full, full)] = gci[:, pl.ds(at * LANE, LANE)].astype(BF)
    for at in range(full // LANE):
        gbuf[pl.ds(tiles * full + at * hidden, hidden)] = gco[:, pl.ds(at * LANE, LANE)].astype(BF)
    gradient_first()
    pair_sums(own - 1)

    def pair_outs(j):
        out_pair(j).wait_recv()
        total = outp[j, first].astype(F32) + outr[j].astype(F32)
        outp[j, first] = total.astype(BF)
        out_across(j).start()

    def norm_back(weighted, scaled, inverse, sums):
        mean = to_column(sums[0:1] * (1.0 / full), rows)
        slant = to_column(sums[1:2] * (1.0 / full), rows)
        return inverse * (weighted - mean - scaled * slant)

    def token_backward(j):
        s2_across(j).wait_recv()
        back_across(j).wait_recv()
        grad_normed = backp[j, first, near].astype(F32) + backx[j].astype(F32)
        scaled = r["sc2"][j].astype(F32)
        grad_out = gb[j, first, near].astype(F32)
        weighted = grad_normed * vown[pl.ds(2, 1), :]
        grad_mid = grad_out + norm_back(weighted, scaled, r["inv2"][j], s2o[j] + s2x[j])
        r["gm"][j] = grad_mid
        vg[pl.ds(2, 1), :] += jnp.sum(grad_normed * scaled, axis=0, keepdims=True)
        vg[pl.ds(3, 1), :] += jnp.sum(grad_normed, axis=0, keepdims=True)
        vg[pl.ds(4, 1), :] += jnp.sum(grad_out, axis=0, keepdims=True)
        low = grad_mid.astype(BF)
        ones = jnp.ones((8, half), BF)
        tg[pl.ds(rows, rows), :] += dot_nt(low, r["ta"][j])
        tg[pl.ds(2 * rows + 8, 8), pl.ds(0, rows)] += dot_nt(ones, low)
        grad_pre = (r["tsl"][j].astype(F32) * dot(tok_out_t[...], low)).astype(BF)
        tg[pl.ds(0, rows), :] += dot_nt(r["n1"][j], grad_pre)
        tg[pl.ds(2 * rows, 8), :] += dot_nt(ones, grad_pre)
        grad_one = dot(tok_in_t[...], grad_pre)
        scaled = r["sc1"][j].astype(F32)
        vg[pl.ds(0, 1), :] += jnp.sum(grad_one * scaled, axis=0, keepdims=True)
        vg[pl.ds(1, 1), :] += jnp.sum(grad_one, axis=0, keepdims=True)
        weighted = grad_one * vown[pl.ds(0, 1), :]
        r["w1"][j] = weighted
        s1o[j, pl.ds(0, 1)] = to_row(row_sum(weighted), rows)
        s1o[j, pl.ds(1, 1)] = to_row(row_sum(weighted * scaled), rows)
        s1_across(j).start()

    def input_grad(j):
        s1_across(j).wait_recv()
        scaled = r["sc1"][j].astype(F32)
        grad = r["gm"][j] + norm_back(r["w1"][j], scaled, r["inv1"][j], s1o[j] + s1x[j])
        gis[j] = turn_out(grad.astype(BF))
        gin_give(j).start()
        gin_keep(j).start()

    def mixed_part(j):
        out_across(j).wait_recv()
        total = outp[j, first, near].astype(F32) + outx[j].astype(F32)
        valid = jnp.where(c * own + j < r["counts"][0], 1.0, 0.0)
        mos[j] = turn_out((valid * (r["mid"][j] + (total + vown[pl.ds(4, 1), :]))).astype(BF))
        mixed_give(j).start()
        mixed_keep(j).start()

    def token_step(e):
        if e == 0:
            tb[...] = tg[...].astype(BF)
            for at in range(hidden // half):
                vg[pl.ds(8 + at, 1), :] = cib[:, pl.ds(at * half, half)]
            t_core.start()
            v_core.start()
        elif e == 1:
            t_core.wait_recv()
            v_core.wait_recv()
            tcur[...] = (tb[tc_keep].astype(F32) + tcore[...].astype(F32)).astype(BF)
            t_across.start()
            vsend[0, pl.ds(0, 8)] = vg[pl.ds(0, 8)] + vcore[...]
            vsend[0, pl.ds(8, 8)] = vg[pl.ds(8, 8)]
            v_dp(0).start()
        elif e == 2:
            t_across.wait_recv()
            tdp[0] = (tcur[tx_keep].astype(F32) + txr[...].astype(F32)).astype(BF)
            t_dp(0).start()
        elif e < 3 + bits:
            t = e - 3
            t_dp(t).wait_recv()
            v_dp(t).wait_recv()
            total = (tdp[t].astype(F32) + trd[t].astype(F32)).astype(BF)
            vec = vsend[t] + vrd[t]
            if t + 1 < bits:
                tdp[t + 1] = total
                vsend[t + 1] = vec
                t_dp(t + 1).start()
                v_dp(t + 1).start()
            else:
                tall[t_mine] = total
                t_back_x.start()
                vec_out[pl.ds(0, 8), :] = jnp.where(c == 0, vec, pltpu.roll(vec, width, 1))[:8]
                vec_out[pl.ds(8, 8), :] = vec[8:]
        elif e == 3 + bits:
            t_back_x.wait_recv()
            t_back_c.start()
        else:
            t_back_c.wait_recv()
            vec_out[pl.ds(16, 16), :] = tall[pl.ds(2 * rows, 16)].astype(F32)

    token_first = own
    token_steps = 5 + bits
    outs_first = own // 2
    mixed_first = 2 * own - 1

    def scatter_phase(i, carry):
        gradient_step(i)

        @pl.when(i < own)
        def _():
            token_backward(i)

        for e in range(token_steps):

            @pl.when(i == token_first + e)
            def _(e=e):
                token_step(e)

        @pl.when((i > 0) & (i <= own))
        def _():
            input_grad(i - 1)

        @pl.when((i >= outs_first) & (i < outs_first + own))
        def _():
            pair_outs(i - outs_first)

        @pl.when((i >= mixed_first) & (i < mixed_first + own))
        def _():
            mixed_part(i - mixed_first)

        return carry

    lax.fori_loop(0, max(gradient_ticks, token_first + token_steps, mixed_first + own), scatter_phase, 0)

    def gradient_end(k, carry):
        gradient_last(k)
        return carry

    lax.fori_loop(0, gradient_items, gradient_end, 0)

    outs = []
    for at in range(tiles):
        lanes = pl.ds(at * LANE, LANE)
        for part, to in enumerate((mine, theirs)):
            outs.append((fbuf.at[pl.ds(at * full + part * half, half)], r["g_chan_in"].at[pl.ds(to, half), lanes]))
    for at in range(full // LANE):
        to = mine if at < half // LANE else theirs
        lanes = pl.ds(pl.multiple_of(to + (at % (half // LANE)) * LANE, LANE), LANE)
        outs.append((fbuf.at[pl.ds(tiles * full + at * hidden, hidden)], r["g_chan_out"].at[:, lanes]))
    outs = [local(src, dst, "sem_out", at) for at, (src, dst) in enumerate(outs)]
    for copy in outs:
        copy.start()

    def drain(j, carry):
        for make in (p_swap, c_swap, p_across, c_across, nt_share, g_share, out_pair, back_pair):
            make(j).wait_send()
        for make in (out_across, back_across, s2_across, s1_across):
            make(j).wait_send()
        for make in (mixed_give, gin_give, mixed_keep, gin_keep):
            make(j).wait()
        return carry

    lax.fori_loop(0, own, drain, 0)
    for copy in [v_swap, v_across, t_core, t_across, t_back_x, t_back_c, v_core]:
        copy.wait_send()
    for t in range(bits):
        t_dp(t).wait_send()
        v_dp(t).wait_send()
    for copy in outs:
        copy.wait()


def run_layer(n_dp, **arrays):
    batch, width, count = arrays["patches"].shape
    own = batch // 2
    full, hidden = arrays["win_hbm"].shape
    half = full // 2
    toks = arrays["tok_in_raw"].shape[1]
    rows = -(-count // 16) * 16
    bits = n_dp.bit_length() - 1
    grad_rows = 2 * full * hidden // LANE
    folded = n_dp == 8
    choices = (24, 12, 6, 2) if folded else (9, 3, 1)
    parts = 4 if folded else n_dp
    chunks = next(k for k in choices if grad_rows % (k * parts * 16) == 0)
    chunk = grad_rows // chunks
    cfg = (n_dp, own, count, rows, half, full, hidden, toks, chunks, chunk)
    vmem = pltpu.VMEM
    dma = pltpu.SemaphoreType.DMA
    pairs = chunks // 2
    two, four = chunk // 2, chunk // 4
    t_rows = -(-(2 * rows + 16) // 64) * 64
    scratch = {
        "win": vmem((full, hidden), BF),
        "wout": vmem((hidden, full), BF),
        "pin": vmem((own, half, count), BF),
        "cin": vmem((own, half, count), BF),
        "vpad": vmem((8, half), F32),
        "hidden_row": vmem((1, hidden), F32),
        "tok_row": vmem((1, toks), F32),
        "vmine": vmem((8, half), F32),
        "vpart": vmem((8, half), F32),
        "vown": vmem((8, half), F32),
        "vother": vmem((8, half), F32),
        "eye": vmem((rows, count), BF),
        "wide": vmem((half, half), BF),
        "tok_in_t": vmem((rows, toks), BF),
        "tok_in": vmem((toks, rows), BF),
        "tok_out": vmem((rows, toks), BF),
        "tok_out_t": vmem((toks, rows), BF),
        "tib": vmem((toks, 1), F32),
        "tob": vmem((rows, 1), F32),
        "raw": vmem((own, rows, full), BF),
        "ntb": vmem((own, 2 * rows, full), BF),
        "gb": vmem((own, 2 * rows, full), BF),
        "acts": vmem((2 * rows, hidden), BF),
        "ghs": vmem((2 * rows, hidden), BF),
        "gci": vmem((full, hidden), F32),
        "gco": vmem((hidden, full), F32),
        "cib": vmem((1, hidden), F32),
        "outp": vmem((own, 2 * rows, full), BF),
        "outr": vmem((own, rows, full), BF),
        "backp": vmem((own, 2 * rows, full), BF),
        "backr": vmem((own, rows, full), BF),
        "outx": vmem((own, rows, half), BF),
        "backx": vmem((own, rows, half), BF),
        "s2o": vmem((own, 8, rows), F32),
        "s2x": vmem((own, 8, rows), F32),
        "s1o": vmem((own, 8, rows), F32),
        "s1x": vmem((own, 8, rows), F32),
        "n1": vmem((own, rows, half), BF),
        "ta": vmem((own, toks, half), BF),
        "tsl": vmem((own, toks, half), BF),
        "mid": vmem((own, rows, half), F32),
        "sc1": vmem((own, rows, half), BF),
        "sc2": vmem((own, rows, half), BF),
        "inv1": vmem((own, rows, 1), F32),
        "inv2": vmem((own, rows, 1), F32),
        "gm": vmem((own, rows, half), F32),
        "w1": vmem((own, rows, half), F32),
        "gis": vmem((own, half, count), BF),
        "mos": vmem((own, half, count), BF),
        "gbuf": vmem((grad_rows, LANE), BF),
        "fbuf": vmem((grad_rows, LANE), BF),
        "tg": vmem((t_rows, toks), F32),
        "tb": vmem((t_rows, toks), BF),
        "tcore": vmem((t_rows // 2, toks), BF),
        "tcur": vmem((t_rows // 2, toks), BF),
        "txr": vmem((t_rows // 4, toks), BF),
        "tdp": vmem((bits, t_rows // 4, toks), BF),
        "trd": vmem((bits, t_rows // 4, toks), BF),
        "vg": vmem((16, half), F32),
        "vcore": vmem((8, half), F32),
        "vsend": vmem((bits, 16, half), F32),
        "vrd": vmem((bits, 16, half), F32),
        "sem_w": dma((4,)),
        "sem_small": dma((10,)),
        "sem_v": dma((2, 2)),
        "sem_out": dma((2 * (hidden // LANE) + full // LANE,)),
        "sem_t": dma((2, 5)),
        "sem_td": dma((2, bits)),
        "sem_vd": dma((2, bits)),
    }
    for name in arrays:
        if name not in ("counts", "patches", "cot", "win_hbm", "wout_hbm"):
            scratch["in_" + name] = vmem(arrays[name].shape, arrays[name].dtype)
    for name in ("pl", "cl", "mk", "gk"):
        scratch["sem_" + name] = dma((own,))
    for name in ("ps", "cs", "px", "cx", "nt", "g", "op", "bp", "ox", "bx", "s2", "s1", "mg", "gg"):
        scratch["sem_" + name] = dma((2, own))
    if folded:
        scratch["e0"] = vmem((pairs * two, LANE), BF)
        scratch["e1"] = vmem((pairs * two, LANE), BF)
        scratch["e2"] = vmem((pairs * four, LANE), BF)
        scratch["o0"] = vmem((pairs * chunk, LANE), BF)
        scratch["o1"] = vmem((pairs * two, LANE), BF)
        scratch["o2"] = vmem((pairs * four, LANE), BF)
        for name in ("e0", "e1", "e2", "e3", "e4", "e5", "o0", "o1", "o2", "o3", "o4", "o5", "o6"):
            scratch["sem_" + name] = dma((2, pairs))
    else:
        scratch["rbuf"] = vmem((chunks * (chunk - (chunk >> bits)), LANE), BF)
        scratch["sem_rs"] = dma((2, bits, chunks))
        scratch["sem_ag"] = dma((2, bits, chunks))
    hbm = pl.BlockSpec(memory_space=pl.ANY)
    inside = pl.BlockSpec(memory_space=pltpu.VMEM)
    places = {"counts": pl.BlockSpec(memory_space=pltpu.SMEM), "tall": inside, "vec_out": inside}
    outs = {
        "mixed": ((batch, width, count), BF),
        "gin": ((batch, width, count), BF),
        "tall": ((t_rows, toks), BF),
        "vec_out": ((32, half), F32),
        "g_chan_in": ((full, hidden), BF),
        "g_chan_out": ((hidden, full), BF),
    }
    names = list(arrays) + list(outs) + list(scratch)
    results = pl.pallas_call(
        functools.partial(layer_kernel, cfg, names),
        out_shape=tuple(jax.ShapeDtypeStruct(*outs[name]) for name in outs),
        in_specs=[places.get(name, hbm) for name in arrays],
        out_specs=tuple(places.get(name, hbm) for name in outs),
        scratch_shapes=list(scratch.values()),
        compiler_params=pltpu.CompilerParams(
            collective_id=0, has_side_effects=True, vmem_limit_bytes=63 * 2**20
        ),
        name="mixer_layer",
    )(*arrays.values())
    return dict(zip(outs, results))


def finish_kernel(names, *refs):
    r = dict(zip(names, refs))
    sems = r["sems"]
    count, toks = r["tok_in"].shape
    rows = -(-count // 16) * 16
    parts = r["pieces"].shape[1]
    step = r["pieces"].shape[2]
    loads, stores = [], []
    whole_in, whole_out = [], []
    for at, name in enumerate(("mixed", "gin")):
        for part in range(2):
            here = pl.ds(part * (r["images"].shape[1] // 2), r["images"].shape[1] // 2)
            sem = 2 + 4 * parts + 4 * at + 2 * part
            whole_in.append(pltpu.make_async_copy(r[name + "_raw"].at[here], r["images"].at[at, here], sems.at[sem]))
            whole_out.append(pltpu.make_async_copy(r["images"].at[at, here], r[name].at[here], sems.at[sem + 1]))
    for at, name in enumerate(("chan_in", "chan_out")):
        for part in range(parts):
            here = pl.ds(part * step, step)
            sem = 2 + at * parts + part
            loads.append(pltpu.make_async_copy(r[name + "_raw"].at[here], r["pieces"].at[at, part], sems.at[sem]))
            stores.append(
                pltpu.make_async_copy(r["wide"].at[at, part], r[name].at[here], sems.at[sem + 2 * parts])
            )
    for copy in loads + whole_in:
        copy.start()
    for at in range(len(loads)):
        loads[at].wait()
        r["wide"][at // parts, at % parts] = r["pieces"][at // parts, at % parts].astype(F32)
        stores[at].start()
    for at in range(len(whole_in)):
        whole_in[at].wait()
        whole_out[at].start()
    vec, tall = r["vec_raw"], r["tok_raw"]
    width = r["ln1_gain"].shape[1]
    for at, name in enumerate(("ln1_gain", "ln1_bias", "ln2_gain", "ln2_bias", "chan_out_bias")):
        r[name][...] = vec[pl.ds(at, 1), :][:, :width]
    half = vec.shape[1]
    for at in range(r["chan_in_bias"].shape[0]):
        row, lane = divmod(at * LANE, half)
        r["chan_in_bias"][pl.ds(at, 1), :] = vec[pl.ds(8 + row, 1), pl.ds(lane, LANE)]
    for at in range(toks // LANE):
        r["tok_in_bias"][pl.ds(at, 1), :] = vec[pl.ds(16, 1), pl.ds(at * LANE, LANE)]
    r["tok_out_bias"][...] = vec[pl.ds(24, 1), :][:, :count]
    r["tok_in"][...] = tall[pl.ds(0, rows)][:count].astype(F32)
    r["tok_out"][...] = tall[pl.ds(rows, rows)][:count].astype(F32)
    for copy in stores + whole_out:
        copy.wait()


def finish(out, count, width):
    full, hidden = out["g_chan_in"].shape
    toks = out["tall"].shape[1]
    hbm = pl.BlockSpec(memory_space=pl.ANY)
    inside = pl.BlockSpec(memory_space=pltpu.VMEM)
    arrays = {
        "mixed_raw": out["mixed"],
        "gin_raw": out["gin"],
        "chan_in_raw": out["g_chan_in"],
        "chan_out_raw": out["g_chan_out"],
        "tok_raw": out["tall"],
        "vec_raw": out["vec_out"],
    }
    outs = {
        "mixed": (out["mixed"].shape, BF),
        "gin": (out["gin"].shape, BF),
        "chan_in": ((full, hidden), F32),
        "chan_out": ((hidden, full), F32),
        "ln1_gain": ((1, width), F32),
        "ln1_bias": ((1, width), F32),
        "ln2_gain": ((1, width), F32),
        "ln2_bias": ((1, width), F32),
        "chan_out_bias": ((1, width), F32),
        "chan_in_bias": ((hidden // LANE, LANE), F32),
        "tok_in_bias": ((toks // LANE, LANE), F32),
        "tok_out_bias": ((1, count), F32),
        "tok_in": ((count, toks), F32),
        "tok_out": ((count, toks), F32),
    }
    parts = 4
    scratch = {
        "pieces": pltpu.VMEM((2, parts, full // parts, hidden), BF),
        "wide": pltpu.VMEM((2, parts, full // parts, hidden), F32),
        "images": pltpu.VMEM((2,) + out["mixed"].shape, BF),
        "sems": pltpu.SemaphoreType.DMA((10 + 4 * parts,)),
    }
    names = list(arrays) + list(outs) + list(scratch)
    results = pl.pallas_call(
        functools.partial(finish_kernel, names),
        out_shape=tuple(jax.ShapeDtypeStruct(*outs[name]) for name in outs),
        in_specs=[hbm] * 4 + [inside] * 2,
        out_specs=(hbm,) * 4 + (inside,) * 10,
        scratch_shapes=list(scratch.values()),
        compiler_params=pltpu.CompilerParams(vmem_limit_bytes=63 * 2**20),
        name="finish",
    )(*arrays.values())
    return dict(zip(outs, results))


def per_device(
    n_dp,
    image_counts,
    patches,
    ln1_gain,
    ln1_bias,
    tok_in_weight,
    tok_in_bias,
    tok_out_weight,
    tok_out_bias,
    ln2_gain,
    ln2_bias,
    chan_in_weight,
    chan_in_bias,
    chan_out_weight,
    chan_out_bias,
    cotangent,
):
    out = run_layer(
        n_dp,
        counts=image_counts,
        patches=jnp.transpose(patches, (1, 2, 0)),
        cot=jnp.transpose(cotangent, (1, 2, 0)),
        ln1_gain=ln1_gain[None, :],
        ln1_bias=ln1_bias[None, :],
        ln2_gain=ln2_gain[None, :],
        ln2_bias=ln2_bias[None, :],
        chan_out_bias=chan_out_bias[None, :],
        hidden_bias=chan_in_bias.reshape(-1, LANE),
        tok_in_bias=tok_in_bias.reshape(-1, LANE),
        tok_out_bias=tok_out_bias[None, :],
        tok_in_raw=tok_in_weight.T,
        tok_out_raw=tok_out_weight,
        win_hbm=chan_in_weight,
        wout_hbm=chan_out_weight,
    )
    out = finish(out, patches.shape[0], patches.shape[2])
    return (
        jnp.transpose(out["mixed"], (2, 0, 1)),
        jnp.transpose(out["gin"], (2, 0, 1)),
        out["ln1_gain"][0],
        out["ln1_bias"][0],
        out["tok_in"].T,
        out["tok_in_bias"].reshape(-1),
        out["tok_out"],
        out["tok_out_bias"][0],
        out["ln2_gain"][0],
        out["ln2_bias"][0],
        out["chan_in"],
        out["chan_in_bias"].reshape(-1),
        out["chan_out"],
        out["chan_out_bias"][0],
    )


def solution(mesh):
    in_specs = (
        P("dp"),
        P(None, "dp", "seq"),
        P("seq"),
        P("seq"),
        P(),
        P(),
        P(),
        P(),
        P("seq"),
        P("seq"),
        P(None, "seq"),
        P("seq"),
        P("seq", None),
        P("seq"),
        P(None, "dp", "seq"),
    )
    out_specs = (
        P(None, "dp", "seq"),
        P(None, "dp", "seq"),
        P("seq"),
        P("seq"),
        P(),
        P(),
        P(),
        P(),
        P("seq"),
        P("seq"),
        P(None, "seq"),
        P("seq"),
        P("seq", None),
        P("seq"),
    )
    return jax.shard_map(
        functools.partial(per_device, mesh.shape["dp"]),
        mesh=mesh,
        in_specs=in_specs,
        out_specs=out_specs,
        check_vma=False,
    )
```

```python
import functools
from types import SimpleNamespace

import jax
import jax.numpy as jnp
from jax import lax
from jax.experimental import pallas as pl
from jax.experimental.pallas import tpu as pltpu
from jax.sharding import PartitionSpec as P

MESH = pl.DeviceIdType.MESH
BF = jnp.bfloat16
F32 = jnp.float32
EPS = 1e-06
GELU_A = 0.7978845608028654
GELU_B = GELU_A * 0.044715
LANE = 128


def gelu_parts(x):
    square = x * x
    tanh = jnp.tanh(x * (GELU_A + GELU_B * square))
    half = 0.5 + 0.5 * tanh
    slope = half + (0.5 * x) * (1.0 - tanh * tanh) * (GELU_A + (3.0 * GELU_B) * square)
    return x * half, slope


def gelu(x):
    return x * (0.5 + 0.5 * jnp.tanh(x * (GELU_A + GELU_B * (x * x))))


def dot(a, b):
    return lax.dot_general(a, b, (((1,), (0,)), ((), ())), preferred_element_type=F32)


def dot_nt(a, b):
    return lax.dot_general(a, b, (((1,), (1,)), ((), ())), preferred_element_type=F32)


def dot_tn(a, b):
    return lax.dot_general(a, b, (((0,), (0,)), ((), ())), preferred_element_type=F32)


def diagonal(rows, columns):
    return lax.broadcasted_iota(jnp.int32, (rows, columns), 0) == lax.broadcasted_iota(
        jnp.int32, (rows, columns), 1
    )


def to_row(values, columns):
    return jnp.sum(jnp.where(diagonal(values.shape[0], columns), values, 0.0), axis=0, keepdims=True)


def to_column(values, rows):
    return jnp.sum(jnp.where(diagonal(rows, values.shape[1]), values, 0.0), axis=1, keepdims=True)


def row_sum(values):
    return jnp.sum(values, axis=-1, keepdims=True)


def layer_kernel(cfg, names, *refs):
    n_dp, own, count, rows, half, full, hidden, toks, chunks, chunk = cfg
    r = SimpleNamespace(**dict(zip(names, refs)))
    width = half // 2
    d = lax.axis_index("dp")
    s = lax.axis_index("seq")
    c = s % 2
    x = s // 2
    core = (d, s + 1 - 2 * c)
    across = (d, s + 2 - 4 * x)
    folded = n_dp == 8
    bits = n_dp.bit_length() - 1

    def dp_bit(t):
        return (d // (1 << t)) % 2

    def dp_peer(t):
        m = 1 << t
        return (d + m - 2 * m * dp_bit(t), s)

    a = d // 2
    b = d % 2
    end = a % 3 == 0
    middle = a % 3 != 0
    m = a // 2
    side = dp_peer(0)
    fold = dp_peer(1)
    mirror = ((n_dp // 2 - 1 - a) * 2 + b, s)
    sum_peers = [side, fold, mirror] if folded else [dp_peer(t) for t in range(bits)]

    def remote(src, dst, sems, at, target):
        return pltpu.make_async_remote_copy(
            src_ref=src,
            dst_ref=dst,
            send_sem=sems.at[(0,) + at],
            recv_sem=sems.at[(1,) + at],
            device_id=target,
            device_id_type=MESH,
        )

    def local(src, dst, sems, at):
        return pltpu.make_async_copy(src, dst, sems.at[at])

    win, wout, pin, cin, raw = r.win, r.wout, r.pin, r.cin, r.raw
    ntb, gb, outp, outr, backp, backr = r.ntb, r.gb, r.outp, r.outr, r.backp, r.backr
    outx, backx, s2o, s2x, s1o, s1x = r.outx, r.backx, r.s2o, r.s2x, r.s1o, r.s1x
    vown, vother, tg, vg, vec_out = r.vown, r.vother, r.tg, r.vg, r.vec_out
    gbuf, fbuf = r.gbuf, r.fbuf
    mos, gis = pin, cin

    mine = pl.multiple_of(x * half, LANE)
    theirs = pl.multiple_of((1 - x) * half, LANE)
    weight_copies = [
        local(r.win_hbm.at[pl.ds(mine, half)], win.at[pl.ds(0, half)], r.sem_w, 0),
        local(r.win_hbm.at[pl.ds(theirs, half)], win.at[pl.ds(half, half)], r.sem_w, 1),
        local(r.wout_hbm.at[:, pl.ds(mine, half)], wout.at[:, pl.ds(0, half)], r.sem_w, 2),
        local(r.wout_hbm.at[:, pl.ds(theirs, half)], wout.at[:, pl.ds(half, half)], r.sem_w, 3),
    ]

    place = pl.ds(pl.multiple_of(c * width, 16), width)

    def p_local(j):
        return local(r.patches.at[c * own + j], pin.at[j, place], r.sem_pl, j)

    def c_local(j):
        return local(r.cot.at[c * own + j], cin.at[j, place], r.sem_cl, j)

    def p_swap(j):
        return remote(r.patches.at[(1 - c) * own + j], pin.at[j, place], r.sem_ps, (j,), core)

    def c_swap(j):
        return remote(r.cot.at[(1 - c) * own + j], cin.at[j, place], r.sem_cs, (j,), core)

    v_swap = remote(r.vmine, r.vpart, r.sem_v, (0,), core)
    v_across = remote(vown, vother, r.sem_v, (1,), across)

    first = pl.ds(0, rows)
    second = pl.ds(rows, rows)
    near = pl.ds(0, half)
    far = pl.ds(half, half)

    def p_across(j):
        return remote(raw.at[j, :, near], raw.at[j, :, far], r.sem_px, (j,), across)

    def c_across(j):
        return remote(gb.at[j, first, near], gb.at[j, first, far], r.sem_cx, (j,), across)

    def nt_share(j):
        return remote(ntb.at[j, first], ntb.at[j, second], r.sem_nt, (j,), core)

    def g_share(j):
        return remote(gb.at[j, first], gb.at[j, second], r.sem_g, (j,), core)

    def out_pair(j):
        return remote(outp.at[j, second], outr.at[j], r.sem_op, (j,), core)

    def back_pair(j):
        return remote(backp.at[j, second], backr.at[j], r.sem_bp, (j,), core)

    def out_across(j):
        return remote(outp.at[j, first, far], outx.at[j], r.sem_ox, (j,), across)

    def back_across(j):
        return remote(backp.at[j, first, far], backx.at[j], r.sem_bx, (j,), across)

    def s2_across(j):
        return remote(s2o.at[j], s2x.at[j], r.sem_s2, (j,), across)

    def s1_across(j):
        return remote(s1o.at[j], s1x.at[j], r.sem_s1, (j,), across)

    other = pl.ds(pl.multiple_of((1 - c) * width, 16), width)

    def mixed_give(j):
        return remote(mos.at[j, other], r.mixed.at[c * own + j], r.sem_mg, (j,), core)

    def gin_give(j):
        return remote(gis.at[j, other], r.gin.at[c * own + j], r.sem_gg, (j,), core)

    def mixed_keep(j):
        return local(mos.at[j, place], r.mixed.at[c * own + j], r.sem_mk, j)

    def gin_keep(j):
        return local(gis.at[j, place], r.gin.at[c * own + j], r.sem_gk, j)

    def span(start, size):
        return pl.ds(pl.multiple_of(start, 16), size)

    def add_into(target, at, source, source_at):
        target[at] = (gbuf[at].astype(F32) + source[source_at].astype(F32)).astype(BF)


    if folded:
        pairs = chunks
        two, four = chunk * 13 // 36, chunk * 13 // 72

        def even(k):
            return k * chunk

        def e_side(k):
            return remote(
                gbuf.at[span(even(k) + (1 - b) * two, two)], r.e0.at[span(k * two, two)], r.sem_e0, (k,), side
            )

        def e_half(k):
            return span(even(k) + b * two, two)

        def e_fold(k):
            return remote(gbuf.at[e_half(k)], r.e1.at[span(k * two, two)], r.sem_e1, (k,), fold)

        def e_mirror(k):
            return remote(
                gbuf.at[span(even(k) + b * two + (1 - m) * four, four)],
                r.e2.at[span(k * four, four)],
                r.sem_e2,
                (k,),
                mirror,
            )

        def e_quarter(k):
            return span(even(k) + b * two + m * four, four)

        def e_mirror_back(k):
            return remote(fbuf.at[e_quarter(k)], fbuf.at[e_quarter(k)], r.sem_e3, (k,), mirror)

        def e_fold_back(k):
            return remote(fbuf.at[e_half(k)], fbuf.at[e_half(k)], r.sem_e4, (k,), fold)

        def e_side_back(k):
            return remote(fbuf.at[e_half(k)], fbuf.at[e_half(k)], r.sem_e5, (k,), side)

        whole, three, six = chunk * 5 // 18, chunk * 5 // 36, chunk * 5 // 72

        def odd(k):
            return k * chunk + 2 * two

        def o_fold(k):
            return remote(gbuf.at[span(odd(k), whole)], r.o0.at[span(k * whole, whole)], r.sem_o0, (k,), fold)

        def o_mirror(k):
            return remote(
                gbuf.at[span(odd(k) + (1 - m) * three, three)],
                r.o1.at[span(k * three, three)],
                r.sem_o1,
                (k,),
                mirror,
            )

        def o_half(k):
            return span(odd(k) + m * three, three)

        def o_rest(k):
            return span(odd(k) + (1 - m) * three, three)

        def o_side(k):
            return remote(
                gbuf.at[span(odd(k) + m * three + (1 - b) * six, six)],
                r.o2.at[span(k * six, six)],
                r.sem_o2,
                (k,),
                side,
            )

        def o_quarter(k):
            return span(odd(k) + m * three + b * six, six)

        def o_side_back(k):
            return remote(fbuf.at[o_quarter(k)], fbuf.at[o_quarter(k)], r.sem_o3, (k,), side)

        def o_mirror_back(k):
            return remote(fbuf.at[o_half(k)], fbuf.at[o_half(k)], r.sem_o4, (k,), mirror)

        def o_fold_back(k):
            return remote(fbuf.at[o_half(k)], fbuf.at[o_half(k)], r.sem_o5, (k,), fold)

        def o_fold_rest(k):
            return remote(fbuf.at[o_rest(k)], fbuf.at[o_rest(k)], r.sem_o6, (k,), fold)

        def e_step(e, k):
            if e == 0:
                e_side(k).wait_recv()
                add_into(gbuf, e_half(k), r.e0, span(k * two, two))

                @pl.when(end)
                def _():
                    e_fold(k).start()

            elif e == 1:

                @pl.when(middle)
                def _():
                    e_fold(k).wait_recv()
                    add_into(gbuf, e_half(k), r.e1, span(k * two, two))
                    e_mirror(k).start()

            elif e == 2:

                @pl.when(middle)
                def _():
                    e_mirror(k).wait_recv()
                    add_into(fbuf, e_quarter(k), r.e2, span(k * four, four))
                    e_mirror_back(k).start()

            elif e == 3:

                @pl.when(middle)
                def _():
                    e_mirror_back(k).wait_recv()
                    e_fold_back(k).start()
                    e_side_back(k).start()

            else:

                @pl.when(end)
                def _():
                    e_fold_back(k).wait_recv()
                    e_side_back(k).start()

        def o_step(e, k):
            @pl.when(middle)
            def _():
                if e == 0:
                    o_fold(k).wait_recv()
                    add_into(gbuf, span(odd(k), whole), r.o0, span(k * whole, whole))
                    o_mirror(k).start()
                elif e == 1:
                    o_mirror(k).wait_recv()
                    add_into(gbuf, o_half(k), r.o1, span(k * three, three))
                    o_side(k).start()
                elif e == 2:
                    o_side(k).wait_recv()
                    add_into(fbuf, o_quarter(k), r.o2, span(k * six, six))
                    o_side_back(k).start()
                elif e == 3:
                    o_side_back(k).wait_recv()
                    o_mirror_back(k).start()
                    o_fold_back(k).start()
                else:
                    o_mirror_back(k).wait_recv()
                    o_fold_rest(k).start()

        e_at = (0, 1, 2, 3, 5)
        o_at = (2, 3, 4, 5, 6)

        def o_first(k):
            @pl.when(end)
            def _():
                o_fold(k).start()

        def gradient_first(before, ready):
            for k in range(pairs):
                if before < (k + 1) * chunk <= ready:
                    e_side(k).start()

        def gradient_step(i):
            @pl.when(i < pairs)
            def _():
                o_first(i)

            for stage, places in ((o_step, o_at), (e_step, e_at)):
                for e, at in enumerate(places):

                    @pl.when((i >= at) & (i < at + pairs))
                    def _(stage=stage, e=e, at=at):
                        stage(e, i - at)

        def gradient_last(k):
            e_side_back(k).wait_recv()
            e_side(k).wait_send()
            e_side_back(k).wait_send()

            @pl.when(end)
            def _():
                o_fold_back(k).wait_recv()
                o_fold_rest(k).wait_recv()
                e_fold(k).wait_send()
                o_fold(k).wait_send()

            @pl.when(middle)
            def _():
                for make in (e_mirror, e_mirror_back, e_fold_back, o_mirror, o_side, o_side_back):
                    make(k).wait_send()
                for make in (o_mirror_back, o_fold_back, o_fold_rest):
                    make(k).wait_send()

        gradient_ticks = pairs + max(e_at[-1], o_at[-1])
        gradient_items = pairs
    else:
        def segment(k, t):
            start = k * chunk
            for u in range(t):
                start = start + dp_bit(u) * (chunk >> (u + 1))
            return start

        bases = [chunks * (chunk - (chunk >> t)) for t in range(bits)]

        def rs_at(k, t):
            size = chunk >> (t + 1)
            return span(bases[t] + k * size, size)

        def rs_send(k, t):
            size = chunk >> (t + 1)
            return remote(
                gbuf.at[span(segment(k, t) + (1 - dp_bit(t)) * size, size)],
                r.rbuf.at[rs_at(k, t)],
                r.sem_rs,
                (t, k),
                dp_peer(t),
            )

        def ag_send(k, t):
            at = span(segment(k, t + 1), chunk >> (t + 1))
            return remote(fbuf.at[at], fbuf.at[at], r.sem_ag, (t, k), dp_peer(t))

        def gradient_first(before, ready):
            for k in range(chunks):
                if before < (k + 1) * chunk <= ready:
                    rs_send(k, 0).start()

        def gradient_step(i):
            for e in reversed(range(2 * bits - 1)):
                k = i - e

                @pl.when((k >= 0) & (k < chunks))
                def _(e=e, k=k):
                    if e < bits:
                        rs_send(k, e).wait_recv()
                        at = span(segment(k, e + 1), chunk >> (e + 1))
                        add_into(gbuf if e + 1 < bits else fbuf, at, r.rbuf, rs_at(k, e))
                        if e + 1 < bits:
                            rs_send(k, e + 1).start()
                        else:
                            ag_send(k, e).start()
                    else:
                        t = 2 * bits - 1 - e
                        ag_send(k, t).wait_recv()
                        ag_send(k, t - 1).start()

        def gradient_last(k):
            ag_send(k, 0).wait_recv()
            for t in range(bits):
                rs_send(k, t).wait_send()
                ag_send(k, t).wait_send()

        gradient_ticks = chunks + 2 * bits - 2
        gradient_items = chunks

    t_half = tg.shape[0] // 2
    t_quarter = t_half // 2
    tc_keep = span(c * t_half, t_half)
    tc_give = span((1 - c) * t_half, t_half)
    tx_keep = span(x * t_quarter, t_quarter)
    tx_give = span((1 - x) * t_quarter, t_quarter)
    t_mine = span(c * t_half + x * t_quarter, t_quarter)
    tb, tcore, tcur, txr, tdp, trd, tall = r.tb, r.tcore, r.tcur, r.txr, r.tdp, r.trd, r.tall
    vcore, tfin = r.vcore, r.tfin
    t_core = remote(tb.at[tc_give], tcore, r.sem_t, (0,), core)
    t_across = remote(tcur.at[tx_give], txr, r.sem_t, (1,), across)
    t_back_x = remote(tall.at[t_mine], tall.at[t_mine], r.sem_t, (2,), across)
    t_back_c = remote(tall.at[tc_keep], tall.at[tc_keep], r.sem_t, (3,), core)
    v_core = remote(vg.at[pl.ds(0, 8)], vcore, r.sem_t, (4,), core)

    if folded:
        piece = tdp.shape[1] // n_dp
        steps_away = range(1, n_dp)

        def ahead(step):
            return (d + step) % n_dp

        def t_rs(step):
            return remote(
                tdp.at[0, span(ahead(step) * piece, piece)], trd.at[d], r.sem_tr, (step,), (ahead(step), s)
            )

        def t_ag(step):
            own_piece = span(d * piece, piece)
            return remote(tfin.at[own_piece], tfin.at[own_piece], r.sem_ta, (step,), (ahead(step), s))

        def t_spread():
            for step in steps_away:
                t_rs(step).start()

        def t_owned():
            for step in steps_away:
                t_rs(step).wait_recv()
            trd[d] = tdp[0, span(d * piece, piece)]
            total = trd[0].astype(F32)
            for at in range(1, n_dp):
                total = total + trd[at].astype(F32)
            tfin[span(d * piece, piece)] = total.astype(BF)
            for step in steps_away:
                t_ag(step).start()

        def t_whole():
            for step in steps_away:
                t_ag(step).wait_recv()

        t_exchange = [t_owned, t_whole]
        t_sends = [t_rs(step) for step in steps_away] + [t_ag(step) for step in steps_away]
        dp_peers = [(ahead(step), s) for step in steps_away]
    else:

        def t_dp(t):
            return remote(tdp.at[t], trd.at[t], r.sem_td, (t,), sum_peers[t])

        def t_spread():
            t_dp(0).start()

        def t_bit(t):
            t_dp(t).wait_recv()
            total = (tdp[t].astype(F32) + trd[t].astype(F32)).astype(BF)
            if t + 1 < bits:
                tdp[t + 1] = total
                t_dp(t + 1).start()
            else:
                tfin[...] = total

        t_exchange = [functools.partial(t_bit, t) for t in range(bits)]
        t_sends = [t_dp(t) for t in range(bits)]
        dp_peers = sum_peers

    barrier = pltpu.get_barrier_semaphore()
    peers = [core, across] + dp_peers
    for peer in peers:
        pl.semaphore_signal(barrier, inc=1, device_id=peer, device_id_type=MESH)

    small_names = names[3:13]
    smalls = [getattr(r, "in_" + n) for n in small_names]
    small_copies = [local(getattr(r, n), smalls[at], r.sem_small, at) for at, n in enumerate(small_names)]
    for copy in small_copies:
        copy.start()

    def start_local(j, carry):
        p_local(j).start()
        c_local(j).start()
        return carry

    lax.fori_loop(0, own, start_local, 0)
    for copy in weight_copies:
        copy.start()

    eye, wide = r.eye, r.wide
    eye[...] = jnp.where(diagonal(rows, count), 1.0, 0.0).astype(BF)
    wide[...] = jnp.where(diagonal(half, half), 1.0, 0.0).astype(BF)
    gci, gco, cib = r.gci, r.gco, r.cib
    gci[...] = jnp.zeros_like(gci)
    gco[...] = jnp.zeros_like(gco)
    cib[...] = jnp.zeros_like(cib)
    tg[...] = jnp.zeros_like(tg)
    vg[...] = jnp.zeros_like(vg)
    s2o[...] = jnp.zeros_like(s2o)
    s1o[...] = jnp.zeros_like(s1o)
    for copy in small_copies:
        copy.wait()
    vpad = r.vpad
    vpad[...] = jnp.zeros_like(vpad)
    for at in range(5):
        vpad[pl.ds(at, 1), pl.ds(0, width)] = smalls[at][...]
    vectors = vpad[...]
    r.vmine[...] = jnp.where(c == 0, vectors, pltpu.roll(vectors, width, 1))
    hidden_bias = r.hidden_row
    for at in range(hidden // LANE):
        hidden_bias[:, pl.ds(at * LANE, LANE)] = r.in_hidden_bias[pl.ds(at, 1), :]
    for at in range(toks // LANE):
        r.tok_row[:, pl.ds(at * LANE, LANE)] = r.in_tok_in_bias[pl.ds(at, 1), :]
    r.tib[...] = to_column(r.tok_row[...], toks)
    r.tob[...] = to_column(r.in_tok_out_bias[...], rows)
    tok_in_t, tok_in, tok_out, tok_out_t = r.tok_in_t, r.tok_in, r.tok_out, r.tok_out_t
    tok_in_t[...] = dot(eye[...], r.in_tok_in_raw[...]).astype(BF)
    tok_in[...] = dot_nt(wide[...], tok_in_t[...]).astype(BF)
    tok_out[...] = dot(eye[...], r.in_tok_out_raw[...]).astype(BF)
    tok_out_t[...] = dot_nt(wide[...], tok_out[...]).astype(BF)

    pl.semaphore_wait(barrier, len(peers))

    def start_images(j, carry):
        p_swap(j).start()
        c_swap(j).start()
        return carry

    v_swap.start()
    lax.fori_loop(0, own, start_images, 0)

    def turn_in(ref, j):
        return dot_nt(eye[...], ref[j])

    def turn_out(values):
        return dot_nt(wide[...], values)[:, :count].astype(BF)

    def merge_send(j):
        p_swap(j).wait_recv()
        p_local(j).wait()
        raw[j, :, near] = turn_in(pin, j).astype(BF)
        p_across(j).start()
        c_swap(j).wait_recv()
        c_local(j).wait()
        valid = jnp.where(c * own + j < r.counts[0], 1.0, 0.0)
        gb[j, first, near] = (turn_in(cin, j) * valid).astype(BF)
        c_across(j).start()

    merge_send(0)
    v_swap.wait_recv()
    vown[...] = r.vmine[...] + r.vpart[...]
    v_across.start()
    merge_send(1)
    merge_send(2)

    v_across.wait_recv()

    def vector(row):
        return jnp.concatenate([vown[pl.ds(row, 1), :], vother[pl.ds(row, 1), :]], axis=1)

    def normalise(values):
        centred = values - row_sum(values) * (1.0 / full)
        inverse = lax.rsqrt(row_sum(centred * centred) * (1.0 / full) + EPS)
        return centred * inverse, inverse

    def token_forward(j):
        values = raw[j].astype(F32)
        scaled, inverse = normalise(values)
        normed = (scaled * vector(0) + vector(1)).astype(BF)
        r.sc1[j] = scaled[:, :half].astype(BF)
        r.inv1[j] = inverse
        r.n1[j] = normed[:, :half]
        act, slope = gelu_parts(dot(tok_in[...], normed[:, :half]) + r.tib[...])
        r.tsl[j] = slope.astype(BF)
        act = act.astype(BF)
        r.ta[j] = act
        rest = gelu(dot(tok_in[...], normed[:, half:]) + r.tib[...]).astype(BF)
        mid = values + (dot(tok_out[...], jnp.concatenate([act, rest], axis=1)) + r.tob[...])
        r.mid[j] = mid[:, :half]
        scaled, inverse = normalise(mid)
        r.sc2[j] = scaled[:, :half].astype(BF)
        r.inv2[j] = inverse
        ntb[j, first] = (scaled * vector(2) + vector(3)).astype(BF)

    ghs, slopes = r.ghs, r.slopes
    step = 256

    def channel_front(j):
        nt = ntb[j]
        for at in range(hidden // step):
            cols = pl.ds(at * step, step)
            act, slope = gelu_parts(dot(nt, win[:, cols]) + hidden_bias[:, cols])
            outp[j, :, cols] = act.astype(BF)
            slopes[:, cols] = slope

    def channel_grads(j):
        g = gb[j]
        for at in range(hidden // step):
            cols = pl.ds(at * step, step)
            grad = (slopes[:, cols] * dot_nt(g, wout[cols, :])).astype(BF)
            ghs[:, cols] = grad
            cib[:, cols] += jnp.sum(grad.astype(F32), axis=0, keepdims=True)

    def channel_back(j):
        backp[j] = dot_nt(ghs[...], win[...]).astype(BF)
        back_pair(j).start()

    tiles = hidden // LANE

    def chan_out_grad(j, last):
        if last:
            for at in range(full // LANE):
                cols = pl.ds(at * LANE, LANE)
                total = gco[:, cols] + dot_tn(outp[j], gb[j, :, cols])
                gbuf[pl.ds(at * hidden, hidden)] = total.astype(BF)
        else:
            gco[...] += dot_tn(outp[j], gb[j])

    def chan_in_grad(j, last):
        if last:
            for at in range(tiles):
                cols = pl.ds(at * LANE, LANE)
                total = gci[:, cols] + dot_tn(ntb[j], ghs[:, cols])
                start = (full // LANE) * hidden + at * full
                gbuf[pl.ds(start, full)] = total.astype(BF)
        else:
            gci[...] += dot_tn(ntb[j], ghs[...])

    def pair_sums(j):
        back_pair(j).wait_recv()
        total = backp[j, first].astype(F32) + backr[j].astype(F32)
        s2o[j, pl.ds(0, 1)] = to_row(row_sum(total * vector(2)), rows)
        s2o[j, pl.ds(1, 1)] = to_row(row_sum(total * (ntb[j, first].astype(F32) - vector(3))), rows)
        backp[j, first] = total.astype(BF)
        s2_across(j).start()
        back_across(j).start()

    def gather_phase(j, carry):
        @pl.when(j + 3 < own)
        def _():
            merge_send(j + 3)

        p_across(j).wait_recv()
        token_forward(j)
        nt_share(j).start()

        @pl.when(j == 0)
        def _():
            for copy in weight_copies:
                copy.wait()

        @pl.when(j > 0)
        def _():
            g_share(j - 1).wait_recv()
            channel_grads(j - 1)
            channel_back(j - 1)
            chan_out_grad(j - 1, False)
            chan_in_grad(j - 1, False)

        c_across(j).wait_recv()
        g_share(j).start()
        nt_share(j).wait_recv()
        channel_front(j)

        @pl.when(j > 1)
        def _():
            pair_sums(j - 2)

        return carry

    lax.fori_loop(0, own, gather_phase, 0)

    g_share(own - 1).wait_recv()
    channel_grads(own - 1)
    chan_out_grad(own - 1, True)
    gradient_first(0, (full // LANE) * hidden)
    chan_in_grad(own - 1, True)
    gradient_first((full // LANE) * hidden, gbuf.shape[0])
    channel_back(own - 1)
    pair_sums(own - 2)
    pair_sums(own - 1)

    def partial_outs(j):
        outp[j] = dot(outp[j], wout[...]).astype(BF)
        out_pair(j).start()

    def pair_outs(j):
        out_pair(j).wait_recv()
        total = outp[j, first].astype(F32) + outr[j].astype(F32)
        outp[j, first] = total.astype(BF)
        out_across(j).start()

    def norm_back(weighted, scaled, inverse, sums):
        mean = to_column(sums[0:1] * (1.0 / full), rows)
        slant = to_column(sums[1:2] * (1.0 / full), rows)
        return inverse * (weighted - mean - scaled * slant)

    def token_backward(j):
        s2_across(j).wait_recv()
        back_across(j).wait_recv()
        grad_normed = backp[j, first, near].astype(F32) + backx[j].astype(F32)
        scaled = r.sc2[j].astype(F32)
        grad_out = gb[j, first, near].astype(F32)
        weighted = grad_normed * vown[pl.ds(2, 1), :]
        grad_mid = grad_out + norm_back(weighted, scaled, r.inv2[j], s2o[j] + s2x[j])
        r.gm[j] = grad_mid
        vg[pl.ds(2, 1), :] += jnp.sum(grad_normed * scaled, axis=0, keepdims=True)
        vg[pl.ds(3, 1), :] += jnp.sum(grad_normed, axis=0, keepdims=True)
        vg[pl.ds(4, 1), :] += jnp.sum(grad_out, axis=0, keepdims=True)
        low = grad_mid.astype(BF)
        ones = jnp.ones((8, half), BF)
        tg[pl.ds(rows, rows), :] += dot_nt(low, r.ta[j])
        tg[pl.ds(2 * rows + 8, 8), pl.ds(0, rows)] += dot_nt(ones, low)
        grad_pre = (r.tsl[j].astype(F32) * dot(tok_out_t[...], low)).astype(BF)
        tg[pl.ds(0, rows), :] += dot_nt(r.n1[j], grad_pre)
        tg[pl.ds(2 * rows, 8), :] += dot_nt(ones, grad_pre)
        grad_one = dot(tok_in_t[...], grad_pre)
        scaled = r.sc1[j].astype(F32)
        vg[pl.ds(0, 1), :] += jnp.sum(grad_one * scaled, axis=0, keepdims=True)
        vg[pl.ds(1, 1), :] += jnp.sum(grad_one, axis=0, keepdims=True)
        weighted = grad_one * vown[pl.ds(0, 1), :]
        r.w1[j] = weighted
        s1o[j, pl.ds(0, 1)] = to_row(row_sum(weighted), rows)
        s1o[j, pl.ds(1, 1)] = to_row(row_sum(weighted * scaled), rows)
        s1_across(j).start()

    def input_grad(j):
        s1_across(j).wait_recv()
        scaled = r.sc1[j].astype(F32)
        grad = r.gm[j] + norm_back(r.w1[j], scaled, r.inv1[j], s1o[j] + s1x[j])
        gis[j] = turn_out(grad.astype(BF))
        gin_give(j).start()
        gin_keep(j).start()

    def mixed_part(j):
        out_across(j).wait_recv()
        total = outp[j, first, near].astype(F32) + outx[j].astype(F32)
        valid = jnp.where(c * own + j < r.counts[0], 1.0, 0.0)
        mos[j] = turn_out((valid * (r.mid[j] + (total + vown[pl.ds(4, 1), :]))).astype(BF))
        mixed_give(j).start()
        mixed_keep(j).start()

    def token_start():
        tb[...] = tg[...].astype(BF)
        for at in range(hidden // half):
            vg[pl.ds(8 + at, 1), :] = cib[:, pl.ds(at * half, half)]
        t_core.start()
        v_core.start()

    def token_core():
        t_core.wait_recv()
        v_core.wait_recv()
        tcur[...] = (tb[tc_keep].astype(F32) + tcore[...].astype(F32)).astype(BF)
        t_across.start()
        vcore[...] = vg[pl.ds(0, 8)] + vcore[...]

    def token_across():
        t_across.wait_recv()
        tdp[0, pl.ds(0, t_quarter)] = (tcur[tx_keep].astype(F32) + txr[...].astype(F32)).astype(BF)
        tdp[0, pl.ds(t_quarter, 16)] = jnp.concatenate([vcore[...], vg[pl.ds(8, 8)]], axis=0).astype(BF)
        t_spread()

    def token_back():
        tall[t_mine] = tfin[pl.ds(0, t_quarter)]
        t_back_x.start()
        vec = tfin[pl.ds(t_quarter, 16)].astype(F32)
        vec_out[pl.ds(0, 8), :] = jnp.where(c == 0, vec, pltpu.roll(vec, width, 1))[:8]
        vec_out[pl.ds(8, 8), :] = vec[8:]

    def token_core_back():
        t_back_x.wait_recv()
        t_back_c.start()

    def token_end():
        t_back_c.wait_recv()
        vec_out[pl.ds(16, 16), :] = tall[pl.ds(2 * rows, 16)].astype(F32)

    token_steps = [token_start, token_core, None, token_across, None]
    for exchange in t_exchange[:-1]:
        token_steps += [exchange, None]

    def token_last():
        t_exchange[-1]()
        token_back()

    token_steps += [token_last, None, token_core_back, token_end]

    token_first = own - 1
    outs_first = 2
    mixed_first = own

    inputs_first = 4

    def scatter_phase(i, carry):
        gradient_step(i)

        def each(start, work):
            @pl.when((i >= start) & (i < start + own))
            def _():
                work(i - start)

        each(0, token_backward)
        for e, token_step in enumerate(token_steps):
            if token_step is not None:
                pl.when(i == token_first + e)(token_step)
        each(inputs_first, input_grad)
        each(outs_first, pair_outs)
        each(outs_first - 1, partial_outs)
        each(mixed_first, mixed_part)
        return carry

    lax.fori_loop(0, max(gradient_ticks, token_first + len(token_steps), mixed_first + own), scatter_phase, 0)

    def gradient_end(k, carry):
        gradient_last(k)
        return carry

    lax.fori_loop(0, gradient_items, gradient_end, 0)

    outs = []
    for at in range(full // LANE):
        to = mine if at < half // LANE else theirs
        lanes = pl.ds(pl.multiple_of(to + (at % (half // LANE)) * LANE, LANE), LANE)
        outs.append((fbuf.at[pl.ds(at * hidden, hidden)], r.g_chan_out.at[:, lanes]))
    for at in range(tiles):
        lanes = pl.ds(at * LANE, LANE)
        for part, to in enumerate((mine, theirs)):
            start = (full // LANE) * hidden + at * full + part * half
            outs.append((fbuf.at[pl.ds(start, half)], r.g_chan_in.at[pl.ds(to, half), lanes]))
    outs = [local(src, dst, r.sem_out, at) for at, (src, dst) in enumerate(outs)]
    for copy in outs:
        copy.start()

    def drain(j, carry):
        for make in (p_swap, c_swap, p_across, c_across, nt_share, g_share, out_pair, back_pair):
            make(j).wait_send()
        for make in (out_across, back_across, s2_across, s1_across):
            make(j).wait_send()
        for make in (mixed_give, gin_give, mixed_keep, gin_keep):
            make(j).wait()
        return carry

    lax.fori_loop(0, own, drain, 0)
    for copy in [v_swap, v_across, t_core, t_across, t_back_x, t_back_c, v_core] + t_sends:
        copy.wait_send()
    for copy in outs:
        copy.wait()


def run_layer(n_dp, **arrays):
    batch, width, count = arrays["patches"].shape
    own = batch // 2
    full, hidden = arrays["win_hbm"].shape
    half = full // 2
    toks = arrays["tok_in_raw"].shape[1]
    rows = -(-count // 16) * 16
    bits = n_dp.bit_length() - 1
    grad_rows = 2 * full * hidden // LANE
    folded = n_dp == 8
    choices = (8, 4, 2) if folded else (9, 3, 1)
    parts = 18 if folded else n_dp
    chunks = next(k for k in choices if grad_rows % (k * parts * (64 if folded else 16)) == 0)
    chunk = grad_rows // chunks
    cfg = (n_dp, own, count, rows, half, full, hidden, toks, chunks, chunk)
    vmem = pltpu.VMEM
    dma = pltpu.SemaphoreType.DMA
    two, whole = chunk * 13 // 36, chunk * 5 // 18
    t_rows = -(-(2 * rows + 16) // 64) * 64
    scratch = dict(
        win=vmem((full, hidden), BF),
        wout=vmem((hidden, full), BF),
        pin=vmem((own, half, count), BF),
        cin=vmem((own, half, count), BF),
        vpad=vmem((8, half), F32),
        hidden_row=vmem((1, hidden), F32),
        tok_row=vmem((1, toks), F32),
        vmine=vmem((8, half), F32),
        vpart=vmem((8, half), F32),
        vown=vmem((8, half), F32),
        vother=vmem((8, half), F32),
        eye=vmem((rows, count), BF),
        wide=vmem((half, half), BF),
        tok_in_t=vmem((rows, toks), BF),
        tok_in=vmem((toks, rows), BF),
        tok_out=vmem((rows, toks), BF),
        tok_out_t=vmem((toks, rows), BF),
        tib=vmem((toks, 1), F32),
        tob=vmem((rows, 1), F32),
        raw=vmem((own, rows, full), BF),
        ntb=vmem((own, 2 * rows, full), BF),
        gb=vmem((own, 2 * rows, full), BF),
        ghs=vmem((2 * rows, hidden), BF),
        slopes=vmem((2 * rows, hidden), F32),
        gci=vmem((full, hidden), F32),
        gco=vmem((hidden, full), F32),
        cib=vmem((1, hidden), F32),
        outp=vmem((own, 2 * rows, full), BF),
        outr=vmem((own, rows, full), BF),
        backp=vmem((own, 2 * rows, full), BF),
        backr=vmem((own, rows, full), BF),
        outx=vmem((own, rows, half), BF),
        backx=vmem((own, rows, half), BF),
        s2o=vmem((own, 8, rows), F32),
        s2x=vmem((own, 8, rows), F32),
        s1o=vmem((own, 8, rows), F32),
        s1x=vmem((own, 8, rows), F32),
        n1=vmem((own, rows, half), BF),
        ta=vmem((own, toks, half), BF),
        tsl=vmem((own, toks, half), BF),
        mid=vmem((own, rows, half), F32),
        sc1=vmem((own, rows, half), BF),
        sc2=vmem((own, rows, half), BF),
        inv1=vmem((own, rows, 1), F32),
        inv2=vmem((own, rows, 1), F32),
        gm=vmem((own, rows, half), F32),
        w1=vmem((own, rows, half), F32),
        gbuf=vmem((grad_rows, LANE), BF),
        fbuf=vmem((grad_rows, LANE), BF),
        tg=vmem((t_rows, toks), F32),
        tb=vmem((t_rows, toks), BF),
        tcore=vmem((t_rows // 2, toks), BF),
        tcur=vmem((t_rows // 2, toks), BF),
        txr=vmem((t_rows // 4, toks), BF),
        tdp=vmem((1 if folded else bits, t_rows // 4 + 16, toks), BF),
        trd=vmem((n_dp, (t_rows // 4 + 16) // n_dp, toks) if folded else (bits, t_rows // 4 + 16, toks), BF),
        tfin=vmem((t_rows // 4 + 16, toks), BF),
        vg=vmem((16, half), F32),
        vcore=vmem((8, half), F32),
        sem_w=dma((4,)),
        sem_small=dma((10,)),
        sem_v=dma((2, 2)),
        sem_out=dma((2 * (hidden // LANE) + full // LANE,)),
        sem_t=dma((2, 5)),
        sem_td=dma((2, bits)),
        sem_tr=dma((2, n_dp)),
        sem_ta=dma((2, n_dp)),
    )
    for name in list(arrays)[3:13]:
        scratch["in_" + name] = vmem(arrays[name].shape, arrays[name].dtype)
    for name in ("pl", "cl", "mk", "gk"):
        scratch["sem_" + name] = dma((own,))
    for name in ("ps", "cs", "px", "cx", "nt", "g", "op", "bp", "ox", "bx", "s2", "s1", "mg", "gg"):
        scratch["sem_" + name] = dma((2, own))
    if folded:
        scratch["e0"] = vmem((chunks * two, LANE), BF)
        scratch["e1"] = vmem((chunks * two, LANE), BF)
        scratch["e2"] = vmem((chunks * two // 2, LANE), BF)
        scratch["o0"] = vmem((chunks * whole, LANE), BF)
        scratch["o1"] = vmem((chunks * whole // 2, LANE), BF)
        scratch["o2"] = vmem((chunks * whole // 4, LANE), BF)
        for name in [e + str(k) for e in "eo" for k in range(7)]:
            scratch["sem_" + name] = dma((2, chunks))
    else:
        scratch["rbuf"] = vmem((chunks * (chunk - (chunk >> bits)), LANE), BF)
        scratch["sem_rs"] = dma((2, bits, chunks))
        scratch["sem_ag"] = dma((2, bits, chunks))
    hbm = pl.BlockSpec(memory_space=pl.ANY)
    inside = pl.BlockSpec(memory_space=pltpu.VMEM)
    places = dict(counts=pl.BlockSpec(memory_space=pltpu.SMEM), tall=inside, vec_out=inside)
    outs = dict(
        mixed=((batch, width, count), BF),
        gin=((batch, width, count), BF),
        tall=((t_rows, toks), BF),
        vec_out=((32, half), F32),
        g_chan_in=((full, hidden), BF),
        g_chan_out=((hidden, full), BF),
    )
    names = list(arrays) + list(outs) + list(scratch)
    results = pl.pallas_call(
        functools.partial(layer_kernel, cfg, names),
        out_shape=tuple(jax.ShapeDtypeStruct(*outs[name]) for name in outs),
        in_specs=[places.get(name, hbm) for name in arrays],
        out_specs=tuple(places.get(name, hbm) for name in outs),
        scratch_shapes=list(scratch.values()),
        compiler_params=pltpu.CompilerParams(
            collective_id=0, has_side_effects=True, vmem_limit_bytes=63 * 2**20
        ),
        name="mixer_layer",
    )(*arrays.values())
    return SimpleNamespace(**dict(zip(outs, results)))


def finish_kernel(names, *refs):
    r = SimpleNamespace(**dict(zip(names, refs)))
    sems = r.sems
    count, toks = r.tok_in.shape
    rows = -(-count // 16) * 16
    parts = r.pieces.shape[1]
    step = r.pieces.shape[2]
    loads, stores = [], []
    whole_in, whole_out = [], []
    for at, (raw, done) in enumerate(((r.mixed_raw, r.mixed), (r.gin_raw, r.gin))):
        for part in range(2):
            here = pl.ds(part * (r.images.shape[1] // 2), r.images.shape[1] // 2)
            sem = 2 + 4 * parts + 4 * at + 2 * part
            whole_in.append(pltpu.make_async_copy(raw.at[here], r.images.at[at, here], sems.at[sem]))
            whole_out.append(pltpu.make_async_copy(r.images.at[at, here], done.at[here], sems.at[sem + 1]))
    for at, (raw, done) in enumerate(((r.chan_in_raw, r.chan_in), (r.chan_out_raw, r.chan_out))):
        for part in range(parts):
            here = pl.ds(part * step, step)
            sem = 2 + at * parts + part
            loads.append(pltpu.make_async_copy(raw.at[here], r.pieces.at[at, part], sems.at[sem]))
            stores.append(
                pltpu.make_async_copy(r.wide.at[at, part], done.at[here], sems.at[sem + 2 * parts])
            )
    for copy in loads + whole_in:
        copy.start()
    for at in range(len(loads)):
        loads[at].wait()
        r.wide[at // parts, at % parts] = r.pieces[at // parts, at % parts].astype(F32)
        stores[at].start()
    for at in range(len(whole_in)):
        whole_in[at].wait()
        whole_out[at].start()
    vec, tall = r.vec_raw, r.tok_raw
    width = r.ln1_gain.shape[1]
    for at, done in enumerate((r.ln1_gain, r.ln1_bias, r.ln2_gain, r.ln2_bias, r.chan_out_bias)):
        done[...] = vec[pl.ds(at, 1), :][:, :width]
    half = vec.shape[1]
    for at in range(r.chan_in_bias.shape[0]):
        row, lane = divmod(at * LANE, half)
        r.chan_in_bias[pl.ds(at, 1), :] = vec[pl.ds(8 + row, 1), pl.ds(lane, LANE)]
    for at in range(toks // LANE):
        r.tok_in_bias[pl.ds(at, 1), :] = vec[pl.ds(16, 1), pl.ds(at * LANE, LANE)]
    r.tok_out_bias[...] = vec[pl.ds(24, 1), :][:, :count]
    r.tok_in[...] = tall[pl.ds(0, rows)][:count].astype(F32)
    r.tok_out[...] = tall[pl.ds(rows, rows)][:count].astype(F32)
    for copy in stores + whole_out:
        copy.wait()


def finish(out, count, width):
    full, hidden = out.g_chan_in.shape
    toks = out.tall.shape[1]
    hbm = pl.BlockSpec(memory_space=pl.ANY)
    inside = pl.BlockSpec(memory_space=pltpu.VMEM)
    arrays = dict(
        mixed_raw=out.mixed,
        gin_raw=out.gin,
        chan_in_raw=out.g_chan_in,
        chan_out_raw=out.g_chan_out,
        tok_raw=out.tall,
        vec_raw=out.vec_out,
    )
    outs = dict(
        mixed=(out.mixed.shape, BF),
        gin=(out.gin.shape, BF),
        chan_in=((full, hidden), F32),
        chan_out=((hidden, full), F32),
        ln1_gain=((1, width), F32),
        ln1_bias=((1, width), F32),
        ln2_gain=((1, width), F32),
        ln2_bias=((1, width), F32),
        chan_out_bias=((1, width), F32),
        chan_in_bias=((hidden // LANE, LANE), F32),
        tok_in_bias=((toks // LANE, LANE), F32),
        tok_out_bias=((1, count), F32),
        tok_in=((count, toks), F32),
        tok_out=((count, toks), F32),
    )
    parts = 4
    scratch = dict(
        pieces=pltpu.VMEM((2, parts, full // parts, hidden), BF),
        wide=pltpu.VMEM((2, parts, full // parts, hidden), F32),
        images=pltpu.VMEM((2,) + out.mixed.shape, BF),
        sems=pltpu.SemaphoreType.DMA((10 + 4 * parts,)),
    )
    names = list(arrays) + list(outs) + list(scratch)
    results = pl.pallas_call(
        functools.partial(finish_kernel, names),
        out_shape=tuple(jax.ShapeDtypeStruct(*outs[name]) for name in outs),
        in_specs=[hbm] * 4 + [inside] * 2,
        out_specs=(hbm,) * 4 + (inside,) * 10,
        scratch_shapes=list(scratch.values()),
        compiler_params=pltpu.CompilerParams(vmem_limit_bytes=63 * 2**20),
        name="finish",
    )(*arrays.values())
    return SimpleNamespace(**dict(zip(outs, results)))


def per_device(
    n_dp,
    image_counts,
    patches,
    ln1_gain,
    ln1_bias,
    tok_in_weight,
    tok_in_bias,
    tok_out_weight,
    tok_out_bias,
    ln2_gain,
    ln2_bias,
    chan_in_weight,
    chan_in_bias,
    chan_out_weight,
    chan_out_bias,
    cotangent,
):
    out = run_layer(
        n_dp,
        counts=image_counts,
        patches=jnp.transpose(patches, (1, 2, 0)),
        cot=jnp.transpose(cotangent, (1, 2, 0)),
        ln1_gain=ln1_gain[None, :],
        ln1_bias=ln1_bias[None, :],
        ln2_gain=ln2_gain[None, :],
        ln2_bias=ln2_bias[None, :],
        chan_out_bias=chan_out_bias[None, :],
        hidden_bias=chan_in_bias.reshape(-1, LANE),
        tok_in_bias=tok_in_bias.reshape(-1, LANE),
        tok_out_bias=tok_out_bias[None, :],
        tok_in_raw=tok_in_weight.T,
        tok_out_raw=tok_out_weight,
        win_hbm=chan_in_weight,
        wout_hbm=chan_out_weight,
    )
    out = finish(out, patches.shape[0], patches.shape[2])
    return (
        jnp.transpose(out.mixed, (2, 0, 1)),
        jnp.transpose(out.gin, (2, 0, 1)),
        out.ln1_gain[0],
        out.ln1_bias[0],
        out.tok_in.T,
        out.tok_in_bias.reshape(-1),
        out.tok_out,
        out.tok_out_bias[0],
        out.ln2_gain[0],
        out.ln2_bias[0],
        out.chan_in,
        out.chan_in_bias.reshape(-1),
        out.chan_out,
        out.chan_out_bias[0],
    )


def solution(mesh):
    in_specs = (
        P("dp"),
        P(None, "dp", "seq"),
        P("seq"),
        P("seq"),
        P(),
        P(),
        P(),
        P(),
        P("seq"),
        P("seq"),
        P(None, "seq"),
        P("seq"),
        P("seq", None),
        P("seq"),
        P(None, "dp", "seq"),
    )
    out_specs = (
        P(None, "dp", "seq"),
        P(None, "dp", "seq"),
        P("seq"),
        P("seq"),
        P(),
        P(),
        P(),
        P(),
        P("seq"),
        P("seq"),
        P(None, "seq"),
        P("seq"),
        P("seq", None),
        P("seq"),
    )
    return jax.shard_map(
        functools.partial(per_device, mesh.shape["dp"]),
        mesh=mesh,
        in_specs=in_specs,
        out_specs=out_specs,
        check_vma=False,
    )
```

```python
import functools
from types import SimpleNamespace

import jax
import jax.numpy as jnp
from jax import lax
from jax.experimental import pallas as pl
from jax.experimental.pallas import tpu as pltpu
from jax.sharding import PartitionSpec as P

MESH = pl.DeviceIdType.MESH
BF = jnp.bfloat16
F32 = jnp.float32
EPS = 1e-06
GELU_A = 0.7978845608028654
GELU_B = GELU_A * 0.044715
LANE = 128


def gelu_parts(x):
    square = x * x
    tanh = jnp.tanh(x * (GELU_A + GELU_B * square))
    half = 0.5 + 0.5 * tanh
    slope = half + (0.5 * x) * (1.0 - tanh * tanh) * (GELU_A + (3.0 * GELU_B) * square)
    return x * half, slope


def gelu(x):
    return x * (0.5 + 0.5 * jnp.tanh(x * (GELU_A + GELU_B * (x * x))))


def dot(a, b):
    return lax.dot_general(a, b, (((1,), (0,)), ((), ())), preferred_element_type=F32)


def dot_nt(a, b):
    return lax.dot_general(a, b, (((1,), (1,)), ((), ())), preferred_element_type=F32)


def dot_tn(a, b):
    return lax.dot_general(a, b, (((0,), (0,)), ((), ())), preferred_element_type=F32)


def diagonal(rows, columns):
    return lax.broadcasted_iota(jnp.int32, (rows, columns), 0) == lax.broadcasted_iota(
        jnp.int32, (rows, columns), 1
    )


def to_row(values, columns):
    return jnp.sum(jnp.where(diagonal(values.shape[0], columns), values, 0.0), axis=0, keepdims=True)


def to_column(values, rows):
    return jnp.sum(jnp.where(diagonal(rows, values.shape[1]), values, 0.0), axis=1, keepdims=True)


def row_sum(values):
    return jnp.sum(values, axis=-1, keepdims=True)


def layer_kernel(cfg, names, *refs):
    n_dp, own, count, rows, half, full, hidden, toks, chunks, chunk = cfg
    r = SimpleNamespace(**dict(zip(names, refs)))
    width = half // 2
    d = lax.axis_index("dp")
    s = lax.axis_index("seq")
    c = s % 2
    x = s // 2
    core = (d, s + 1 - 2 * c)
    across = (d, s + 2 - 4 * x)
    folded = n_dp == 8
    bits = n_dp.bit_length() - 1

    def dp_bit(t):
        return (d // (1 << t)) % 2

    def dp_peer(t):
        m = 1 << t
        return (d + m - 2 * m * dp_bit(t), s)

    a = d // 2
    b = d % 2
    end = a % 3 == 0
    middle = a % 3 != 0
    m = a // 2
    side = dp_peer(0)
    fold = dp_peer(1)
    mirror = ((n_dp // 2 - 1 - a) * 2 + b, s)
    sum_peers = [side, fold, mirror] if folded else [dp_peer(t) for t in range(bits)]

    def remote(src, dst, sems, at, target):
        return pltpu.make_async_remote_copy(
            src_ref=src,
            dst_ref=dst,
            send_sem=sems.at[(0,) + at],
            recv_sem=sems.at[(1,) + at],
            device_id=target,
            device_id_type=MESH,
        )

    def local(src, dst, sems, at):
        return pltpu.make_async_copy(src, dst, sems.at[at])

    win, wout, pin, cin, raw = r.win, r.wout, r.pin, r.cin, r.raw
    ntb, gb, outp, outr, backp, backr = r.ntb, r.gb, r.outp, r.outr, r.backp, r.backr
    outx, backx, s2o, s2x, s1o, s1x = r.outx, r.backx, r.s2o, r.s2x, r.s1o, r.s1x
    vown, vother, tg, vg, vec_out = r.vown, r.vother, r.tg, r.vg, r.vec_out
    gbuf, fbuf = r.gbuf, r.fbuf
    mos, gis = pin, cin

    mine = pl.multiple_of(x * half, LANE)
    theirs = pl.multiple_of((1 - x) * half, LANE)
    weight_copies = [
        local(r.win_hbm.at[pl.ds(mine, half)], win.at[pl.ds(0, half)], r.sem_w, 0),
        local(r.win_hbm.at[pl.ds(theirs, half)], win.at[pl.ds(half, half)], r.sem_w, 1),
        local(r.wout_hbm.at[:, pl.ds(mine, half)], wout.at[:, pl.ds(0, half)], r.sem_w, 2),
        local(r.wout_hbm.at[:, pl.ds(theirs, half)], wout.at[:, pl.ds(half, half)], r.sem_w, 3),
    ]

    place = pl.ds(pl.multiple_of(c * width, 16), width)

    def p_local(j):
        return local(r.patches.at[c * own + j], pin.at[j, place], r.sem_pl, j)

    def c_local(j):
        return local(r.cot.at[c * own + j], cin.at[j, place], r.sem_cl, j)

    def p_swap(j):
        return remote(r.patches.at[(1 - c) * own + j], pin.at[j, place], r.sem_ps, (j,), core)

    def c_swap(j):
        return remote(r.cot.at[(1 - c) * own + j], cin.at[j, place], r.sem_cs, (j,), core)

    v_swap = remote(r.vmine, r.vpart, r.sem_v, (0,), core)
    v_across = remote(vown, vother, r.sem_v, (1,), across)

    first = pl.ds(0, rows)
    second = pl.ds(rows, rows)
    near = pl.ds(0, half)
    far = pl.ds(half, half)

    def p_across(j):
        return remote(raw.at[j, :, near], raw.at[j, :, far], r.sem_px, (j,), across)

    def c_across(j):
        return remote(gb.at[j, first, near], gb.at[j, first, far], r.sem_cx, (j,), across)

    def nt_share(j):
        return remote(ntb.at[j, first], ntb.at[j, second], r.sem_nt, (j,), core)

    def g_share(j):
        return remote(gb.at[j, first], gb.at[j, second], r.sem_g, (j,), core)

    def out_pair(j):
        return remote(outp.at[j, second], outr.at[j], r.sem_op, (j,), core)

    def back_pair(j):
        return remote(backp.at[j, second], backr.at[j], r.sem_bp, (j,), core)

    def out_across(j):
        return remote(outp.at[j, first, far], outx.at[j], r.sem_ox, (j,), across)

    def back_across(j):
        return remote(backp.at[j, first, far], backx.at[j], r.sem_bx, (j,), across)

    def s2_across(j):
        return remote(s2o.at[j], s2x.at[j], r.sem_s2, (j,), across)

    def s1_across(j):
        return remote(s1o.at[j], s1x.at[j], r.sem_s1, (j,), across)

    other = pl.ds(pl.multiple_of((1 - c) * width, 16), width)

    def mixed_give(j):
        return remote(mos.at[j, other], r.mixed.at[c * own + j], r.sem_mg, (j,), core)

    def gin_give(j):
        return remote(gis.at[j, other], r.gin.at[c * own + j], r.sem_gg, (j,), core)

    def mixed_keep(j):
        return local(mos.at[j, place], r.mixed.at[c * own + j], r.sem_mk, j)

    def gin_keep(j):
        return local(gis.at[j, place], r.gin.at[c * own + j], r.sem_gk, j)

    def span(start, size):
        return pl.ds(pl.multiple_of(start, 16), size)

    def add_into(target, at, source, source_at):
        target[at] = (gbuf[at].astype(F32) + source[source_at].astype(F32)).astype(BF)


    if folded:
        pairs = chunks
        two, four = chunk * 14 // 36, chunk * 14 // 72

        def even(k):
            return k * chunk

        def e_side(k):
            return remote(
                gbuf.at[span(even(k) + (1 - b) * two, two)], r.e0.at[span(k * two, two)], r.sem_e0, (k,), side
            )

        def e_half(k):
            return span(even(k) + b * two, two)

        def e_fold(k):
            return remote(gbuf.at[e_half(k)], r.e1.at[span(k * two, two)], r.sem_e1, (k,), fold)

        def e_mirror(k):
            return remote(
                gbuf.at[span(even(k) + b * two + (1 - m) * four, four)],
                r.e2.at[span(k * four, four)],
                r.sem_e2,
                (k,),
                mirror,
            )

        def e_quarter(k):
            return span(even(k) + b * two + m * four, four)

        def e_mirror_back(k):
            return remote(fbuf.at[e_quarter(k)], fbuf.at[e_quarter(k)], r.sem_e3, (k,), mirror)

        def e_fold_back(k):
            return remote(fbuf.at[e_half(k)], fbuf.at[e_half(k)], r.sem_e4, (k,), fold)

        def e_side_back(k):
            return remote(fbuf.at[e_half(k)], fbuf.at[e_half(k)], r.sem_e5, (k,), side)

        whole, three, six = chunk * 4 // 18, chunk * 4 // 36, chunk * 4 // 72

        def odd(k):
            return k * chunk + 2 * two

        def o_fold(k):
            return remote(gbuf.at[span(odd(k), whole)], r.o0.at[span(k * whole, whole)], r.sem_o0, (k,), fold)

        def o_mirror(k):
            return remote(
                gbuf.at[span(odd(k) + (1 - m) * three, three)],
                r.o1.at[span(k * three, three)],
                r.sem_o1,
                (k,),
                mirror,
            )

        def o_half(k):
            return span(odd(k) + m * three, three)

        def o_rest(k):
            return span(odd(k) + (1 - m) * three, three)

        def o_side(k):
            return remote(
                gbuf.at[span(odd(k) + m * three + (1 - b) * six, six)],
                r.o2.at[span(k * six, six)],
                r.sem_o2,
                (k,),
                side,
            )

        def o_quarter(k):
            return span(odd(k) + m * three + b * six, six)

        def o_side_back(k):
            return remote(fbuf.at[o_quarter(k)], fbuf.at[o_quarter(k)], r.sem_o3, (k,), side)

        def o_mirror_back(k):
            return remote(fbuf.at[o_half(k)], fbuf.at[o_half(k)], r.sem_o4, (k,), mirror)

        def o_fold_back(k):
            return remote(fbuf.at[o_half(k)], fbuf.at[o_half(k)], r.sem_o5, (k,), fold)

        def o_fold_rest(k):
            return remote(fbuf.at[o_rest(k)], fbuf.at[o_rest(k)], r.sem_o6, (k,), fold)

        def e_step(e, k):
            if e == 0:
                e_side(k).wait_recv()
                add_into(gbuf, e_half(k), r.e0, span(k * two, two))

                @pl.when(end)
                def _():
                    e_fold(k).start()

            elif e == 1:

                @pl.when(middle)
                def _():
                    e_fold(k).wait_recv()
                    add_into(gbuf, e_half(k), r.e1, span(k * two, two))
                    e_mirror(k).start()

            elif e == 2:

                @pl.when(middle)
                def _():
                    e_mirror(k).wait_recv()
                    add_into(fbuf, e_quarter(k), r.e2, span(k * four, four))
                    e_mirror_back(k).start()

            elif e == 3:

                @pl.when(middle)
                def _():
                    e_mirror_back(k).wait_recv()
                    e_fold_back(k).start()
                    e_side_back(k).start()

            else:

                @pl.when(end)
                def _():
                    e_fold_back(k).wait_recv()
                    e_side_back(k).start()

        def o_step(e, k):
            @pl.when(middle)
            def _():
                if e == 0:
                    o_fold(k).wait_recv()
                    add_into(gbuf, span(odd(k), whole), r.o0, span(k * whole, whole))
                    o_mirror(k).start()
                elif e == 1:
                    o_mirror(k).wait_recv()
                    add_into(gbuf, o_half(k), r.o1, span(k * three, three))
                    o_side(k).start()
                elif e == 2:
                    o_side(k).wait_recv()
                    add_into(fbuf, o_quarter(k), r.o2, span(k * six, six))
                    o_side_back(k).start()
                elif e == 3:
                    o_side_back(k).wait_recv()
                    o_mirror_back(k).start()
                    o_fold_back(k).start()
                else:
                    o_mirror_back(k).wait_recv()
                    o_fold_rest(k).start()

        e_at = (1, 2, 3, 4, 6)
        o_at = (1, 3, 5, 6, 7)

        def o_first(k):
            @pl.when(end)
            def _():
                o_fold(k).start()

        def gradient_first(before, ready):
            for k in range(pairs):
                if before < (k + 1) * chunk <= ready:
                    e_side(k).start()

        def gradient_step(i):
            @pl.when(i < pairs)
            def _():
                o_first(i)

            for stage, places in ((o_step, o_at), (e_step, e_at)):
                for e, at in enumerate(places):

                    @pl.when((i >= at) & (i < at + pairs))
                    def _(stage=stage, e=e, at=at):
                        stage(e, i - at)

        def gradient_last(k):
            e_side_back(k).wait_recv()

            @pl.when(end)
            def _():
                o_fold_back(k).wait_recv()
                o_fold_rest(k).wait_recv()

        def gradient_sent(k):
            e_side(k).wait_send()
            e_side_back(k).wait_send()

            @pl.when(end)
            def _():
                e_fold(k).wait_send()
                o_fold(k).wait_send()

            @pl.when(middle)
            def _():
                for make in (e_mirror, e_mirror_back, e_fold_back, o_mirror, o_side, o_side_back):
                    make(k).wait_send()
                for make in (o_mirror_back, o_fold_back, o_fold_rest):
                    make(k).wait_send()

        gradient_ticks = pairs + max(e_at[-1], o_at[-1])
        gradient_items = pairs
    else:
        def segment(k, t):
            start = k * chunk
            for u in range(t):
                start = start + dp_bit(u) * (chunk >> (u + 1))
            return start

        bases = [chunks * (chunk - (chunk >> t)) for t in range(bits)]

        def rs_at(k, t):
            size = chunk >> (t + 1)
            return span(bases[t] + k * size, size)

        def rs_send(k, t):
            size = chunk >> (t + 1)
            return remote(
                gbuf.at[span(segment(k, t) + (1 - dp_bit(t)) * size, size)],
                r.rbuf.at[rs_at(k, t)],
                r.sem_rs,
                (t, k),
                dp_peer(t),
            )

        def ag_send(k, t):
            at = span(segment(k, t + 1), chunk >> (t + 1))
            return remote(fbuf.at[at], fbuf.at[at], r.sem_ag, (t, k), dp_peer(t))

        def gradient_first(before, ready):
            for k in range(chunks):
                if before < (k + 1) * chunk <= ready:
                    rs_send(k, 0).start()

        def gradient_step(i):
            for e in reversed(range(2 * bits - 1)):
                k = i - e

                @pl.when((k >= 0) & (k < chunks))
                def _(e=e, k=k):
                    if e < bits:
                        rs_send(k, e).wait_recv()
                        at = span(segment(k, e + 1), chunk >> (e + 1))
                        add_into(gbuf if e + 1 < bits else fbuf, at, r.rbuf, rs_at(k, e))
                        if e + 1 < bits:
                            rs_send(k, e + 1).start()
                        else:
                            ag_send(k, e).start()
                    else:
                        t = 2 * bits - 1 - e
                        ag_send(k, t).wait_recv()
                        ag_send(k, t - 1).start()

        def gradient_last(k):
            ag_send(k, 0).wait_recv()

        def gradient_sent(k):
            for t in range(bits):
                rs_send(k, t).wait_send()
                ag_send(k, t).wait_send()

        gradient_ticks = chunks + 2 * bits - 2
        gradient_items = chunks

    t_half = tg.shape[0] // 2
    t_quarter = t_half // 2
    tc_keep = span(c * t_half, t_half)
    tc_give = span((1 - c) * t_half, t_half)
    tx_keep = span(x * t_quarter, t_quarter)
    tx_give = span((1 - x) * t_quarter, t_quarter)
    t_mine = span(c * t_half + x * t_quarter, t_quarter)
    tb, tcore, tcur, txr, tdp, trd, tall = r.tb, r.tcore, r.tcur, r.txr, r.tdp, r.trd, r.tall
    vcore, tfin = r.vcore, r.tfin
    t_core = remote(tb.at[tc_give], tcore, r.sem_t, (0,), core)
    t_across = remote(tcur.at[tx_give], txr, r.sem_t, (1,), across)
    t_back_x = remote(tall.at[t_mine], tall.at[t_mine], r.sem_t, (2,), across)
    t_back_c = remote(tall.at[tc_keep], tall.at[tc_keep], r.sem_t, (3,), core)
    v_core = remote(vg.at[pl.ds(0, 8)], vcore, r.sem_t, (4,), core)

    if folded:
        piece = tdp.shape[1] // n_dp
        steps_away = range(1, n_dp)

        def ahead(step):
            return (d + step) % n_dp

        def t_rs(step):
            return remote(
                tdp.at[0, span(ahead(step) * piece, piece)], trd.at[d], r.sem_tr, (step,), (ahead(step), s)
            )

        def t_ag(step):
            own_piece = span(d * piece, piece)
            return remote(tfin.at[own_piece], tfin.at[own_piece], r.sem_ta, (step,), (ahead(step), s))

        def t_spread():
            for step in steps_away:
                t_rs(step).start()

        def t_owned():
            for step in steps_away:
                t_rs(step).wait_recv()
            trd[d] = tdp[0, span(d * piece, piece)]
            total = trd[0].astype(F32)
            for at in range(1, n_dp):
                total = total + trd[at].astype(F32)
            tfin[span(d * piece, piece)] = total.astype(BF)
            for step in steps_away:
                t_ag(step).start()

        def t_whole():
            for step in steps_away:
                t_ag(step).wait_recv()

        t_exchange = [t_owned, t_whole]
        t_sends = [t_rs(step) for step in steps_away] + [t_ag(step) for step in steps_away]
        dp_peers = [(ahead(step), s) for step in steps_away]
    else:

        def t_dp(t):
            return remote(tdp.at[t], trd.at[t], r.sem_td, (t,), sum_peers[t])

        def t_spread():
            t_dp(0).start()

        def t_bit(t):
            t_dp(t).wait_recv()
            total = (tdp[t].astype(F32) + trd[t].astype(F32)).astype(BF)
            if t + 1 < bits:
                tdp[t + 1] = total
                t_dp(t + 1).start()
            else:
                tfin[...] = total

        t_exchange = [functools.partial(t_bit, t) for t in range(bits)]
        t_sends = [t_dp(t) for t in range(bits)]
        dp_peers = sum_peers

    barrier = pltpu.get_barrier_semaphore()
    peers = [core, across] + dp_peers
    for peer in peers:
        pl.semaphore_signal(barrier, inc=1, device_id=peer, device_id_type=MESH)

    small_names = names[3:13]
    smalls = [getattr(r, "in_" + n) for n in small_names]
    small_copies = [local(getattr(r, n), smalls[at], r.sem_small, at) for at, n in enumerate(small_names)]
    for copy in small_copies:
        copy.start()

    def start_local(j, carry):
        p_local(j).start()
        c_local(j).start()
        return carry

    lax.fori_loop(0, own, start_local, 0)
    for copy in weight_copies:
        copy.start()

    eye, wide, vpad = r.eye, r.wide, r.vpad
    eye[...] = jnp.where(diagonal(rows, count), 1.0, 0.0).astype(BF)
    vpad[...] = jnp.zeros_like(vpad)
    for copy in small_copies:
        copy.wait()
    for at in range(5):
        vpad[pl.ds(at, 1), pl.ds(0, width)] = smalls[at][...]
    vectors = vpad[...]
    r.vmine[...] = jnp.where(c == 0, vectors, pltpu.roll(vectors, width, 1))

    pl.semaphore_wait(barrier, len(peers))

    def start_images(j, carry):
        p_swap(j).start()
        c_swap(j).start()
        return carry

    v_swap.start()
    lax.fori_loop(0, own, start_images, 0)

    def turn_in(ref, j):
        return dot_nt(eye[...], ref[j])

    def turn_out(values):
        return dot_nt(wide[...], values)[:, :count].astype(BF)

    def merge_send(j):
        p_swap(j).wait_recv()
        p_local(j).wait()
        raw[j, :, near] = turn_in(pin, j).astype(BF)
        p_across(j).start()
        c_swap(j).wait_recv()
        c_local(j).wait()
        valid = jnp.where(c * own + j < r.counts[0], 1.0, 0.0)
        gb[j, first, near] = (turn_in(cin, j) * valid).astype(BF)
        c_across(j).start()

    v_swap.wait_recv()
    vown[...] = r.vmine[...] + r.vpart[...]
    v_across.start()
    merge_send(0)

    wide[...] = jnp.where(diagonal(half, half), 1.0, 0.0).astype(BF)
    hidden_bias = r.hidden_row
    for at in range(hidden // LANE):
        hidden_bias[:, pl.ds(at * LANE, LANE)] = r.in_hidden_bias[pl.ds(at, 1), :]
    for at in range(toks // LANE):
        r.tok_row[:, pl.ds(at * LANE, LANE)] = r.in_tok_in_bias[pl.ds(at, 1), :]
    r.tib[...] = to_column(r.tok_row[...], toks)
    r.tob[...] = to_column(r.in_tok_out_bias[...], rows)
    tok_in_t, tok_in, tok_out, tok_out_t = r.tok_in_t, r.tok_in, r.tok_out, r.tok_out_t
    tok_in_t[...] = dot(eye[...], r.in_tok_in_raw[...]).astype(BF)
    tok_in[...] = dot_nt(wide[...], tok_in_t[...]).astype(BF)
    tok_out[...] = dot(eye[...], r.in_tok_out_raw[...]).astype(BF)
    tok_out_t[...] = dot_nt(wide[...], tok_out[...]).astype(BF)
    merge_send(1)
    gci, gco, cib = r.gci, r.gco, r.cib
    gci[...] = jnp.zeros_like(gci)
    gco[...] = jnp.zeros_like(gco)
    cib[...] = jnp.zeros_like(cib)
    tg[...] = jnp.zeros_like(tg)
    vg[...] = jnp.zeros_like(vg)
    s2o[...] = jnp.zeros_like(s2o)
    s1o[...] = jnp.zeros_like(s1o)
    merge_send(2)
    v_across.wait_recv()

    def vector(row):
        return jnp.concatenate([vown[pl.ds(row, 1), :], vother[pl.ds(row, 1), :]], axis=1)

    def normalise(values):
        centred = values - row_sum(values) * (1.0 / full)
        inverse = lax.rsqrt(row_sum(centred * centred) * (1.0 / full) + EPS)
        return centred * inverse, inverse

    def token_forward(j):
        values = raw[j].astype(F32)
        scaled, inverse = normalise(values)
        normed = (scaled * vector(0) + vector(1)).astype(BF)
        r.sc1[j] = scaled[:, :half].astype(BF)
        r.inv1[j] = inverse
        r.n1[j] = normed[:, :half]
        act, slope = gelu_parts(dot(tok_in[...], normed[:, :half]) + r.tib[...])
        r.tsl[j] = slope.astype(BF)
        act = act.astype(BF)
        r.ta[j] = act
        rest = gelu(dot(tok_in[...], normed[:, half:]) + r.tib[...]).astype(BF)
        mid = values + (dot(tok_out[...], jnp.concatenate([act, rest], axis=1)) + r.tob[...])
        r.mid[j] = mid[:, :half]
        scaled, inverse = normalise(mid)
        r.sc2[j] = scaled[:, :half].astype(BF)
        r.inv2[j] = inverse
        ntb[j, first] = (scaled * vector(2) + vector(3)).astype(BF)

    ghs, slopes = r.ghs, r.slopes
    step = 256

    def channel_front(j):
        nt = ntb[j]
        for at in range(hidden // step):
            cols = pl.ds(at * step, step)
            act, slope = gelu_parts(dot(nt, win[:, cols]) + hidden_bias[:, cols])
            outp[j, :, cols] = act.astype(BF)
            slopes[:, cols] = slope

    def channel_grads(j, part):
        g = gb[j, part]
        for at in range(hidden // step):
            cols = pl.ds(at * step, step)
            grad = (slopes[part, cols] * dot_nt(g, wout[cols, :])).astype(BF)
            ghs[j % 2, part, cols] = grad
            cib[:, cols] += jnp.sum(grad.astype(F32), axis=0, keepdims=True)

    def channel_back(j):
        backp[j] = dot_nt(ghs[j % 2], win[...]).astype(BF)
        back_pair(j).start()

    tiles = hidden // LANE

    def chan_out_grad(j, last):
        if last:
            for at in range(full // LANE):
                cols = pl.ds(at * LANE, LANE)
                total = gco[:, cols] + dot_tn(outp[j], gb[j, :, cols])
                gbuf[pl.ds(at * hidden, hidden)] = total.astype(BF)
        else:
            gco[...] += dot_tn(outp[j], gb[j])

    def chan_in_grad(j, last):
        if last:
            for at in range(tiles):
                cols = pl.ds(at * LANE, LANE)
                total = gci[:, cols] + dot_tn(ntb[j], ghs[j % 2, :, cols])
                start = (full // LANE) * hidden + at * full
                gbuf[pl.ds(start, full)] = total.astype(BF)
        else:
            gci[...] += dot_tn(ntb[j], ghs[j % 2])

    def pair_sums(j):
        back_pair(j).wait_recv()
        total = backp[j, first].astype(F32) + backr[j].astype(F32)
        s2o[j, pl.ds(0, 1)] = to_row(row_sum(total * vector(2)), rows)
        s2o[j, pl.ds(1, 1)] = to_row(row_sum(total * (ntb[j, first].astype(F32) - vector(3))), rows)
        backp[j, first] = total.astype(BF)
        s2_across(j).start()
        back_across(j).start()

    def gather_phase(j, carry):
        @pl.when(j + 3 < own)
        def _():
            merge_send(j + 3)

        p_across(j).wait_recv()
        token_forward(j)
        nt_share(j).start()

        @pl.when(j == 0)
        def _():
            for copy in weight_copies:
                copy.wait()

        @pl.when(j > 0)
        def _():
            g_share(j - 1).wait_recv()
            channel_grads(j - 1, pl.ds(0, 2 * rows))
            chan_out_grad(j - 1, False)

        @pl.when(j > 0)
        def _():
            channel_back(j - 1)

        @pl.when((j > 0) & (j < own - 1))
        def _():
            chan_in_grad(j - 1, False)

        c_across(j).wait_recv()
        g_share(j).start()
        nt_share(j).wait_recv()
        channel_front(j)

        @pl.when((j > 1) & (j < own - 1))
        def _():
            pair_sums(j - 2)

        return carry

    lax.fori_loop(0, own, gather_phase, 0)

    channel_grads(own - 1, first)
    g_share(own - 1).wait_recv()
    channel_grads(own - 1, second)
    chan_out_grad(own - 1, True)
    gradient_first(0, (full // LANE) * hidden)
    chan_in_grad(own - 2, False)
    chan_in_grad(own - 1, True)
    gradient_first((full // LANE) * hidden, gbuf.shape[0])
    def partial_outs(j):
        outp[j] = dot(outp[j], wout[...]).astype(BF)
        out_pair(j).start()

    def pair_outs(j):
        out_pair(j).wait_recv()
        total = outp[j, first].astype(F32) + outr[j].astype(F32)
        outp[j, first] = total.astype(BF)
        out_across(j).start()

    def norm_back(weighted, scaled, inverse, sums):
        mean = to_column(sums[0:1] * (1.0 / full), rows)
        slant = to_column(sums[1:2] * (1.0 / full), rows)
        return inverse * (weighted - mean - scaled * slant)

    def token_backward(j):
        s2_across(j).wait_recv()
        back_across(j).wait_recv()
        grad_normed = backp[j, first, near].astype(F32) + backx[j].astype(F32)
        scaled = r.sc2[j].astype(F32)
        grad_out = gb[j, first, near].astype(F32)
        weighted = grad_normed * vown[pl.ds(2, 1), :]
        grad_mid = grad_out + norm_back(weighted, scaled, r.inv2[j], s2o[j] + s2x[j])
        r.gm[j] = grad_mid
        vg[pl.ds(2, 1), :] += jnp.sum(grad_normed * scaled, axis=0, keepdims=True)
        vg[pl.ds(3, 1), :] += jnp.sum(grad_normed, axis=0, keepdims=True)
        vg[pl.ds(4, 1), :] += jnp.sum(grad_out, axis=0, keepdims=True)
        low = grad_mid.astype(BF)
        ones = jnp.ones((8, half), BF)
        tg[pl.ds(rows, rows), :] += dot_nt(low, r.ta[j])
        tg[pl.ds(2 * rows + 8, 8), pl.ds(0, rows)] += dot_nt(ones, low)
        grad_pre = (r.tsl[j].astype(F32) * dot(tok_out_t[...], low)).astype(BF)
        tg[pl.ds(0, rows), :] += dot_nt(r.n1[j], grad_pre)
        tg[pl.ds(2 * rows, 8), :] += dot_nt(ones, grad_pre)
        grad_one = dot(tok_in_t[...], grad_pre)
        scaled = r.sc1[j].astype(F32)
        vg[pl.ds(0, 1), :] += jnp.sum(grad_one * scaled, axis=0, keepdims=True)
        vg[pl.ds(1, 1), :] += jnp.sum(grad_one, axis=0, keepdims=True)
        weighted = grad_one * vown[pl.ds(0, 1), :]
        r.w1[j] = weighted
        s1o[j, pl.ds(0, 1)] = to_row(row_sum(weighted), rows)
        s1o[j, pl.ds(1, 1)] = to_row(row_sum(weighted * scaled), rows)
        s1_across(j).start()

    def input_grad(j):
        s1_across(j).wait_recv()
        scaled = r.sc1[j].astype(F32)
        grad = r.gm[j] + norm_back(r.w1[j], scaled, r.inv1[j], s1o[j] + s1x[j])
        gis[j] = turn_out(grad.astype(BF))
        gin_give(j).start()
        gin_keep(j).start()

    def mixed_part(j):
        out_across(j).wait_recv()
        total = outp[j, first, near].astype(F32) + outx[j].astype(F32)
        valid = jnp.where(c * own + j < r.counts[0], 1.0, 0.0)
        mos[j] = turn_out((valid * (r.mid[j] + (total + vown[pl.ds(4, 1), :]))).astype(BF))
        mixed_give(j).start()
        mixed_keep(j).start()

    def token_start():
        tb[...] = tg[...].astype(BF)
        for at in range(hidden // half):
            vg[pl.ds(8 + at, 1), :] = cib[:, pl.ds(at * half, half)]
        t_core.start()
        v_core.start()

    def token_core():
        t_core.wait_recv()
        v_core.wait_recv()
        tcur[...] = (tb[tc_keep].astype(F32) + tcore[...].astype(F32)).astype(BF)
        t_across.start()
        vcore[...] = vg[pl.ds(0, 8)] + vcore[...]

    def token_across():
        t_across.wait_recv()
        tdp[0, pl.ds(0, t_quarter)] = (tcur[tx_keep].astype(F32) + txr[...].astype(F32)).astype(BF)
        tdp[0, pl.ds(t_quarter, 16)] = jnp.concatenate([vcore[...], vg[pl.ds(8, 8)]], axis=0).astype(BF)
        t_spread()

    def token_back():
        tall[t_mine] = tfin[pl.ds(0, t_quarter)]
        t_back_x.start()
        vec = tfin[pl.ds(t_quarter, 16)].astype(F32)
        vec_out[pl.ds(0, 8), :] = jnp.where(c == 0, vec, pltpu.roll(vec, width, 1))[:8]
        vec_out[pl.ds(8, 8), :] = vec[8:]

    def token_core_back():
        t_back_x.wait_recv()
        t_back_c.start()

    token_outs = [local(tall, r.tok_grads, r.sem_tok, 0), local(vec_out, r.vec_grads, r.sem_tok, 1)]

    def token_end():
        t_back_c.wait_recv()
        vec_out[pl.ds(16, 16), :] = tall[pl.ds(2 * rows, 16)].astype(F32)
        for copy in token_outs:
            copy.start()

    token_steps = [token_start, token_core, None, token_across, None]
    for exchange in t_exchange[:-1]:
        token_steps += [exchange, None]

    def token_last():
        t_exchange[-1]()
        token_back()

    token_steps += [token_last, None, token_core_back, token_end]

    token_first = own - 1
    outs_first = 2
    mixed_first = own

    inputs_first = 5

    def scatter_phase(i, carry):
        gradient_step(i)

        def each(start, work):
            @pl.when((i >= start) & (i < start + own))
            def _():
                work(i - start)

        @pl.when(i == 0)
        def _():
            channel_back(own - 1)

        @pl.when(i == 1)
        def _():
            for j in range(own - 3, own):
                pair_sums(j)

        each(0, token_backward)
        for e, token_step in enumerate(token_steps):
            if token_step is not None:
                pl.when(i == token_first + e)(token_step)
        each(inputs_first, input_grad)
        each(outs_first, pair_outs)
        each(outs_first - 1, partial_outs)
        each(mixed_first, mixed_part)
        return carry

    lax.fori_loop(0, max(gradient_ticks, token_first + len(token_steps), mixed_first + own), scatter_phase, 0)

    outs = []
    for at in range(full // LANE):
        to = mine if at < half // LANE else theirs
        lanes = pl.ds(pl.multiple_of(to + (at % (half // LANE)) * LANE, LANE), LANE)
        here = pl.ds(at * hidden, hidden)
        outs.append((here, local(fbuf.at[here], r.g_chan_out.at[:, lanes], r.sem_out, len(outs))))
    for at in range(tiles):
        lanes = pl.ds(at * LANE, LANE)
        for part, to in enumerate((mine, theirs)):
            here = pl.ds((full // LANE) * hidden + at * full + part * half, half)
            outs.append((here, local(fbuf.at[here], r.g_chan_in.at[pl.ds(to, half), lanes], r.sem_out, len(outs))))
    for k in range(gradient_items):
        gradient_last(k)
        for here, copy in outs:
            if k * chunk < here.start + here.size <= (k + 1) * chunk:
                copy.start()

    def gradient_drain(k, carry):
        gradient_sent(k)
        return carry

    lax.fori_loop(0, gradient_items, gradient_drain, 0)

    def drain(j, carry):
        for make in (p_swap, c_swap, p_across, c_across, nt_share, g_share, out_pair, back_pair):
            make(j).wait_send()
        for make in (out_across, back_across, s2_across, s1_across):
            make(j).wait_send()
        for make in (mixed_give, gin_give, mixed_keep, gin_keep):
            make(j).wait()
        return carry

    lax.fori_loop(0, own, drain, 0)
    for copy in [v_swap, v_across, t_core, t_across, t_back_x, t_back_c, v_core] + t_sends:
        copy.wait_send()
    for _, copy in outs:
        copy.wait()
    for copy in token_outs:
        copy.wait()


def run_layer(n_dp, **arrays):
    batch, width, count = arrays["patches"].shape
    own = batch // 2
    full, hidden = arrays["win_hbm"].shape
    half = full // 2
    toks = arrays["tok_in_raw"].shape[1]
    rows = -(-count // 16) * 16
    bits = n_dp.bit_length() - 1
    grad_rows = 2 * full * hidden // LANE
    folded = n_dp == 8
    choices = (8, 4, 2) if folded else (9, 3, 1)
    parts = 18 if folded else n_dp
    chunks = next(k for k in choices if grad_rows % (k * parts * (64 if folded else 16)) == 0)
    chunk = grad_rows // chunks
    cfg = (n_dp, own, count, rows, half, full, hidden, toks, chunks, chunk)
    vmem = pltpu.VMEM
    dma = pltpu.SemaphoreType.DMA
    two, whole = chunk * 14 // 36, chunk * 4 // 18
    t_rows = -(-(2 * rows + 16) // 64) * 64
    scratch = dict(
        win=vmem((full, hidden), BF),
        wout=vmem((hidden, full), BF),
        pin=vmem((own, half, count), BF),
        cin=vmem((own, half, count), BF),
        vpad=vmem((8, half), F32),
        hidden_row=vmem((1, hidden), F32),
        tok_row=vmem((1, toks), F32),
        vmine=vmem((8, half), F32),
        vpart=vmem((8, half), F32),
        vown=vmem((8, half), F32),
        vother=vmem((8, half), F32),
        eye=vmem((rows, count), BF),
        wide=vmem((half, half), BF),
        tok_in_t=vmem((rows, toks), BF),
        tok_in=vmem((toks, rows), BF),
        tok_out=vmem((rows, toks), BF),
        tok_out_t=vmem((toks, rows), BF),
        tib=vmem((toks, 1), F32),
        tob=vmem((rows, 1), F32),
        raw=vmem((own, rows, full), BF),
        ntb=vmem((own, 2 * rows, full), BF),
        gb=vmem((own, 2 * rows, full), BF),
        ghs=vmem((2, 2 * rows, hidden), BF),
        slopes=vmem((2 * rows, hidden), F32),
        gci=vmem((full, hidden), F32),
        gco=vmem((hidden, full), F32),
        cib=vmem((1, hidden), F32),
        outp=vmem((own, 2 * rows, full), BF),
        outr=vmem((own, rows, full), BF),
        backp=vmem((own, 2 * rows, full), BF),
        backr=vmem((own, rows, full), BF),
        outx=vmem((own, rows, half), BF),
        backx=vmem((own, rows, half), BF),
        s2o=vmem((own, 8, rows), F32),
        s2x=vmem((own, 8, rows), F32),
        s1o=vmem((own, 8, rows), F32),
        s1x=vmem((own, 8, rows), F32),
        n1=vmem((own, rows, half), BF),
        ta=vmem((own, toks, half), BF),
        tsl=vmem((own, toks, half), BF),
        mid=vmem((own, rows, half), F32),
        sc1=vmem((own, rows, half), BF),
        sc2=vmem((own, rows, half), BF),
        inv1=vmem((own, rows, 1), F32),
        inv2=vmem((own, rows, 1), F32),
        gm=vmem((own, rows, half), F32),
        w1=vmem((own, rows, half), F32),
        gbuf=vmem((grad_rows, LANE), BF),
        fbuf=vmem((grad_rows, LANE), BF),
        tg=vmem((t_rows, toks), F32),
        tb=vmem((t_rows, toks), BF),
        tcore=vmem((t_rows // 2, toks), BF),
        tcur=vmem((t_rows // 2, toks), BF),
        txr=vmem((t_rows // 4, toks), BF),
        tdp=vmem((1 if folded else bits, t_rows // 4 + 16, toks), BF),
        trd=vmem((n_dp, (t_rows // 4 + 16) // n_dp, toks) if folded else (bits, t_rows // 4 + 16, toks), BF),
        tall=vmem((t_rows, toks), BF),
        vec_out=vmem((32, half), F32),
        sem_tok=dma((2,)),
        tfin=vmem((t_rows // 4 + 16, toks), BF),
        vg=vmem((16, half), F32),
        vcore=vmem((8, half), F32),
        sem_w=dma((4,)),
        sem_small=dma((10,)),
        sem_v=dma((2, 2)),
        sem_out=dma((2 * (hidden // LANE) + full // LANE,)),
        sem_t=dma((2, 5)),
        sem_td=dma((2, bits)),
        sem_tr=dma((2, n_dp)),
        sem_ta=dma((2, n_dp)),
    )
    for name in list(arrays)[3:13]:
        scratch["in_" + name] = vmem(arrays[name].shape, arrays[name].dtype)
    for name in ("pl", "cl", "mk", "gk"):
        scratch["sem_" + name] = dma((own,))
    for name in ("ps", "cs", "px", "cx", "nt", "g", "op", "bp", "ox", "bx", "s2", "s1", "mg", "gg"):
        scratch["sem_" + name] = dma((2, own))
    if folded:
        scratch["e0"] = vmem((chunks * two, LANE), BF)
        scratch["e1"] = vmem((chunks * two, LANE), BF)
        scratch["e2"] = vmem((chunks * two // 2, LANE), BF)
        scratch["o0"] = vmem((chunks * whole, LANE), BF)
        scratch["o1"] = vmem((chunks * whole // 2, LANE), BF)
        scratch["o2"] = vmem((chunks * whole // 4, LANE), BF)
        for name in [e + str(k) for e in "eo" for k in range(7)]:
            scratch["sem_" + name] = dma((2, chunks))
    else:
        scratch["rbuf"] = vmem((chunks * (chunk - (chunk >> bits)), LANE), BF)
        scratch["sem_rs"] = dma((2, bits, chunks))
        scratch["sem_ag"] = dma((2, bits, chunks))
    hbm = pl.BlockSpec(memory_space=pl.ANY)
    places = dict(counts=pl.BlockSpec(memory_space=pltpu.SMEM))
    outs = dict(
        mixed=((batch, width, count), BF),
        gin=((batch, width, count), BF),
        tok_grads=((t_rows, toks), BF),
        vec_grads=((32, half), F32),
        g_chan_in=((full, hidden), BF),
        g_chan_out=((hidden, full), BF),
    )
    names = list(arrays) + list(outs) + list(scratch)
    results = pl.pallas_call(
        functools.partial(layer_kernel, cfg, names),
        out_shape=tuple(jax.ShapeDtypeStruct(*outs[name]) for name in outs),
        in_specs=[places.get(name, hbm) for name in arrays],
        out_specs=tuple(places.get(name, hbm) for name in outs),
        scratch_shapes=list(scratch.values()),
        compiler_params=pltpu.CompilerParams(
            collective_id=0, has_side_effects=True, vmem_limit_bytes=63 * 2**20
        ),
        name="mixer_layer",
    )(*arrays.values())
    return SimpleNamespace(**dict(zip(outs, results)))


def finish_kernel(names, smalls, *refs):
    r = SimpleNamespace(**dict(zip(names, refs)))
    count, toks = r.tok_in.shape
    rows = -(-count // 16) * 16
    parts, step = r.pieces.shape[1:3]
    images = r.images.shape[1] // 2

    def copy(src, dst, at):
        return pltpu.make_async_copy(src, dst, r.sems.at[at])

    loads, stores = [], []
    for at, (raw, done) in enumerate(((r.chan_out_raw, r.chan_out), (r.chan_in_raw, r.chan_in))):
        for part in range(parts):
            here = pl.ds(part * step, step)
            loads.append(copy(raw.at[here], r.pieces.at[at, part], len(loads)))
            stores.append(copy(r.wide.at[at, part], done.at[here], 2 * parts + len(stores)))
    first = 4 * parts
    images_in, images_out = [], []
    for at, (raw, done) in enumerate(((r.mixed_raw, r.mixed), (r.gin_raw, r.gin))):
        for part in range(2):
            here = pl.ds(part * images, images)
            images_in.append(copy(raw.at[here], r.images.at[at, here], first + len(images_in)))
            images_out.append(copy(r.images.at[at, here], done.at[here], first + 4 + len(images_out)))
    first += 8
    tok_load = copy(r.tok_raw, r.tall, first)
    vec_load = copy(r.vec_raw, r.vec, first + 1)
    small_stores = [
        copy(getattr(r, "out_" + name), getattr(r, name), first + 2 + at) for at, name in enumerate(smalls)
    ]
    for load in loads[:2] + [tok_load, vec_load] + loads[2:] + images_in:
        load.start()

    def widen(at):
        loads[at].wait()
        r.wide[at // parts, at % parts] = r.pieces[at // parts, at % parts].astype(F32)
        stores[at].start()

    widen(0)
    widen(1)
    tok_load.wait()
    vec_load.wait()
    vec, tall = r.vec, r.tall
    width = r.ln1_gain.shape[1]
    half = vec.shape[1]
    r.out_tok_in[...] = tall[pl.ds(0, rows)][:count].astype(F32)
    r.out_tok_out[...] = tall[pl.ds(rows, rows)][:count].astype(F32)
    outs = (r.out_ln1_gain, r.out_ln1_bias, r.out_ln2_gain, r.out_ln2_bias, r.out_chan_out_bias)
    for at, done in enumerate(outs):
        done[...] = vec[pl.ds(at, 1), :][:, :width]
    for at in range(r.chan_in_bias.shape[0]):
        row, lane = divmod(at * LANE, half)
        r.out_chan_in_bias[pl.ds(at, 1), :] = vec[pl.ds(8 + row, 1), pl.ds(lane, LANE)]
    for at in range(toks // LANE):
        r.out_tok_in_bias[pl.ds(at, 1), :] = vec[pl.ds(16, 1), pl.ds(at * LANE, LANE)]
    r.out_tok_out_bias[...] = vec[pl.ds(24, 1), :][:, :count]
    for store in small_stores:
        store.start()
    for at in range(2, len(loads)):
        widen(at)
    for load, store in zip(images_in, images_out):
        load.wait()
        store.start()
    for store in stores + images_out + small_stores:
        store.wait()


def finish(out, count, width):
    full, hidden = out.g_chan_in.shape
    toks = out.tok_grads.shape[1]
    hbm = pl.BlockSpec(memory_space=pl.ANY)
    arrays = dict(
        mixed_raw=out.mixed,
        gin_raw=out.gin,
        chan_in_raw=out.g_chan_in,
        chan_out_raw=out.g_chan_out,
        tok_raw=out.tok_grads,
        vec_raw=out.vec_grads,
    )
    outs = dict(
        mixed=(out.mixed.shape, BF),
        gin=(out.gin.shape, BF),
        chan_in=((full, hidden), F32),
        chan_out=((hidden, full), F32),
        tok_in=((count, toks), F32),
        tok_out=((count, toks), F32),
        ln1_gain=((1, width), F32),
        ln1_bias=((1, width), F32),
        ln2_gain=((1, width), F32),
        ln2_bias=((1, width), F32),
        chan_out_bias=((1, width), F32),
        chan_in_bias=((hidden // LANE, LANE), F32),
        tok_in_bias=((toks // LANE, LANE), F32),
        tok_out_bias=((1, count), F32),
    )
    smalls = list(outs)[4:]
    parts = 4
    scratch = dict(
        pieces=pltpu.VMEM((2, parts, full // parts, hidden), BF),
        wide=pltpu.VMEM((2, parts, full // parts, hidden), F32),
        images=pltpu.VMEM((2,) + out.mixed.shape, BF),
        tall=pltpu.VMEM(out.tok_grads.shape, BF),
        vec=pltpu.VMEM(out.vec_grads.shape, F32),
        sems=pltpu.SemaphoreType.DMA((4 * parts + 10 + len(smalls),)),
    )
    for name in smalls:
        scratch["out_" + name] = pltpu.VMEM(*outs[name])
    names = list(arrays) + list(outs) + list(scratch)
    results = pl.pallas_call(
        functools.partial(finish_kernel, names, smalls),
        out_shape=tuple(jax.ShapeDtypeStruct(*outs[name]) for name in outs),
        in_specs=[hbm] * len(arrays),
        out_specs=(hbm,) * len(outs),
        scratch_shapes=list(scratch.values()),
        compiler_params=pltpu.CompilerParams(vmem_limit_bytes=63 * 2**20),
        name="finish",
    )(*arrays.values())
    return SimpleNamespace(**dict(zip(outs, results)))


def per_device(
    n_dp,
    image_counts,
    patches,
    ln1_gain,
    ln1_bias,
    tok_in_weight,
    tok_in_bias,
    tok_out_weight,
    tok_out_bias,
    ln2_gain,
    ln2_bias,
    chan_in_weight,
    chan_in_bias,
    chan_out_weight,
    chan_out_bias,
    cotangent,
):
    out = run_layer(
        n_dp,
        counts=image_counts,
        patches=jnp.transpose(patches, (1, 2, 0)),
        cot=jnp.transpose(cotangent, (1, 2, 0)),
        ln1_gain=ln1_gain[None, :],
        ln1_bias=ln1_bias[None, :],
        ln2_gain=ln2_gain[None, :],
        ln2_bias=ln2_bias[None, :],
        chan_out_bias=chan_out_bias[None, :],
        hidden_bias=chan_in_bias.reshape(-1, LANE),
        tok_in_bias=tok_in_bias.reshape(-1, LANE),
        tok_out_bias=tok_out_bias[None, :],
        tok_in_raw=tok_in_weight.T,
        tok_out_raw=tok_out_weight,
        win_hbm=chan_in_weight,
        wout_hbm=chan_out_weight,
    )
    out = finish(out, patches.shape[0], patches.shape[2])
    return (
        jnp.transpose(out.mixed, (2, 0, 1)),
        jnp.transpose(out.gin, (2, 0, 1)),
        out.ln1_gain[0],
        out.ln1_bias[0],
        out.tok_in.T,
        out.tok_in_bias.reshape(-1),
        out.tok_out,
        out.tok_out_bias[0],
        out.ln2_gain[0],
        out.ln2_bias[0],
        out.chan_in,
        out.chan_in_bias.reshape(-1),
        out.chan_out,
        out.chan_out_bias[0],
    )


def solution(mesh):
    in_specs = (
        P("dp"),
        P(None, "dp", "seq"),
        P("seq"),
        P("seq"),
        P(),
        P(),
        P(),
        P(),
        P("seq"),
        P("seq"),
        P(None, "seq"),
        P("seq"),
        P("seq", None),
        P("seq"),
        P(None, "dp", "seq"),
    )
    out_specs = (
        P(None, "dp", "seq"),
        P(None, "dp", "seq"),
        P("seq"),
        P("seq"),
        P(),
        P(),
        P(),
        P(),
        P("seq"),
        P("seq"),
        P(None, "seq"),
        P("seq"),
        P("seq", None),
        P("seq"),
    )
    return jax.shard_map(
        functools.partial(per_device, mesh.shape["dp"]),
        mesh=mesh,
        in_specs=in_specs,
        out_specs=out_specs,
        check_vma=False,
    )
```

```python
import functools
from types import SimpleNamespace

import jax
import jax.numpy as jnp
from jax import lax
from jax.experimental import pallas as pl
from jax.experimental.pallas import tpu as pltpu
from jax.sharding import PartitionSpec as P

MESH = pl.DeviceIdType.MESH
BF = jnp.bfloat16
F32 = jnp.float32
EPS = 1e-06
GELU_A = 0.7978845608028654
GELU_B = GELU_A * 0.044715
LANE = 128


def gelu_parts(x):
    square = x * x
    tanh = jnp.tanh(x * (GELU_A + GELU_B * square))
    half = 0.5 + 0.5 * tanh
    slope = half + (0.5 * x) * (1.0 - tanh * tanh) * (GELU_A + (3.0 * GELU_B) * square)
    return x * half, slope


def gelu(x):
    return x * (0.5 + 0.5 * jnp.tanh(x * (GELU_A + GELU_B * (x * x))))


def dot(a, b):
    return lax.dot_general(a, b, (((1,), (0,)), ((), ())), preferred_element_type=F32)


def dot_nt(a, b):
    return lax.dot_general(a, b, (((1,), (1,)), ((), ())), preferred_element_type=F32)


def dot_tn(a, b):
    return lax.dot_general(a, b, (((0,), (0,)), ((), ())), preferred_element_type=F32)


def diagonal(rows, columns):
    return lax.broadcasted_iota(jnp.int32, (rows, columns), 0) == lax.broadcasted_iota(
        jnp.int32, (rows, columns), 1
    )


def to_row(values, columns):
    return jnp.sum(jnp.where(diagonal(values.shape[0], columns), values, 0.0), axis=0, keepdims=True)


def to_column(values, rows):
    return jnp.sum(jnp.where(diagonal(rows, values.shape[1]), values, 0.0), axis=1, keepdims=True)


def row_sum(values):
    return jnp.sum(values, axis=-1, keepdims=True)


def layer_kernel(cfg, names, *refs):
    n_dp, own, count, rows, half, full, hidden, toks, chunks, chunk = cfg
    r = SimpleNamespace(**dict(zip(names, refs)))
    width = half // 2
    d = lax.axis_index("dp")
    s = lax.axis_index("seq")
    c = s % 2
    x = s // 2
    core = (d, s + 1 - 2 * c)
    across = (d, s + 2 - 4 * x)
    folded = n_dp == 8
    bits = n_dp.bit_length() - 1

    def dp_bit(t):
        return (d // (1 << t)) % 2

    def dp_peer(t):
        m = 1 << t
        return (d + m - 2 * m * dp_bit(t), s)

    a = d // 2
    b = d % 2
    end = a % 3 == 0
    middle = a % 3 != 0
    m = a // 2
    side = dp_peer(0)
    fold = dp_peer(1)
    mirror = ((n_dp // 2 - 1 - a) * 2 + b, s)
    sum_peers = [side, fold, mirror] if folded else [dp_peer(t) for t in range(bits)]

    def remote(src, dst, sems, at, target):
        return pltpu.make_async_remote_copy(
            src_ref=src,
            dst_ref=dst,
            send_sem=sems.at[(0,) + at],
            recv_sem=sems.at[(1,) + at],
            device_id=target,
            device_id_type=MESH,
        )

    def local(src, dst, sems, at):
        return pltpu.make_async_copy(src, dst, sems.at[at])

    win, wout, pin, cin, raw = r.win, r.wout, r.pin, r.cin, r.raw
    ntb, gb, outp, outr, backp, backr = r.ntb, r.gb, r.outp, r.outr, r.backp, r.backr
    outx, backx, s2o, s2x, s1o, s1x = r.outx, r.backx, r.s2o, r.s2x, r.s1o, r.s1x
    vown, vother, tg, vg, vec_out = r.vown, r.vother, r.tg, r.vg, r.vec_out
    gbuf, fbuf = r.gbuf, r.fbuf
    mos, gis = pin, cin

    mine = pl.multiple_of(x * half, LANE)
    theirs = pl.multiple_of((1 - x) * half, LANE)
    weight_copies = [
        local(r.win_hbm.at[pl.ds(mine, half)], win.at[pl.ds(0, half)], r.sem_w, 0),
        local(r.win_hbm.at[pl.ds(theirs, half)], win.at[pl.ds(half, half)], r.sem_w, 1),
        local(r.wout_hbm.at[:, pl.ds(mine, half)], wout.at[:, pl.ds(0, half)], r.sem_w, 2),
        local(r.wout_hbm.at[:, pl.ds(theirs, half)], wout.at[:, pl.ds(half, half)], r.sem_w, 3),
    ]

    place = pl.ds(pl.multiple_of(c * width, 16), width)

    def p_local(j):
        return local(r.patches.at[c * own + j], pin.at[j, place], r.sem_pl, j)

    def c_local(j):
        return local(r.cot.at[c * own + j], cin.at[j, place], r.sem_cl, j)

    def p_swap(j):
        return remote(r.patches.at[(1 - c) * own + j], pin.at[j, place], r.sem_ps, (j,), core)

    def c_swap(j):
        return remote(r.cot.at[(1 - c) * own + j], cin.at[j, place], r.sem_cs, (j,), core)

    v_swap = remote(r.vmine, r.vpart, r.sem_v, (0,), core)
    v_across = remote(vown, vother, r.sem_v, (1,), across)

    first = pl.ds(0, rows)
    second = pl.ds(rows, rows)
    near = pl.ds(0, half)
    far = pl.ds(half, half)

    def p_across(j):
        return remote(raw.at[j, :, near], raw.at[j, :, far], r.sem_px, (j,), across)

    def c_across(j):
        return remote(gb.at[j, first, near], gb.at[j, first, far], r.sem_cx, (j,), across)

    def nt_share(j):
        return remote(ntb.at[j, first], ntb.at[j, second], r.sem_nt, (j,), core)

    def g_share(j):
        return remote(gb.at[j, first], gb.at[j, second], r.sem_g, (j,), core)

    def out_pair(j):
        return remote(outp.at[j, second], outr.at[j], r.sem_op, (j,), core)

    def back_pair(j):
        return remote(backp.at[j, second], backr.at[j], r.sem_bp, (j,), core)

    def out_across(j):
        return remote(outp.at[j, first, far], outx.at[j], r.sem_ox, (j,), across)

    def back_across(j):
        return remote(backp.at[j, first, far], backx.at[j], r.sem_bx, (j,), across)

    def s2_across(j):
        return remote(s2o.at[j], s2x.at[j], r.sem_s2, (j,), across)

    def s1_across(j):
        return remote(s1o.at[j], s1x.at[j], r.sem_s1, (j,), across)

    other = pl.ds(pl.multiple_of((1 - c) * width, 16), width)

    def mixed_give(j):
        return remote(mos.at[j, other], r.mixed.at[c * own + j], r.sem_mg, (j,), core)

    def gin_give(j):
        return remote(gis.at[j, other], r.gin.at[c * own + j], r.sem_gg, (j,), core)

    def mixed_keep(j):
        return local(mos.at[j, place], r.mixed.at[c * own + j], r.sem_mk, j)

    def gin_keep(j):
        return local(gis.at[j, place], r.gin.at[c * own + j], r.sem_gk, j)

    def span(start, size):
        return pl.ds(pl.multiple_of(start, 16), size)

    def add_into(target, at, source, source_at):
        target[at] = (gbuf[at].astype(F32) + source[source_at].astype(F32)).astype(BF)


    if folded:
        pairs = chunks
        two, four = chunk * 14 // 36, chunk * 14 // 72

        def even(k):
            return k * chunk

        def e_side(k):
            return remote(
                gbuf.at[span(even(k) + (1 - b) * two, two)], r.e0.at[span(k * two, two)], r.sem_e0, (k,), side
            )

        def e_half(k):
            return span(even(k) + b * two, two)

        def e_fold(k):
            return remote(gbuf.at[e_half(k)], r.e1.at[span(k * two, two)], r.sem_e1, (k,), fold)

        def e_mirror(k):
            return remote(
                gbuf.at[span(even(k) + b * two + (1 - m) * four, four)],
                r.e2.at[span(k * four, four)],
                r.sem_e2,
                (k,),
                mirror,
            )

        def e_quarter(k):
            return span(even(k) + b * two + m * four, four)

        def e_mirror_back(k):
            return remote(fbuf.at[e_quarter(k)], fbuf.at[e_quarter(k)], r.sem_e3, (k,), mirror)

        def e_fold_back(k):
            return remote(fbuf.at[e_half(k)], fbuf.at[e_half(k)], r.sem_e4, (k,), fold)

        def e_side_back(k):
            return remote(fbuf.at[e_half(k)], fbuf.at[e_half(k)], r.sem_e5, (k,), side)

        whole, three, six = chunk * 4 // 18, chunk * 4 // 36, chunk * 4 // 72

        def odd(k):
            return k * chunk + 2 * two

        def o_fold(k):
            return remote(gbuf.at[span(odd(k), whole)], r.o0.at[span(k * whole, whole)], r.sem_o0, (k,), fold)

        def o_mirror(k):
            return remote(
                gbuf.at[span(odd(k) + (1 - m) * three, three)],
                r.o1.at[span(k * three, three)],
                r.sem_o1,
                (k,),
                mirror,
            )

        def o_half(k):
            return span(odd(k) + m * three, three)

        def o_rest(k):
            return span(odd(k) + (1 - m) * three, three)

        def o_side(k):
            return remote(
                gbuf.at[span(odd(k) + m * three + (1 - b) * six, six)],
                r.o2.at[span(k * six, six)],
                r.sem_o2,
                (k,),
                side,
            )

        def o_quarter(k):
            return span(odd(k) + m * three + b * six, six)

        def o_side_back(k):
            return remote(fbuf.at[o_quarter(k)], fbuf.at[o_quarter(k)], r.sem_o3, (k,), side)

        def o_mirror_back(k):
            return remote(fbuf.at[o_half(k)], fbuf.at[o_half(k)], r.sem_o4, (k,), mirror)

        def o_fold_back(k):
            return remote(fbuf.at[o_half(k)], fbuf.at[o_half(k)], r.sem_o5, (k,), fold)

        def o_fold_rest(k):
            return remote(fbuf.at[o_rest(k)], fbuf.at[o_rest(k)], r.sem_o6, (k,), fold)

        def e_step(e, k):
            if e == 0:
                e_side(k).wait_recv()
                add_into(gbuf, e_half(k), r.e0, span(k * two, two))

                @pl.when(end)
                def _():
                    e_fold(k).start()

            elif e == 1:

                @pl.when(middle)
                def _():
                    e_fold(k).wait_recv()
                    add_into(gbuf, e_half(k), r.e1, span(k * two, two))
                    e_mirror(k).start()

            elif e == 2:

                @pl.when(middle)
                def _():
                    e_mirror(k).wait_recv()
                    add_into(fbuf, e_quarter(k), r.e2, span(k * four, four))
                    e_mirror_back(k).start()

            elif e == 3:

                @pl.when(middle)
                def _():
                    e_mirror_back(k).wait_recv()
                    e_fold_back(k).start()
                    e_side_back(k).start()

            else:

                @pl.when(end)
                def _():
                    e_fold_back(k).wait_recv()
                    e_side_back(k).start()

        def o_step(e, k):
            @pl.when(middle)
            def _():
                if e == 0:
                    o_fold(k).wait_recv()
                    add_into(gbuf, span(odd(k), whole), r.o0, span(k * whole, whole))
                    o_mirror(k).start()
                elif e == 1:
                    o_mirror(k).wait_recv()
                    add_into(gbuf, o_half(k), r.o1, span(k * three, three))
                    o_side(k).start()
                elif e == 2:
                    o_side(k).wait_recv()
                    add_into(fbuf, o_quarter(k), r.o2, span(k * six, six))
                    o_side_back(k).start()
                elif e == 3:
                    o_side_back(k).wait_recv()
                    o_mirror_back(k).start()
                    o_fold_back(k).start()
                else:
                    o_mirror_back(k).wait_recv()
                    o_fold_rest(k).start()

        e_at = (0, 1, 2, 3, 5)
        o_at = (1, 3, 5, 6, 7)

        def o_first(k):
            @pl.when(end)
            def _():
                o_fold(k).start()

        def gradient_first(before, ready):
            for k in range(pairs):
                if before < (k + 1) * chunk <= ready:
                    e_side(k).start()

        def gradient_step(i):
            @pl.when(i < pairs)
            def _():
                o_first(i)

            for stage, places in ((o_step, o_at), (e_step, e_at)):
                for e, at in enumerate(places):

                    @pl.when((i >= at) & (i < at + pairs))
                    def _(stage=stage, e=e, at=at):
                        stage(e, i - at)

        def gradient_last(k):
            e_side_back(k).wait_recv()

            @pl.when(end)
            def _():
                o_fold_back(k).wait_recv()
                o_fold_rest(k).wait_recv()

        def gradient_sent(k):
            e_side(k).wait_send()
            e_side_back(k).wait_send()

            @pl.when(end)
            def _():
                e_fold(k).wait_send()
                o_fold(k).wait_send()

            @pl.when(middle)
            def _():
                for make in (e_mirror, e_mirror_back, e_fold_back, o_mirror, o_side, o_side_back):
                    make(k).wait_send()
                for make in (o_mirror_back, o_fold_back, o_fold_rest):
                    make(k).wait_send()

        gradient_ticks = pairs + max(e_at[-1], o_at[-1])
        gradient_items = pairs
    else:
        def segment(k, t):
            start = k * chunk
            for u in range(t):
                start = start + dp_bit(u) * (chunk >> (u + 1))
            return start

        bases = [chunks * (chunk - (chunk >> t)) for t in range(bits)]

        def rs_at(k, t):
            size = chunk >> (t + 1)
            return span(bases[t] + k * size, size)

        def rs_send(k, t):
            size = chunk >> (t + 1)
            return remote(
                gbuf.at[span(segment(k, t) + (1 - dp_bit(t)) * size, size)],
                r.rbuf.at[rs_at(k, t)],
                r.sem_rs,
                (t, k),
                dp_peer(t),
            )

        def ag_send(k, t):
            at = span(segment(k, t + 1), chunk >> (t + 1))
            return remote(fbuf.at[at], fbuf.at[at], r.sem_ag, (t, k), dp_peer(t))

        def gradient_first(before, ready):
            for k in range(chunks):
                if before < (k + 1) * chunk <= ready:
                    rs_send(k, 0).start()

        def gradient_step(i):
            for e in reversed(range(2 * bits - 1)):
                k = i - e

                @pl.when((k >= 0) & (k < chunks))
                def _(e=e, k=k):
                    if e < bits:
                        rs_send(k, e).wait_recv()
                        at = span(segment(k, e + 1), chunk >> (e + 1))
                        add_into(gbuf if e + 1 < bits else fbuf, at, r.rbuf, rs_at(k, e))
                        if e + 1 < bits:
                            rs_send(k, e + 1).start()
                        else:
                            ag_send(k, e).start()
                    else:
                        t = 2 * bits - 1 - e
                        ag_send(k, t).wait_recv()
                        ag_send(k, t - 1).start()

        def gradient_last(k):
            ag_send(k, 0).wait_recv()

        def gradient_sent(k):
            for t in range(bits):
                rs_send(k, t).wait_send()
                ag_send(k, t).wait_send()

        gradient_ticks = chunks + 2 * bits - 2
        gradient_items = chunks

    t_half = tg.shape[0] // 2
    t_quarter = t_half // 2
    tc_keep = span(c * t_half, t_half)
    tc_give = span((1 - c) * t_half, t_half)
    tx_keep = span(x * t_quarter, t_quarter)
    tx_give = span((1 - x) * t_quarter, t_quarter)
    t_mine = span(c * t_half + x * t_quarter, t_quarter)
    tb, tcore, tcur, txr, tdp, trd, tall = r.tb, r.tcore, r.tcur, r.txr, r.tdp, r.trd, r.tall
    vcore, tfin = r.vcore, r.tfin
    t_core = remote(tb.at[tc_give], tcore, r.sem_t, (0,), core)
    t_across = remote(tcur.at[tx_give], txr, r.sem_t, (1,), across)
    t_back_x = remote(tall.at[t_mine], tall.at[t_mine], r.sem_t, (2,), across)
    t_back_c = remote(tall.at[tc_keep], tall.at[tc_keep], r.sem_t, (3,), core)
    v_core = remote(vg.at[pl.ds(0, 8)], vcore, r.sem_t, (4,), core)

    if folded:
        piece = tdp.shape[1] // n_dp
        steps_away = range(1, n_dp)

        def ahead(step):
            return (d + step) % n_dp

        def t_rs(step):
            return remote(
                tdp.at[0, span(ahead(step) * piece, piece)], trd.at[d], r.sem_tr, (step,), (ahead(step), s)
            )

        def t_ag(step):
            own_piece = span(d * piece, piece)
            return remote(tfin.at[own_piece], tfin.at[own_piece], r.sem_ta, (step,), (ahead(step), s))

        def t_spread():
            for step in steps_away:
                t_rs(step).start()

        def t_owned():
            for step in steps_away:
                t_rs(step).wait_recv()
            trd[d] = tdp[0, span(d * piece, piece)]
            total = trd[0].astype(F32)
            for at in range(1, n_dp):
                total = total + trd[at].astype(F32)
            tfin[span(d * piece, piece)] = total.astype(BF)
            for step in steps_away:
                t_ag(step).start()

        def t_whole():
            for step in steps_away:
                t_ag(step).wait_recv()

        t_exchange = [t_owned, t_whole]
        t_sends = [t_rs(step) for step in steps_away] + [t_ag(step) for step in steps_away]
        dp_peers = [(ahead(step), s) for step in steps_away]
    else:

        def t_dp(t):
            return remote(tdp.at[t], trd.at[t], r.sem_td, (t,), sum_peers[t])

        def t_spread():
            t_dp(0).start()

        def t_bit(t):
            t_dp(t).wait_recv()
            total = (tdp[t].astype(F32) + trd[t].astype(F32)).astype(BF)
            if t + 1 < bits:
                tdp[t + 1] = total
                t_dp(t + 1).start()
            else:
                tfin[...] = total

        t_exchange = [functools.partial(t_bit, t) for t in range(bits)]
        t_sends = [t_dp(t) for t in range(bits)]
        dp_peers = sum_peers

    barrier = pltpu.get_barrier_semaphore()
    peers = [core, across] + dp_peers
    for peer in peers:
        pl.semaphore_signal(barrier, inc=1, device_id=peer, device_id_type=MESH)

    small_names = names[3:13]
    smalls = [getattr(r, "in_" + n) for n in small_names]
    small_copies = [local(getattr(r, n), smalls[at], r.sem_small, at) for at, n in enumerate(small_names)]
    for copy in small_copies:
        copy.start()

    def start_local(j, carry):
        p_local(j).start()
        c_local(j).start()
        return carry

    lax.fori_loop(0, own, start_local, 0)
    for copy in weight_copies:
        copy.start()

    eye, wide, vpad = r.eye, r.wide, r.vpad
    eye[...] = jnp.where(diagonal(rows, count), 1.0, 0.0).astype(BF)
    vpad[...] = jnp.zeros_like(vpad)
    for copy in small_copies:
        copy.wait()
    for at in range(5):
        vpad[pl.ds(at, 1), pl.ds(0, width)] = smalls[at][...]
    vectors = vpad[...]
    r.vmine[...] = jnp.where(c == 0, vectors, pltpu.roll(vectors, width, 1))

    pl.semaphore_wait(barrier, len(peers))

    def start_images(j, carry):
        p_swap(j).start()
        c_swap(j).start()
        return carry

    v_swap.start()
    lax.fori_loop(0, own, start_images, 0)

    def turn_in(ref, j):
        return dot_nt(eye[...], ref[j])

    def turn_out(values):
        return dot_nt(wide[...], values)[:, :count].astype(BF)

    def merge_send(j):
        p_swap(j).wait_recv()
        p_local(j).wait()
        raw[j, :, near] = turn_in(pin, j).astype(BF)
        p_across(j).start()
        c_swap(j).wait_recv()
        c_local(j).wait()
        valid = jnp.where(c * own + j < r.counts[0], 1.0, 0.0)
        gb[j, first, near] = (turn_in(cin, j) * valid).astype(BF)
        c_across(j).start()

    v_swap.wait_recv()
    vown[...] = r.vmine[...] + r.vpart[...]
    v_across.start()
    merge_send(0)

    wide[...] = jnp.where(diagonal(half, half), 1.0, 0.0).astype(BF)
    hidden_bias = r.hidden_row
    for at in range(hidden // LANE):
        hidden_bias[:, pl.ds(at * LANE, LANE)] = r.in_hidden_bias[pl.ds(at, 1), :]
    for at in range(toks // LANE):
        r.tok_row[:, pl.ds(at * LANE, LANE)] = r.in_tok_in_bias[pl.ds(at, 1), :]
    r.tib[...] = to_column(r.tok_row[...], toks)
    r.tob[...] = to_column(r.in_tok_out_bias[...], rows)
    tok_in_t, tok_in, tok_out, tok_out_t = r.tok_in_t, r.tok_in, r.tok_out, r.tok_out_t
    tok_in_t[...] = dot(eye[...], r.in_tok_in_raw[...]).astype(BF)
    tok_in[...] = dot_nt(wide[...], tok_in_t[...]).astype(BF)
    tok_out[...] = dot(eye[...], r.in_tok_out_raw[...]).astype(BF)
    tok_out_t[...] = dot_nt(wide[...], tok_out[...]).astype(BF)
    merge_send(1)
    gci, gco, cib = r.gci, r.gco, r.cib
    gci[...] = jnp.zeros_like(gci)
    gco[...] = jnp.zeros_like(gco)
    cib[...] = jnp.zeros_like(cib)
    tg[...] = jnp.zeros_like(tg)
    vg[...] = jnp.zeros_like(vg)
    s2o[...] = jnp.zeros_like(s2o)
    s1o[...] = jnp.zeros_like(s1o)
    merge_send(2)
    v_across.wait_recv()

    def vector(row):
        return jnp.concatenate([vown[pl.ds(row, 1), :], vother[pl.ds(row, 1), :]], axis=1)

    def normalise(values):
        centred = values - row_sum(values) * (1.0 / full)
        inverse = lax.rsqrt(row_sum(centred * centred) * (1.0 / full) + EPS)
        return centred * inverse, inverse

    def token_forward(j):
        values = raw[j].astype(F32)
        scaled, inverse = normalise(values)
        normed = (scaled * vector(0) + vector(1)).astype(BF)
        r.sc1[j] = scaled[:, :half].astype(BF)
        r.inv1[j] = inverse
        r.n1[j] = normed[:, :half]
        act, slope = gelu_parts(dot(tok_in[...], normed[:, :half]) + r.tib[...])
        r.tsl[j] = slope.astype(BF)
        act = act.astype(BF)
        r.ta[j] = act
        rest = gelu(dot(tok_in[...], normed[:, half:]) + r.tib[...]).astype(BF)
        mid = values + (dot(tok_out[...], jnp.concatenate([act, rest], axis=1)) + r.tob[...])
        r.mid[j] = mid[:, :half]
        scaled, inverse = normalise(mid)
        r.sc2[j] = scaled[:, :half].astype(BF)
        r.inv2[j] = inverse
        ntb[j, first] = (scaled * vector(2) + vector(3)).astype(BF)

    ghs, slopes = r.ghs, r.slopes
    step = 256

    def channel_front(j):
        nt = ntb[j]
        for at in range(hidden // step):
            cols = pl.ds(at * step, step)
            act, slope = gelu_parts(dot(nt, win[:, cols]) + hidden_bias[:, cols])
            outp[j, :, cols] = act.astype(BF)
            slopes[:, cols] = slope

    def channel_grads(j, part):
        g = gb[j, part]
        for at in range(hidden // step):
            cols = pl.ds(at * step, step)
            grad = (slopes[part, cols] * dot_nt(g, wout[cols, :])).astype(BF)
            ghs[j % 2, part, cols] = grad
            cib[:, cols] += jnp.sum(grad.astype(F32), axis=0, keepdims=True)

    def channel_back(j):
        backp[j] = dot_nt(ghs[j % 2], win[...]).astype(BF)
        back_pair(j).start()

    tiles = hidden // LANE

    def chan_out_grad(j, last):
        if last:
            for at in range(full // LANE):
                cols = pl.ds(at * LANE, LANE)
                total = gco[:, cols] + dot_tn(outp[j], gb[j, :, cols])
                gbuf[pl.ds(at * hidden, hidden)] = total.astype(BF)
        else:
            gco[...] += dot_tn(outp[j], gb[j])

    def chan_in_grad(j, last):
        if last:
            for at in range(tiles):
                cols = pl.ds(at * LANE, LANE)
                total = gci[:, cols] + dot_tn(ntb[j], ghs[j % 2, :, cols])
                start = (full // LANE) * hidden + at * full
                gbuf[pl.ds(start, full)] = total.astype(BF)
        else:
            gci[...] += dot_tn(ntb[j], ghs[j % 2])

    def pair_sums(j):
        back_pair(j).wait_recv()
        total = backp[j, first].astype(F32) + backr[j].astype(F32)
        s2o[j, pl.ds(0, 1)] = to_row(row_sum(total * vector(2)), rows)
        s2o[j, pl.ds(1, 1)] = to_row(row_sum(total * (ntb[j, first].astype(F32) - vector(3))), rows)
        backp[j, first] = total.astype(BF)
        s2_across(j).start()
        back_across(j).start()

    def gather_phase(j, carry):
        @pl.when(j + 3 < own)
        def _():
            merge_send(j + 3)

        p_across(j).wait_recv()
        token_forward(j)
        nt_share(j).start()

        @pl.when(j == 0)
        def _():
            for copy in weight_copies:
                copy.wait()

        @pl.when(j > 0)
        def _():
            g_share(j - 1).wait_recv()
            channel_grads(j - 1, pl.ds(0, 2 * rows))
            chan_out_grad(j - 1, False)

        @pl.when(j > 0)
        def _():
            channel_back(j - 1)

        @pl.when((j > 0) & (j < own - 1))
        def _():
            chan_in_grad(j - 1, False)

        c_across(j).wait_recv()
        g_share(j).start()
        nt_share(j).wait_recv()
        channel_front(j)

        @pl.when((j > 1) & (j < own - 1))
        def _():
            pair_sums(j - 2)

        return carry

    lax.fori_loop(0, own, gather_phase, 0)

    channel_grads(own - 1, first)
    g_share(own - 1).wait_recv()
    channel_grads(own - 1, second)
    chan_out_grad(own - 1, True)
    gradient_first(0, (full // LANE) * hidden)
    chan_in_grad(own - 2, False)
    chan_in_grad(own - 1, True)
    gradient_first((full // LANE) * hidden, gbuf.shape[0])
    def partial_outs(j):
        outp[j] = dot(outp[j], wout[...]).astype(BF)
        out_pair(j).start()

    def pair_outs(j):
        out_pair(j).wait_recv()
        total = outp[j, first].astype(F32) + outr[j].astype(F32)
        outp[j, first] = total.astype(BF)
        out_across(j).start()

    def norm_back(weighted, scaled, inverse, sums):
        mean = to_column(sums[0:1] * (1.0 / full), rows)
        slant = to_column(sums[1:2] * (1.0 / full), rows)
        return inverse * (weighted - mean - scaled * slant)

    def token_backward(j):
        s2_across(j).wait_recv()
        back_across(j).wait_recv()
        grad_normed = backp[j, first, near].astype(F32) + backx[j].astype(F32)
        scaled = r.sc2[j].astype(F32)
        grad_out = gb[j, first, near].astype(F32)
        weighted = grad_normed * vown[pl.ds(2, 1), :]
        grad_mid = grad_out + norm_back(weighted, scaled, r.inv2[j], s2o[j] + s2x[j])
        r.gm[j] = grad_mid
        vg[pl.ds(2, 1), :] += jnp.sum(grad_normed * scaled, axis=0, keepdims=True)
        vg[pl.ds(3, 1), :] += jnp.sum(grad_normed, axis=0, keepdims=True)
        vg[pl.ds(4, 1), :] += jnp.sum(grad_out, axis=0, keepdims=True)
        low = grad_mid.astype(BF)
        ones = jnp.ones((8, half), BF)
        tg[pl.ds(rows, rows), :] += dot_nt(low, r.ta[j])
        tg[pl.ds(2 * rows + 8, 8), pl.ds(0, rows)] += dot_nt(ones, low)
        grad_pre = (r.tsl[j].astype(F32) * dot(tok_out_t[...], low)).astype(BF)
        tg[pl.ds(0, rows), :] += dot_nt(r.n1[j], grad_pre)
        tg[pl.ds(2 * rows, 8), :] += dot_nt(ones, grad_pre)
        grad_one = dot(tok_in_t[...], grad_pre)
        scaled = r.sc1[j].astype(F32)
        vg[pl.ds(0, 1), :] += jnp.sum(grad_one * scaled, axis=0, keepdims=True)
        vg[pl.ds(1, 1), :] += jnp.sum(grad_one, axis=0, keepdims=True)
        weighted = grad_one * vown[pl.ds(0, 1), :]
        r.w1[j] = weighted
        s1o[j, pl.ds(0, 1)] = to_row(row_sum(weighted), rows)
        s1o[j, pl.ds(1, 1)] = to_row(row_sum(weighted * scaled), rows)
        s1_across(j).start()

    def input_grad(j):
        s1_across(j).wait_recv()
        scaled = r.sc1[j].astype(F32)
        grad = r.gm[j] + norm_back(r.w1[j], scaled, r.inv1[j], s1o[j] + s1x[j])
        gis[j] = turn_out(grad.astype(BF))
        gin_give(j).start()
        gin_keep(j).start()

    def mixed_part(j):
        out_across(j).wait_recv()
        total = outp[j, first, near].astype(F32) + outx[j].astype(F32)
        valid = jnp.where(c * own + j < r.counts[0], 1.0, 0.0)
        mos[j] = turn_out((valid * (r.mid[j] + (total + vown[pl.ds(4, 1), :]))).astype(BF))
        mixed_give(j).start()
        mixed_keep(j).start()

    def token_start():
        tb[...] = tg[...].astype(BF)
        for at in range(hidden // half):
            vg[pl.ds(8 + at, 1), :] = cib[:, pl.ds(at * half, half)]
        t_core.start()
        v_core.start()

    def token_core():
        t_core.wait_recv()
        v_core.wait_recv()
        tcur[...] = (tb[tc_keep].astype(F32) + tcore[...].astype(F32)).astype(BF)
        t_across.start()
        vcore[...] = vg[pl.ds(0, 8)] + vcore[...]

    def token_across():
        t_across.wait_recv()
        tdp[0, pl.ds(0, t_quarter)] = (tcur[tx_keep].astype(F32) + txr[...].astype(F32)).astype(BF)
        tdp[0, pl.ds(t_quarter, 16)] = jnp.concatenate([vcore[...], vg[pl.ds(8, 8)]], axis=0).astype(BF)
        t_spread()

    def token_back():
        tall[t_mine] = tfin[pl.ds(0, t_quarter)]
        t_back_x.start()
        vec = tfin[pl.ds(t_quarter, 16)].astype(F32)
        vec_out[pl.ds(0, 8), :] = jnp.where(c == 0, vec, pltpu.roll(vec, width, 1))[:8]
        vec_out[pl.ds(8, 8), :] = vec[8:]

    def token_core_back():
        t_back_x.wait_recv()
        t_back_c.start()

    token_outs = [local(tall, r.tok_grads, r.sem_tok, 0), local(vec_out, r.vec_grads, r.sem_tok, 1)]

    def token_end():
        t_back_c.wait_recv()
        vec_out[pl.ds(16, 16), :] = tall[pl.ds(2 * rows, 16)].astype(F32)
        for copy in token_outs:
            copy.start()

    token_steps = [token_start, token_core, None, token_across, None]
    for exchange in t_exchange[:-1]:
        token_steps += [exchange, None]

    def token_last():
        t_exchange[-1]()
        token_back()

    token_steps += [token_last, None, token_core_back, token_end]

    token_first = own - 1
    outs_first = 2
    mixed_first = own

    inputs_first = 5

    def scatter_phase(i, carry):
        gradient_step(i)

        def each(start, work):
            @pl.when((i >= start) & (i < start + own))
            def _():
                work(i - start)

        @pl.when(i == 0)
        def _():
            channel_back(own - 1)

        @pl.when(i == 1)
        def _():
            for j in range(own - 3, own):
                pair_sums(j)

        each(0, token_backward)
        for e, token_step in enumerate(token_steps):
            if token_step is not None:
                pl.when(i == token_first + e)(token_step)
        each(inputs_first, input_grad)
        each(outs_first, pair_outs)
        each(outs_first - 1, partial_outs)
        each(mixed_first, mixed_part)
        return carry

    lax.fori_loop(0, max(gradient_ticks, token_first + len(token_steps), mixed_first + own), scatter_phase, 0)

    outs = []
    for at in range(full // LANE):
        to = mine if at < half // LANE else theirs
        lanes = pl.ds(pl.multiple_of(to + (at % (half // LANE)) * LANE, LANE), LANE)
        here = pl.ds(at * hidden, hidden)
        outs.append((here, local(fbuf.at[here], r.g_chan_out.at[:, lanes], r.sem_out, len(outs))))
    for at in range(tiles):
        lanes = pl.ds(at * LANE, LANE)
        for part, to in enumerate((mine, theirs)):
            here = pl.ds((full // LANE) * hidden + at * full + part * half, half)
            outs.append((here, local(fbuf.at[here], r.g_chan_in.at[pl.ds(to, half), lanes], r.sem_out, len(outs))))
    for k in range(gradient_items):
        gradient_last(k)
        for here, copy in outs:
            if k * chunk < here.start + here.size <= (k + 1) * chunk:
                copy.start()

    def gradient_drain(k, carry):
        gradient_sent(k)
        return carry

    lax.fori_loop(0, gradient_items, gradient_drain, 0)

    def drain(j, carry):
        for make in (p_swap, c_swap, p_across, c_across, nt_share, g_share, out_pair, back_pair):
            make(j).wait_send()
        for make in (out_across, back_across, s2_across, s1_across):
            make(j).wait_send()
        for make in (mixed_give, gin_give, mixed_keep, gin_keep):
            make(j).wait()
        return carry

    lax.fori_loop(0, own, drain, 0)
    for copy in [v_swap, v_across, t_core, t_across, t_back_x, t_back_c, v_core] + t_sends:
        copy.wait_send()
    for _, copy in outs:
        copy.wait()
    for copy in token_outs:
        copy.wait()


def run_layer(n_dp, **arrays):
    batch, width, count = arrays["patches"].shape
    own = batch // 2
    full, hidden = arrays["win_hbm"].shape
    half = full // 2
    toks = arrays["tok_in_raw"].shape[1]
    rows = -(-count // 16) * 16
    bits = n_dp.bit_length() - 1
    grad_rows = 2 * full * hidden // LANE
    folded = n_dp == 8
    choices = (8, 4, 2) if folded else (9, 3, 1)
    parts = 18 if folded else n_dp
    chunks = next(k for k in choices if grad_rows % (k * parts * (64 if folded else 16)) == 0)
    chunk = grad_rows // chunks
    cfg = (n_dp, own, count, rows, half, full, hidden, toks, chunks, chunk)
    vmem = pltpu.VMEM
    dma = pltpu.SemaphoreType.DMA
    two, whole = chunk * 14 // 36, chunk * 4 // 18
    t_rows = -(-(2 * rows + 16) // 64) * 64
    scratch = dict(
        win=vmem((full, hidden), BF),
        wout=vmem((hidden, full), BF),
        pin=vmem((own, half, count), BF),
        cin=vmem((own, half, count), BF),
        vpad=vmem((8, half), F32),
        hidden_row=vmem((1, hidden), F32),
        tok_row=vmem((1, toks), F32),
        vmine=vmem((8, half), F32),
        vpart=vmem((8, half), F32),
        vown=vmem((8, half), F32),
        vother=vmem((8, half), F32),
        eye=vmem((rows, count), BF),
        wide=vmem((half, half), BF),
        tok_in_t=vmem((rows, toks), BF),
        tok_in=vmem((toks, rows), BF),
        tok_out=vmem((rows, toks), BF),
        tok_out_t=vmem((toks, rows), BF),
        tib=vmem((toks, 1), F32),
        tob=vmem((rows, 1), F32),
        raw=vmem((own, rows, full), BF),
        ntb=vmem((own, 2 * rows, full), BF),
        gb=vmem((own, 2 * rows, full), BF),
        ghs=vmem((2, 2 * rows, hidden), BF),
        slopes=vmem((2 * rows, hidden), F32),
        gci=vmem((full, hidden), F32),
        gco=vmem((hidden, full), F32),
        cib=vmem((1, hidden), F32),
        outp=vmem((own, 2 * rows, full), BF),
        outr=vmem((own, rows, full), BF),
        backp=vmem((own, 2 * rows, full), BF),
        backr=vmem((own, rows, full), BF),
        outx=vmem((own, rows, half), BF),
        backx=vmem((own, rows, half), BF),
        s2o=vmem((own, 8, rows), F32),
        s2x=vmem((own, 8, rows), F32),
        s1o=vmem((own, 8, rows), F32),
        s1x=vmem((own, 8, rows), F32),
        n1=vmem((own, rows, half), BF),
        ta=vmem((own, toks, half), BF),
        tsl=vmem((own, toks, half), BF),
        mid=vmem((own, rows, half), F32),
        sc1=vmem((own, rows, half), BF),
        sc2=vmem((own, rows, half), BF),
        inv1=vmem((own, rows, 1), F32),
        inv2=vmem((own, rows, 1), F32),
        gm=vmem((own, rows, half), F32),
        w1=vmem((own, rows, half), F32),
        gbuf=vmem((grad_rows, LANE), BF),
        fbuf=vmem((grad_rows, LANE), BF),
        tg=vmem((t_rows, toks), F32),
        tb=vmem((t_rows, toks), BF),
        tcore=vmem((t_rows // 2, toks), BF),
        tcur=vmem((t_rows // 2, toks), BF),
        txr=vmem((t_rows // 4, toks), BF),
        tdp=vmem((1 if folded else bits, t_rows // 4 + 16, toks), BF),
        trd=vmem((n_dp, (t_rows // 4 + 16) // n_dp, toks) if folded else (bits, t_rows // 4 + 16, toks), BF),
        tall=vmem((t_rows, toks), BF),
        vec_out=vmem((32, half), F32),
        sem_tok=dma((2,)),
        tfin=vmem((t_rows // 4 + 16, toks), BF),
        vg=vmem((16, half), F32),
        vcore=vmem((8, half), F32),
        sem_w=dma((4,)),
        sem_small=dma((10,)),
        sem_v=dma((2, 2)),
        sem_out=dma((2 * (hidden // LANE) + full // LANE,)),
        sem_t=dma((2, 5)),
        sem_td=dma((2, bits)),
        sem_tr=dma((2, n_dp)),
        sem_ta=dma((2, n_dp)),
    )
    for name in list(arrays)[3:13]:
        scratch["in_" + name] = vmem(arrays[name].shape, arrays[name].dtype)
    for name in ("pl", "cl", "mk", "gk"):
        scratch["sem_" + name] = dma((own,))
    for name in ("ps", "cs", "px", "cx", "nt", "g", "op", "bp", "ox", "bx", "s2", "s1", "mg", "gg"):
        scratch["sem_" + name] = dma((2, own))
    if folded:
        scratch["e0"] = vmem((chunks * two, LANE), BF)
        scratch["e1"] = vmem((chunks * two, LANE), BF)
        scratch["e2"] = vmem((chunks * two // 2, LANE), BF)
        scratch["o0"] = vmem((chunks * whole, LANE), BF)
        scratch["o1"] = vmem((chunks * whole // 2, LANE), BF)
        scratch["o2"] = vmem((chunks * whole // 4, LANE), BF)
        for name in [e + str(k) for e in "eo" for k in range(7)]:
            scratch["sem_" + name] = dma((2, chunks))
    else:
        scratch["rbuf"] = vmem((chunks * (chunk - (chunk >> bits)), LANE), BF)
        scratch["sem_rs"] = dma((2, bits, chunks))
        scratch["sem_ag"] = dma((2, bits, chunks))
    hbm = pl.BlockSpec(memory_space=pl.ANY)
    places = dict(counts=pl.BlockSpec(memory_space=pltpu.SMEM))
    outs = dict(
        mixed=((batch, width, count), BF),
        gin=((batch, width, count), BF),
        tok_grads=((t_rows, toks), BF),
        vec_grads=((32, half), F32),
        g_chan_in=((full, hidden), BF),
        g_chan_out=((hidden, full), BF),
    )
    names = list(arrays) + list(outs) + list(scratch)
    results = pl.pallas_call(
        functools.partial(layer_kernel, cfg, names),
        out_shape=tuple(jax.ShapeDtypeStruct(*outs[name]) for name in outs),
        in_specs=[places.get(name, hbm) for name in arrays],
        out_specs=tuple(places.get(name, hbm) for name in outs),
        scratch_shapes=list(scratch.values()),
        compiler_params=pltpu.CompilerParams(
            collective_id=0, has_side_effects=True, vmem_limit_bytes=63 * 2**20
        ),
        name="mixer_layer",
    )(*arrays.values())
    return SimpleNamespace(**dict(zip(outs, results)))


def finish_kernel(names, smalls, *refs):
    r = SimpleNamespace(**dict(zip(names, refs)))
    count, toks = r.tok_in.shape
    rows = -(-count // 16) * 16
    parts, step = r.pieces.shape[1:3]
    images = r.images.shape[1] // 2

    def copy(src, dst, at):
        return pltpu.make_async_copy(src, dst, r.sems.at[at])

    loads, stores = [], []
    for at, (raw, done) in enumerate(((r.chan_out_raw, r.chan_out), (r.chan_in_raw, r.chan_in))):
        for part in range(parts):
            here = pl.ds(part * step, step)
            loads.append(copy(raw.at[here], r.pieces.at[at, part], len(loads)))
            stores.append(copy(r.wide.at[at, part], done.at[here], 2 * parts + len(stores)))
    first = 4 * parts
    images_in, images_out = [], []
    for at, (raw, done) in enumerate(((r.mixed_raw, r.mixed), (r.gin_raw, r.gin))):
        for part in range(2):
            here = pl.ds(part * images, images)
            images_in.append(copy(raw.at[here], r.images.at[at, here], first + len(images_in)))
            images_out.append(copy(r.images.at[at, here], done.at[here], first + 4 + len(images_out)))
    first += 8
    tok_load = copy(r.tok_raw, r.tall, first)
    vec_load = copy(r.vec_raw, r.vec, first + 1)
    small_stores = [
        copy(getattr(r, "out_" + name), getattr(r, name), first + 2 + at) for at, name in enumerate(smalls)
    ]
    for load in loads[:2] + [tok_load, vec_load] + loads[2:] + images_in:
        load.start()

    def widen(at):
        loads[at].wait()
        r.wide[at // parts, at % parts] = r.pieces[at // parts, at % parts].astype(F32)
        stores[at].start()

    widen(0)
    widen(1)
    tok_load.wait()
    vec_load.wait()
    vec, tall = r.vec, r.tall
    width = r.ln1_gain.shape[1]
    half = vec.shape[1]
    r.out_tok_in[...] = tall[pl.ds(0, rows)][:count].astype(F32)
    r.out_tok_out[...] = tall[pl.ds(rows, rows)][:count].astype(F32)
    outs = (r.out_ln1_gain, r.out_ln1_bias, r.out_ln2_gain, r.out_ln2_bias, r.out_chan_out_bias)
    for at, done in enumerate(outs):
        done[...] = vec[pl.ds(at, 1), :][:, :width]
    for at in range(r.chan_in_bias.shape[0]):
        row, lane = divmod(at * LANE, half)
        r.out_chan_in_bias[pl.ds(at, 1), :] = vec[pl.ds(8 + row, 1), pl.ds(lane, LANE)]
    for at in range(toks // LANE):
        r.out_tok_in_bias[pl.ds(at, 1), :] = vec[pl.ds(16, 1), pl.ds(at * LANE, LANE)]
    r.out_tok_out_bias[...] = vec[pl.ds(24, 1), :][:, :count]
    for store in small_stores:
        store.start()
    for at in range(2, len(loads)):
        widen(at)
    for load, store in zip(images_in, images_out):
        load.wait()
        store.start()
    for store in stores + images_out + small_stores:
        store.wait()


def finish(out, count, width):
    full, hidden = out.g_chan_in.shape
    toks = out.tok_grads.shape[1]
    hbm = pl.BlockSpec(memory_space=pl.ANY)
    arrays = dict(
        mixed_raw=out.mixed,
        gin_raw=out.gin,
        chan_in_raw=out.g_chan_in,
        chan_out_raw=out.g_chan_out,
        tok_raw=out.tok_grads,
        vec_raw=out.vec_grads,
    )
    outs = dict(
        mixed=(out.mixed.shape, BF),
        gin=(out.gin.shape, BF),
        chan_in=((full, hidden), F32),
        chan_out=((hidden, full), F32),
        tok_in=((count, toks), F32),
        tok_out=((count, toks), F32),
        ln1_gain=((1, width), F32),
        ln1_bias=((1, width), F32),
        ln2_gain=((1, width), F32),
        ln2_bias=((1, width), F32),
        chan_out_bias=((1, width), F32),
        chan_in_bias=((hidden // LANE, LANE), F32),
        tok_in_bias=((toks // LANE, LANE), F32),
        tok_out_bias=((1, count), F32),
    )
    smalls = list(outs)[4:]
    parts = 4
    scratch = dict(
        pieces=pltpu.VMEM((2, parts, full // parts, hidden), BF),
        wide=pltpu.VMEM((2, parts, full // parts, hidden), F32),
        images=pltpu.VMEM((2,) + out.mixed.shape, BF),
        tall=pltpu.VMEM(out.tok_grads.shape, BF),
        vec=pltpu.VMEM(out.vec_grads.shape, F32),
        sems=pltpu.SemaphoreType.DMA((4 * parts + 10 + len(smalls),)),
    )
    for name in smalls:
        scratch["out_" + name] = pltpu.VMEM(*outs[name])
    names = list(arrays) + list(outs) + list(scratch)
    results = pl.pallas_call(
        functools.partial(finish_kernel, names, smalls),
        out_shape=tuple(jax.ShapeDtypeStruct(*outs[name]) for name in outs),
        in_specs=[hbm] * len(arrays),
        out_specs=(hbm,) * len(outs),
        scratch_shapes=list(scratch.values()),
        compiler_params=pltpu.CompilerParams(vmem_limit_bytes=63 * 2**20),
        name="finish",
    )(*arrays.values())
    return SimpleNamespace(**dict(zip(outs, results)))


def per_device(
    n_dp,
    image_counts,
    patches,
    ln1_gain,
    ln1_bias,
    tok_in_weight,
    tok_in_bias,
    tok_out_weight,
    tok_out_bias,
    ln2_gain,
    ln2_bias,
    chan_in_weight,
    chan_in_bias,
    chan_out_weight,
    chan_out_bias,
    cotangent,
):
    out = run_layer(
        n_dp,
        counts=image_counts,
        patches=jnp.transpose(patches, (1, 2, 0)),
        cot=jnp.transpose(cotangent, (1, 2, 0)),
        ln1_gain=ln1_gain[None, :],
        ln1_bias=ln1_bias[None, :],
        ln2_gain=ln2_gain[None, :],
        ln2_bias=ln2_bias[None, :],
        chan_out_bias=chan_out_bias[None, :],
        hidden_bias=chan_in_bias.reshape(-1, LANE),
        tok_in_bias=tok_in_bias.reshape(-1, LANE),
        tok_out_bias=tok_out_bias[None, :],
        tok_in_raw=tok_in_weight.T,
        tok_out_raw=tok_out_weight,
        win_hbm=chan_in_weight,
        wout_hbm=chan_out_weight,
    )
    out = finish(out, patches.shape[0], patches.shape[2])
    return (
        jnp.transpose(out.mixed, (2, 0, 1)),
        jnp.transpose(out.gin, (2, 0, 1)),
        out.ln1_gain[0],
        out.ln1_bias[0],
        out.tok_in.T,
        out.tok_in_bias.reshape(-1),
        out.tok_out,
        out.tok_out_bias[0],
        out.ln2_gain[0],
        out.ln2_bias[0],
        out.chan_in,
        out.chan_in_bias.reshape(-1),
        out.chan_out,
        out.chan_out_bias[0],
    )


def solution(mesh):
    in_specs = (
        P("dp"),
        P(None, "dp", "seq"),
        P("seq"),
        P("seq"),
        P(),
        P(),
        P(),
        P(),
        P("seq"),
        P("seq"),
        P(None, "seq"),
        P("seq"),
        P("seq", None),
        P("seq"),
        P(None, "dp", "seq"),
    )
    out_specs = (
        P(None, "dp", "seq"),
        P(None, "dp", "seq"),
        P("seq"),
        P("seq"),
        P(),
        P(),
        P(),
        P(),
        P("seq"),
        P("seq"),
        P(None, "seq"),
        P("seq"),
        P("seq", None),
        P("seq"),
    )
    return jax.shard_map(
        functools.partial(per_device, mesh.shape["dp"]),
        mesh=mesh,
        in_specs=in_specs,
        out_specs=out_specs,
        check_vma=False,
    )
```
